32 devices in a mesh: dp: 4 (over y, core), shard: 8 (over z, x).
Axes of the slice: x: 2, y: 2, z: 4, core: 2. Of those that a mesh axis runs over, the one named last changes fastest.
Arguments:
- tokens: bfloat16 [16384, 768], P(('dp', 'shard')), may hold values from -36 to 36
- picture_ids: int32 [16384], P(('dp', 'shard')), may hold values from 0 to 4, as said below
- cotangent: bfloat16 [16384, 768], P(('dp', 'shard')), may hold values from -38 to 38
- w_qkv: float32 [768, 2304], P('shard'), may hold values from -0.21875 to 0.21875
- w_out: float32 [768, 768], P('shard'), may hold values from -0.875 to 0.875
- w_fc1: float32 [768, 3072], P('shard'), may hold values from -0.21875 to 0.21875
- w_fc2: float32 [3072, 768], P('shard'), may hold values from -0.109375 to 0.109375
- vectors: float32 [8, 768], P(None, 'shard'), may hold values from -2 to 2
- fc1_bias: float32 [3072], P('shard'), may hold values from -3 to 3
- moments_qkv: float32 [2, 768, 2304], P(None, 'shard'), may hold values from -0.002 to 0.002, as said below
- moments_out: float32 [2, 768, 768], P(None, 'shard'), may hold values from -0.002 to 0.002, as said below
- moments_fc1: float32 [2, 768, 3072], P(None, 'shard'), may hold values from -0.002 to 0.002, as said below
- moments_fc2: float32 [2, 3072, 768], P(None, 'shard'), may hold values from -0.002 to 0.002, as said below
- moments_vectors: float32 [2, 8, 768], P(None, None, 'shard'), may hold values from -0.002 to 0.002, as said below
- moments_fc1_bias: float32 [2, 3072], P(None, 'shard'), may hold values from -0.002 to 0.002, as said below
Outputs:
- layer_out: bfloat16 [16384, 768], P(('dp', 'shard'))
- tokens_grad: bfloat16 [16384, 768], P(('dp', 'shard'))
- grad_qkv: float32 [768, 2304], P('shard')
- grad_out: float32 [768, 768], P('shard')
- grad_fc1: float32 [768, 3072], P('shard')
- grad_fc2: float32 [3072, 768], P('shard')
- grad_vectors: float32 [8, 768], P(None, 'shard')
- grad_fc1_bias: float32 [3072], P('shard')
- new_qkv: float32 [768, 2304], P('shard')
- new_out: float32 [768, 768], P('shard')
- new_fc1: float32 [768, 3072], P('shard')
- new_fc2: float32 [3072, 768], P('shard')
- vectors_step: float32 [8, 768], P(None, 'shard')
- new_fc1_bias: float32 [3072], P('shard')
- stream_rms: float32 [5], replicated
The draws below stay inside these ranges and needn't reach their ends.
Inputs may be any that keep to these rules, and one draw needn't show every extreme that they name: `picture_ids`: within each row of 512 tokens the pictures are numbered 1, 2, ... from the row's start, one to four a row, each of 100 or more tokens; 0 marks padding, fewer than 100 tokens at a row's end; the first row is one picture of all 512 tokens. `moments_qkv`: the second moments are positive. `moments_out`: the second moments are positive. `moments_fc1`: the second moments are positive. `moments_fc2`: the second moments are positive. `moments_vectors`: the second moments are positive. `moments_fc1_bias`: the second moments are positive.
All inputs are finite; a program needn't handle non-finite values.
Results may differ from the reference program's by a relative error of at most 0.012.
The reference program's roundings to bfloat16 on the way count: a program that leaves them out, or rounds other values in their place, can miss the bound.
Values may be sent and summed in bfloat16 or wider, within the bound.
No kernel may reach another device: no remote copies, remote signals or barrier semaphores. Data moves between devices by JAX's collectives and lax.ppermute only.
A program may use at most 256 MiB of HBM per device.

```python
import math
import jax
import jax.numpy as jnp
from jax import lax

D = 768
HEADS = 12
HEAD_DIM = 64
FF = 3072
ROW = 512
PIC_MIN = 100
STEP = 2
TOKENS = 16384


def base_field(base_key, shape):
    return jnp.clip(jax.random.normal(base_key, shape, jnp.float32), -6.0, 6.0)


def draw_tokens(key, part):
    base_key, scale_key = jax.random.split(jax.random.fold_in(key, 11))
    base_draw = base_field(base_key, (TOKENS, D))
    position = jnp.arange(TOKENS, dtype=jnp.float32) / max(TOKENS - 1, 1)
    rising = jnp.exp(math.log(3.0) * position)[:, None]
    row_scale = jnp.exp(jax.random.uniform(scale_key, (TOKENS, 1), jnp.float32, math.log(0.5), math.log(2.0)))
    return (base_draw * rising * row_scale).astype(jnp.bfloat16)


def draw_cotangent(key, part):
    base_key, row_key, column_key = jax.random.split(jax.random.fold_in(key, 23), 3)
    base_draw = base_field(base_key, (TOKENS, D))
    row_scale = jnp.exp(jax.random.uniform(row_key, (TOKENS, 1), jnp.float32, math.log(0.4), math.log(2.5)))
    column_scale = jnp.exp(jax.random.uniform(column_key, (1, D), jnp.float32, math.log(0.4), math.log(2.5)))
    return (base_draw * row_scale * column_scale).astype(jnp.bfloat16)


def draw_picture_ids(key, part):
    row_count = TOKENS // ROW
    count_key, pad_key, share_key = jax.random.split(jax.random.fold_in(key, 37), 3)
    row_index = jnp.arange(row_count, dtype=jnp.int32)[:, None]
    opening = row_index == 0
    pictures = jnp.where(opening, 1, jax.random.randint(count_key, (row_count, 1), 1, 5))
    padding = jnp.where(opening, 0, jax.random.randint(pad_key, (row_count, 1), 0, PIC_MIN))
    spare_tokens = ROW - padding - pictures * PIC_MIN
    slot_index = jnp.arange(4, dtype=jnp.int32)[None, :]
    shares = jnp.where(slot_index < pictures, jax.random.randint(share_key, (row_count, 4), 1, 101), 0)
    share_total = jnp.sum(shares, axis=1, keepdims=True)
    picture_ends = (slot_index + 1) * PIC_MIN + spare_tokens * jnp.cumsum(shares, axis=1) // share_total
    picture_ends = jnp.where(slot_index < pictures, picture_ends, ROW + 1)
    position = jnp.arange(ROW, dtype=jnp.int32)[None, :, None]
    passed = jnp.sum((position >= picture_ends[:, None, :]).astype(jnp.int32), axis=2)
    inside = position[:, :, 0] < ROW - padding
    return jnp.where(inside, 1 + passed, 0).reshape(TOKENS).astype(jnp.int32)


def draw_vectors(key, part):
    gain_key, shift_key = jax.random.split(jax.random.fold_in(key, 41))
    gains = jax.random.uniform(gain_key, (8, D), jnp.float32, 0.5, 1.5)
    shifts = 0.3 * jnp.clip(jax.random.normal(shift_key, (8, D), jnp.float32), -6.0, 6.0)
    row_number = jnp.arange(8, dtype=jnp.int32)[:, None]
    is_gain = (row_number == 0) | (row_number == 5)
    return jnp.where(is_gain, gains, shifts)


def moment_pair(key, shape):
    first_key, second_key = jax.random.split(key)
    first_moment = 0.0003 * jnp.clip(jax.random.normal(first_key, shape, jnp.float32), -6.0, 6.0)
    second_moment = jnp.exp(jax.random.uniform(second_key, shape, jnp.float32, math.log(1e-08), math.log(1e-06)))
    return jnp.stack([first_moment, second_moment])


def draw_moments_qkv(key, part):
    own_key = jax.random.fold_in(key, 101)
    return moment_pair(own_key, (D, 3 * D))


def draw_moments_out(key, part):
    own_key = jax.random.fold_in(key, 103)
    return moment_pair(own_key, (D, D))


def draw_moments_fc1(key, part):
    own_key = jax.random.fold_in(key, 107)
    return moment_pair(own_key, (D, FF))


def draw_moments_fc2(key, part):
    own_key = jax.random.fold_in(key, 109)
    return moment_pair(own_key, (FF, D))


def draw_moments_vectors(key, part):
    own_key = jax.random.fold_in(key, 113)
    return moment_pair(own_key, (8, D))


def draw_moments_fc1_bias(key, part):
    own_key = jax.random.fold_in(key, 127)
    return moment_pair(own_key, (FF,))


def block_scale(key, dims, shards, low, largest):
    def one(dim, blocks):
        heights = jax.random.uniform(jax.random.fold_in(jax.random.fold_in(key, 6), dim), (blocks,), jnp.float32, low / len(shards), largest / len(shards))
        return jnp.repeat(jnp.exp(heights), dims[dim] // blocks).reshape((-1,) + (1,) * (len(dims) - dim - 1))

    loudness = one(*shards[0])
    for cut in shards[1:]:
        loudness = loudness * one(*cut)
    return loudness


def scatter_about(stream_key, dims, width, most, cuts=(), kind=jnp.bfloat16):
    level = block_scale(stream_key, dims, cuts, -0.22, 0.18) if cuts else 1.0
    values = jax.random.normal(stream_key, dims, jnp.float32) * width * level
    return jnp.minimum(jnp.maximum(values, -most), most).astype(kind)


def setup_inputs(seed: int = 0) -> dict:
    arg_keys = jax.random.split(jax.random.key(seed), 16)
    return {
        "tokens": draw_tokens(jax.random.fold_in(arg_keys[15], 71), 0),
        "picture_ids": draw_picture_ids(jax.random.fold_in(arg_keys[15], 71), 0),
        "cotangent": draw_cotangent(jax.random.fold_in(arg_keys[15], 71), 0),
        "w_qkv": scatter_about(arg_keys[3], (D, 3 * D), D ** -0.5, 0.21875, ((0, 8),), jnp.float32),
        "w_out": scatter_about(arg_keys[4], (D, D), (D // 16) ** -0.5, 0.875, ((0, 8),), jnp.float32),
        "w_fc1": scatter_about(arg_keys[5], (D, FF), D ** -0.5, 0.21875, ((0, 8),), jnp.float32),
        "w_fc2": scatter_about(arg_keys[6], (FF, D), FF ** -0.5, 0.109375, ((0, 8),), jnp.float32),
        "vectors": draw_vectors(jax.random.fold_in(arg_keys[15], 71), 0),
        "fc1_bias": scatter_about(arg_keys[8], (FF,), 0.5, 3.0, ((0, 8),), jnp.float32),
        "moments_qkv": draw_moments_qkv(jax.random.fold_in(arg_keys[15], 71), 0),
        "moments_out": draw_moments_out(jax.random.fold_in(arg_keys[15], 71), 0),
        "moments_fc1": draw_moments_fc1(jax.random.fold_in(arg_keys[15], 71), 0),
        "moments_fc2": draw_moments_fc2(jax.random.fold_in(arg_keys[15], 71), 0),
        "moments_vectors": draw_moments_vectors(jax.random.fold_in(arg_keys[15], 71), 0),
        "moments_fc1_bias": draw_moments_fc1_bias(jax.random.fold_in(arg_keys[15], 71), 0),
    }


NORM_EPS = 1e-06
ADAM_BETA = 0.5
LEARN_RATE = 0.03
WEIGHT_DECAY = 0.1
ADAM_EPS = 1e-08
CLIP_NORM = 1.0
MASKED = -1e+30
PRECISE = lax.Precision.HIGHEST

@jax.custom_vjp
def low(v):
    return lax.optimization_barrier(v.astype(jnp.bfloat16)).astype(jnp.float32)

@jax.custom_vjp
def low_back(v):
    return v

def low_keep(v):
    return (low(v), None)

def low_pass(kept, grad):
    return (grad,)

def back_keep(v):
    return (v, None)

def back_low(kept, grad):
    return (low(grad),)
low.defvjp(low_keep, low_pass)
low_back.defvjp(back_keep, back_low)

def layer_norm(entries, scale_row, shift_row):
    center = entries - lax.optimization_barrier(jnp.mean(entries, axis=-1, keepdims=True))
    spread = lax.optimization_barrier(jnp.mean(center * center, axis=-1, keepdims=True))
    return center * lax.rsqrt(spread + NORM_EPS) * scale_row + shift_row

def matmul(left, right):
    return jnp.dot(left, right, precision=PRECISE, preferred_element_type=jnp.float32)

def attend_row(queries, key_rows, values, picture):
    head_shape = (ROW, HEADS, HEAD_DIM)
    scores = jnp.einsum('qhd,khd->hqk', queries.reshape(head_shape), key_rows.reshape(head_shape), precision=PRECISE) * HEAD_DIM ** (-0.5)
    scores = low_back(scores)
    same_picture = picture[:, None] == picture[None, :]
    scores = jnp.where(same_picture[None], scores, MASKED)
    row_max = lax.optimization_barrier(jnp.max(scores, axis=-1, keepdims=True))
    weights = jnp.exp(scores - row_max)
    weights_low = low(weights / lax.optimization_barrier(jnp.sum(weights, axis=-1, keepdims=True)))
    mixture = jnp.einsum('hqk,khd->qhd', weights_low, values.reshape(head_shape), precision=PRECISE)
    return mixture.reshape(ROW, HEADS * HEAD_DIM)

def attend_item(blocks_in):
    return jax.checkpoint(attend_row)(blocks_in[0], blocks_in[1], blocks_in[2], blocks_in[3])

def forward(params, stream, picture):
    w_qkv, w_out, w_fc1, w_fc2, vector_rows, fc1_bias = [low(entry) for entry in params]
    model_width = stream.shape[1]
    normed_one = low(layer_norm(stream, vector_rows[0], vector_rows[1]))
    projected = low_back(matmul(normed_one, w_qkv))
    queries = low(projected[:, :model_width] + vector_rows[2])
    key_rows = low(projected[:, model_width:2 * model_width])
    values = low(projected[:, 2 * model_width:] + vector_rows[3])
    row_count = stream.shape[0] // ROW
    block_shape = (row_count, ROW, model_width)
    mixture = lax.map(attend_item, (queries.reshape(block_shape), key_rows.reshape(block_shape), values.reshape(block_shape), picture.reshape(row_count, ROW)))
    mixture = low(low_back(mixture.reshape(-1, model_width)))
    attention = low_back(matmul(mixture, w_out)) + vector_rows[4]
    middle = stream + attention
    normed_two = low(layer_norm(middle, vector_rows[5], vector_rows[6]))
    preact = low_back(matmul(normed_two, w_fc1)) + fc1_bias
    hidden = low(jax.nn.gelu(preact, approximate=True))
    feedforward = low_back(matmul(hidden, w_fc2)) + vector_rows[7]
    result = middle + feedforward
    return (result, (attention, middle, feedforward))

def reference(tokens, picture_ids, cotangent, w_qkv, w_out, w_fc1, w_fc2, vectors, fc1_bias, moments_qkv, moments_out, moments_fc1, moments_fc2, moments_vectors, moments_fc1_bias):
    params = (w_qkv, w_out, w_fc1, w_fc2, vectors, fc1_bias)
    moments = (moments_qkv, moments_out, moments_fc1, moments_fc2, moments_vectors, moments_fc1_bias)
    model_width = tokens.shape[1]
    total_rows = tokens.shape[0] // ROW
    row_limit = max(1, 4096 // ROW)
    group_rows = max((number for number in range(1, row_limit + 1) if total_rows % number == 0))
    step_blocks = total_rows // group_rows
    block_tokens = group_rows * ROW
    stream_all = tokens.astype(jnp.float32).reshape(step_blocks, block_tokens, model_width)
    picture_all = picture_ids.reshape(step_blocks, block_tokens)
    cot_all = cotangent.astype(jnp.float32).reshape(step_blocks, block_tokens, model_width)

    def scan_step(carried, blocks_in):
        grad_sums, stream_sums = carried
        stream_block, picture_block, cot_block = blocks_in

        def block_forward(weights_in, stream_in):
            return forward(weights_in, stream_in, picture_block)
        result, backward_fn, branches = jax.vjp(block_forward, params, stream_block, has_aux=True)
        grad_params, grad_stream = backward_fn(cot_block)
        grad_sums = jax.tree.map(jnp.add, grad_sums, grad_params)
        valid_rows = (picture_block != 0).astype(jnp.float32)[:, None]
        parts_list = [stream_block, branches[0], branches[1], branches[2], result]
        block_sums = jnp.stack([jnp.sum(valid_rows * entry * entry) for entry in parts_list] + [jnp.sum(valid_rows * jnp.ones((1, 1), jnp.float32))])
        return ((grad_sums, stream_sums + block_sums), (result.astype(jnp.bfloat16), grad_stream.astype(jnp.bfloat16)))
    initial = (tuple((jnp.zeros_like(entry) for entry in params)), jnp.zeros((6,), jnp.float32))
    (grad_sums, stream_sums), (outputs, grads_in) = lax.scan(scan_step, initial, (stream_all, picture_all, cot_all))
    layer_out = outputs.reshape(tokens.shape)
    tokens_grad = grads_in.reshape(tokens.shape)
    stream_rms = jnp.sqrt(stream_sums[:5] / (stream_sums[5] * model_width))
    square_sum = sum((jnp.sum(entry * entry) for entry in grad_sums))
    clip_factor = CLIP_NORM / jnp.maximum(jnp.sqrt(square_sum), CLIP_NORM)
    correction = 1.0 - ADAM_BETA ** STEP
    updated = []
    for number in range(6):
        clipped = grad_sums[number] * clip_factor
        first_moment = ADAM_BETA * moments[number][0] + (1.0 - ADAM_BETA) * clipped
        second_moment = ADAM_BETA * moments[number][1] + (1.0 - ADAM_BETA) * clipped * clipped
        change = first_moment / correction / (jnp.sqrt(second_moment / correction) + ADAM_EPS)
        if number < 4:
            change = change + WEIGHT_DECAY * params[number]
        if number == 4:
            updated.append(LEARN_RATE * change)
        else:
            updated.append(params[number] - LEARN_RATE * change)
    return (layer_out, tokens_grad, grad_sums[0], grad_sums[1], grad_sums[2], grad_sums[3], grad_sums[4], grad_sums[5], updated[0], updated[1], updated[2], updated[3], updated[4], updated[5], stream_rms)
```

```python
from functools import partial

import jax
import jax.numpy as jnp
from jax import lax
from jax.experimental import pallas as pl
from jax.experimental.pallas import tpu as pltpu
from jax.sharding import PartitionSpec as P

HEADS = 12
HEAD_DIM = 64
ROW = 512
STEP = 2


NORM_EPS = 1e-06
ADAM_BETA = 0.5
LEARN_RATE = 0.03
WEIGHT_DECAY = 0.1
ADAM_EPS = 1e-08
CLIP_NORM = 1.0
MASKED = -1e30


def layer_norm(entries, scale_row, shift_row):
    center = entries - jnp.mean(entries, axis=-1, keepdims=True)
    spread = jnp.mean(center * center, axis=-1, keepdims=True)
    return center * lax.rsqrt(spread + NORM_EPS) * scale_row + shift_row


def gelu_tanh(entries):
    return jax.nn.gelu(entries, approximate=True)


def block_scores(query_block, key_rows, picture, start_row, block_size, score_scale):
    scores = (
        jnp.einsum("qhd,khd->hqk", query_block, key_rows, preferred_element_type=jnp.float32)
        * score_scale
    )
    same_picture = picture[start_row : start_row + block_size, None] == picture[None, :]
    return jnp.where(same_picture[None], scores, MASKED)


def attend_forward(blocks_in, block_size, score_scale):
    queries, key_rows, values_in, picture = blocks_in
    scores = block_scores(queries, key_rows, picture, 0, block_size, score_scale)
    row_max = jnp.max(scores, axis=-1, keepdims=True)
    weights = jnp.exp(scores - row_max)
    row_total = jnp.sum(weights, axis=-1, keepdims=True)
    weights_low = (weights / row_total).astype(jnp.bfloat16)
    mixtures = [
        jnp.einsum("hqk,khd->qhd", weights_low, values_in, preferred_element_type=jnp.float32)
    ]
    log_totals = [(row_max + jnp.log(row_total))[:, :, 0]]
    return (jnp.concatenate(mixtures, 0), jnp.concatenate(log_totals, 1))


def attend_backward(blocks_in, block_size, score_scale):
    queries, key_rows, values_in, grad_mix, picture, log_total = blocks_in
    grad_keys = jnp.zeros(key_rows.shape, jnp.float32)
    grad_values = jnp.zeros(values_in.shape, jnp.float32)
    scores = block_scores(queries, key_rows, picture, 0, block_size, score_scale)
    weights = jnp.exp(scores - log_total[:, 0:block_size, None])
    grad_weights = jnp.einsum(
        "qhd,khd->hqk", grad_mix, values_in, preferred_element_type=jnp.float32
    )
    row_inner = jnp.sum(weights * grad_weights, axis=-1, keepdims=True)
    grad_scores = (weights * (grad_weights - row_inner)).astype(jnp.bfloat16)
    grad_queries = [
        jnp.einsum("hqk,khd->qhd", grad_scores, key_rows, preferred_element_type=jnp.float32)
        * score_scale
    ]
    grad_keys = (
        grad_keys
        + jnp.einsum("hqk,qhd->khd", grad_scores, queries, preferred_element_type=jnp.float32)
        * score_scale
    )
    grad_values = grad_values + jnp.einsum(
        "hqk,qhd->khd", weights.astype(jnp.bfloat16), grad_mix, preferred_element_type=jnp.float32
    )
    return (jnp.concatenate(grad_queries, 0), grad_keys, grad_values)


def swap(entry, axis, mask):
    count = lax.axis_size(axis)
    return lax.ppermute(entry, axis, [(place, place ^ mask) for place in range(count)])


def places():
    shard = lax.axis_index("shard")
    data = lax.axis_index("dp")
    return shard, data % 2, (data // 2) % 2


def assemble_kernel(place_ref, near, far, side, near2, far2, side2, full, sems):
    shard, core, plane = place_ref[0], place_ref[1], place_ref[2]
    rows = near.shape[2]
    copies = []

    def put(source, owner, part, which):
        row = pl.multiple_of(((owner * 3 + part) * 2 + which) * rows, rows)
        copies.append(
            pltpu.make_async_copy(source, full.at[pl.ds(row, rows), :], sems.at[len(copies)])
        )

    for which, (one, two, three) in ((core, (near, far, side)), (1 - core, (near2, far2, side2))):
        for step in range(4):
            for flip, ref in ((0, one), (1, two)):
                owner = shard ^ (2 * step + flip)
                put(ref.at[step, 0], owner, plane, which)
                put(ref.at[step, 1], owner, 2, which)
                put(three.at[4 * flip + step], owner, 1 - plane, which)
    for copy in copies:
        copy.start()
    for copy in copies:
        copy.wait()


def gather_weight(weight, place):
    shard, core, plane = place
    rows, columns = weight.shape[0] // 6, weight.shape[1]
    pieces = weight.astype(jnp.bfloat16).reshape(3, 2, rows, columns)
    mine = lax.dynamic_index_in_dim(pieces, core, 1, keepdims=False)
    own = jnp.stack([lax.dynamic_index_in_dim(mine, plane, 0, keepdims=False), mine[2]])
    near = jnp.stack([own] + [swap(own, "shard", mask) for mask in (2, 4, 6)])
    far = swap(near, "shard", 1)
    side = swap(jnp.concatenate([near[:, 0], far[:, 0]]), "dp", 2)
    near2, far2, side2 = (swap(entry, "dp", 1) for entry in (near, far, side))
    return pl.pallas_call(
        assemble_kernel,
        out_shape=jax.ShapeDtypeStruct((weight.shape[0] * 8, columns), jnp.bfloat16),
        in_specs=[pl.BlockSpec(memory_space=pltpu.SMEM)] + [pl.BlockSpec(memory_space=pl.ANY)] * 6,
        out_specs=pl.BlockSpec(memory_space=pltpu.VMEM),
        scratch_shapes=[pltpu.SemaphoreType.DMA((48,))],
    )(jnp.stack(place).astype(jnp.int32), near, far, side, near2, far2, side2)


def plus(*entries):
    return sum(entry.astype(jnp.float32) for entry in entries).astype(jnp.bfloat16)


def scatter_gradient(gradient, place):
    shard, core, plane = place
    rows, columns = gradient.shape[0] // 48, gradient.shape[1]
    low = gradient.astype(jnp.bfloat16).reshape(8, 3, 2, rows, columns)
    pick = partial(lax.dynamic_index_in_dim, keepdims=False)
    half = plus(pick(low, core, 2), swap(pick(low, 1 - core, 2), "dp", 1))
    part = plus(pick(half, plane, 1), swap(pick(half, 1 - plane, 1), "dp", 2))
    both = jnp.stack([part, half[:, 2]], axis=1).reshape(4, 2, 2, rows, columns)
    flip = shard % 2
    column = plus(pick(both, flip, 1), swap(pick(both, 1 - flip, 1), "shard", 1))
    depth = shard // 2
    piece = plus(
        pick(column, depth, 0),
        *(swap(pick(column, depth ^ mask, 0), "shard", 2 * mask) for mask in (1, 2, 3)),
    )
    for bit in range(2, lax.axis_size("dp").bit_length() - 1):
        piece = plus(piece, swap(piece, "dp", 2**bit))
    other = swap(piece, "dp", 2)
    shared = plus(piece[1], other[1])
    first = jnp.where(plane == 0, piece[0], other[0])
    second = jnp.where(plane == 0, other[0], piece[0])
    mine = jnp.stack([first, second, shared])
    theirs = swap(mine, "dp", 1)
    low_core = jnp.where(core == 0, mine, theirs)
    high_core = jnp.where(core == 0, theirs, mine)
    whole = jnp.stack([low_core, high_core], axis=1).reshape(6 * rows, columns)
    return whole.astype(jnp.float32)


def total(entry, axes):
    for axis in axes:
        for bit in range(lax.axis_size(axis).bit_length() - 1):
            entry = entry + swap(entry, axis, 2**bit)
    return entry


def body(
    tokens,
    picture_ids,
    cotangent,
    w_qkv,
    w_out,
    w_fc1,
    w_fc2,
    vectors,
    fc1_bias,
    moments_qkv,
    moments_out,
    moments_fc1,
    moments_fc2,
    moments_vectors,
    moments_fc1_bias,
):
    model_width = tokens.shape[1]
    masters = (w_qkv, w_out, w_fc1, w_fc2, vectors, fc1_bias)
    moments = (
        moments_qkv,
        moments_out,
        moments_fc1,
        moments_fc2,
        moments_vectors,
        moments_fc1_bias,
    )
    place = places()
    shard = place[0]
    model_owned = vectors.shape[1]
    hidden_owned = fc1_bias.shape[0]
    small = jnp.concatenate([vectors.reshape(-1), fc1_bias]).astype(jnp.bfloat16).reshape(1, 1, -1)
    for mask in (1, 2, 4):
        small = jnp.concatenate([small, swap(small, "shard", mask)])
    small = jnp.take(small.reshape(8, -1), shard ^ jnp.arange(8), axis=0)
    vector_low = jnp.moveaxis(small[:, : 8 * model_owned].reshape(8, 8, model_owned), 0, 1).reshape(8, -1)
    fc1_bias_low = small[:, 8 * model_owned :].reshape(-1)
    qkv_low, out_low, fc1_low, fc2_low = (
        gather_weight(entry, place) for entry in (w_qkv, w_out, w_fc1, w_fc2)
    )
    vector_rows = vector_low.astype(jnp.float32)
    fc1_shift = fc1_bias_low.astype(jnp.float32)
    stream = tokens.astype(jnp.float32)
    normed_one, norm_one_back = jax.vjp(layer_norm, stream, vector_rows[0], vector_rows[1])
    act_one = normed_one.astype(jnp.bfloat16)
    projected = jnp.dot(act_one, qkv_low, preferred_element_type=jnp.float32)
    queries = (projected[:, :model_width] + vector_rows[2]).astype(jnp.bfloat16)
    key_rows = projected[:, model_width : 2 * model_width].astype(jnp.bfloat16)
    values = (projected[:, 2 * model_width :] + vector_rows[3]).astype(jnp.bfloat16)
    row_count = tokens.shape[0] // ROW
    head_shape = (row_count, ROW, HEADS, HEAD_DIM)
    block_size = min(512, ROW)
    score_scale = HEAD_DIM ** (-0.5)
    row_pictures = picture_ids.reshape(row_count, ROW)
    query_heads = queries.reshape(head_shape)
    key_heads = key_rows.reshape(head_shape)
    value_heads = values.reshape(head_shape)
    mixture, log_total = lax.map(
        partial(attend_forward, block_size=block_size, score_scale=score_scale),
        (query_heads, key_heads, value_heads, row_pictures),
    )
    mixture_low = mixture.reshape(-1, model_width).astype(jnp.bfloat16)
    attention = jnp.dot(mixture_low, out_low, preferred_element_type=jnp.float32) + vector_rows[4]
    middle = stream + attention
    normed_two, norm_two_back = jax.vjp(layer_norm, middle, vector_rows[5], vector_rows[6])
    act_two = normed_two.astype(jnp.bfloat16)
    preact = jnp.dot(act_two, fc1_low, preferred_element_type=jnp.float32) + fc1_shift
    hidden, gelu_back = jax.vjp(gelu_tanh, preact)
    hidden_low = hidden.astype(jnp.bfloat16)
    feedforward = jnp.dot(hidden_low, fc2_low, preferred_element_type=jnp.float32) + vector_rows[7]
    result = middle + feedforward
    layer_out = result.astype(jnp.bfloat16)
    valid_rows = (picture_ids != 0).astype(jnp.float32)[:, None]
    stream_local = jnp.stack(
        [
            jnp.sum(valid_rows * entry * entry)
            for entry in (stream, attention, middle, feedforward, result)
        ]
        + [jnp.sum(valid_rows)]
    )
    grad_result = cotangent.astype(jnp.float32)
    grad_fc2_shift = jnp.sum(grad_result, axis=0)
    grad_fc2 = jnp.einsum("tf,td->fd", hidden_low, cotangent, preferred_element_type=jnp.float32)
    grad_hidden = jnp.einsum("td,fd->tf", cotangent, fc2_low, preferred_element_type=jnp.float32)
    grad_preact = gelu_back(grad_hidden)[0]
    grad_fc1_shift = jnp.sum(grad_preact, axis=0)
    grad_preact_low = grad_preact.astype(jnp.bfloat16)
    grad_fc1 = jnp.einsum("te,tf->ef", act_two, grad_preact_low, preferred_element_type=jnp.float32)
    grad_act_two = jnp.einsum(
        "tf,ef->te", grad_preact_low, fc1_low, preferred_element_type=jnp.float32
    )
    grad_mid_norm, grad_scale_two, grad_shift_two = norm_two_back(grad_act_two)
    grad_middle = grad_result + grad_mid_norm
    grad_out_shift = jnp.sum(grad_middle, axis=0)
    grad_middle_low = grad_middle.astype(jnp.bfloat16)
    grad_out = jnp.einsum(
        "te,td->ed", mixture_low, grad_middle_low, preferred_element_type=jnp.float32
    )
    grad_mixture = jnp.einsum(
        "td,ed->te", grad_middle_low, out_low, preferred_element_type=jnp.float32
    ).astype(jnp.bfloat16)
    grad_q, grad_k, grad_v = lax.map(
        partial(attend_backward, block_size=block_size, score_scale=score_scale),
        (
            query_heads,
            key_heads,
            value_heads,
            grad_mixture.reshape(head_shape),
            row_pictures,
            log_total,
        ),
    )
    grad_q = grad_q.reshape(-1, model_width)
    grad_k = grad_k.reshape(-1, model_width)
    grad_v = grad_v.reshape(-1, model_width)
    grad_query_shift = jnp.sum(grad_q, axis=0)
    grad_value_shift = jnp.sum(grad_v, axis=0)
    grad_projected = jnp.concatenate([grad_q, grad_k, grad_v], axis=1).astype(jnp.bfloat16)
    grad_qkv = jnp.einsum("te,tf->ef", act_one, grad_projected, preferred_element_type=jnp.float32)
    grad_act_one = jnp.einsum(
        "tf,ef->te", grad_projected, qkv_low, preferred_element_type=jnp.float32
    )
    grad_stream_norm, grad_scale_one, grad_shift_one = norm_one_back(grad_act_one)
    tokens_grad = (grad_middle + grad_stream_norm).astype(jnp.bfloat16)
    grad_vectors = jnp.stack(
        [
            grad_scale_one,
            grad_shift_one,
            grad_query_shift,
            grad_value_shift,
            grad_out_shift,
            grad_scale_two,
            grad_shift_two,
            grad_fc2_shift,
        ]
    )
    vector_count = grad_vectors.size
    small_sums = total(
        jnp.concatenate([grad_vectors.reshape(-1), grad_fc1_shift, stream_local]), ("dp", "shard")
    )
    stream_sums = small_sums[-6:]
    vector_sums = small_sums[:vector_count].reshape(grad_vectors.shape)
    shift_sums = small_sums[vector_count:-6]
    owner_grads = [
        scatter_gradient(entry, place) for entry in (grad_fc2, grad_fc1, grad_out, grad_qkv)
    ][::-1]
    square_sum = total(sum(jnp.sum(entry * entry) for entry in owner_grads), ("shard",))
    square_sum = square_sum + jnp.sum(small_sums[:-6] * small_sums[:-6])
    owner_grads = (
        *owner_grads,
        lax.dynamic_slice_in_dim(vector_sums, shard * model_owned, model_owned, 1),
        lax.dynamic_slice_in_dim(shift_sums, shard * hidden_owned, hidden_owned, 0),
    )
    stream_rms = jnp.sqrt(stream_sums[:5] / (stream_sums[5] * model_width))
    clip_factor = CLIP_NORM / jnp.maximum(jnp.sqrt(square_sum), CLIP_NORM)
    correction = 1.0 - ADAM_BETA**STEP
    updated = []
    for number in range(6):
        clipped = owner_grads[number] * clip_factor
        first_moment = ADAM_BETA * moments[number][0] + (1.0 - ADAM_BETA) * clipped
        second_moment = ADAM_BETA * moments[number][1] + (1.0 - ADAM_BETA) * clipped * clipped
        change = first_moment / correction / (jnp.sqrt(second_moment / correction) + ADAM_EPS)
        if number < 4:
            change = change + WEIGHT_DECAY * masters[number]
        if number == 4:
            updated.append(LEARN_RATE * change)
        else:
            updated.append(masters[number] - LEARN_RATE * change)
    return (
        layer_out,
        tokens_grad,
        owner_grads[0],
        owner_grads[1],
        owner_grads[2],
        owner_grads[3],
        owner_grads[4],
        owner_grads[5],
        updated[0],
        updated[1],
        updated[2],
        updated[3],
        updated[4],
        updated[5],
        stream_rms,
    )


def solution(mesh):
    placed = (
        P(("dp", "shard"), None),
        P(("dp", "shard")),
        P(("dp", "shard"), None),
        P("shard", None),
        P("shard", None),
        P("shard", None),
        P("shard", None),
        P(None, "shard"),
        P("shard"),
        P(None, "shard", None),
        P(None, "shard", None),
        P(None, "shard", None),
        P(None, "shard", None),
        P(None, None, "shard"),
        P(None, "shard"),
    )
    return jax.shard_map(
        body,
        mesh=mesh,
        in_specs=placed,
        out_specs=(
            P(("dp", "shard"), None),
            P(("dp", "shard"), None),
            P("shard", None),
            P("shard", None),
            P("shard", None),
            P("shard", None),
            P(None, "shard"),
            P("shard"),
            P("shard", None),
            P("shard", None),
            P("shard", None),
            P("shard", None),
            P(None, "shard"),
            P("shard"),
            P(),
        ),
        check_vma=False,
    )
```

```python
from functools import partial

import jax
import jax.numpy as jnp
from jax import lax
from jax.experimental import pallas as pl
from jax.experimental.pallas import tpu as pltpu
from jax.sharding import PartitionSpec as P

HEADS = 12
HEAD_DIM = 64
ROW = 512
STEP = 2

NORM_EPS = 1e-06
ADAM_BETA = 0.5
LEARN_RATE = 0.03
WEIGHT_DECAY = 0.1
ADAM_EPS = 1e-08
CLIP_NORM = 1.0
MASKED = -1e30
GELU_SCALE = 0.7978845608028654
GELU_CUBE = 0.044715

LOW = jnp.bfloat16
WIDE = jnp.float32


def swap(entry, axis, mask, name="sums"):
    count = lax.axis_size(axis)
    with jax.named_scope(name + "_" + axis + str(mask)):
        return lax.ppermute(entry, axis, [(place, place ^ mask) for place in range(count)])


def in_vmem():
    return pl.BlockSpec(memory_space=pltpu.VMEM)


def in_hbm():
    return pl.BlockSpec(memory_space=pltpu.HBM)


def hbm(entries):
    return [pltpu.with_memory_space_constraint(entry, pltpu.HBM) for entry in entries]


def in_smem():
    return pl.BlockSpec(memory_space=pltpu.SMEM)


def shape(dims, kind=LOW):
    return jax.ShapeDtypeStruct(dims, kind)


def cost(flops, moved):
    return pl.CostEstimate(flops=1, bytes_accessed=1, transcendentals=0)


def kernel_params(mib):
    return pltpu.CompilerParams(vmem_limit_bytes=mib * 2**20)


def dot(left, right):
    return jnp.dot(left, right, preferred_element_type=WIDE)


def dot_t(left, right):
    return lax.dot_general(left, right, (((1,), (1,)), ((), ())), preferred_element_type=WIDE)


def normalize(entries):
    center = entries - jnp.mean(entries, axis=-1, keepdims=True)
    scale = lax.rsqrt(jnp.mean(center * center, axis=-1, keepdims=True) + NORM_EPS)
    return center * scale, scale


def normalize_back(grad, normed, scale):
    inner = jnp.mean(grad * normed, axis=-1, keepdims=True)
    return scale * (grad - jnp.mean(grad, axis=-1, keepdims=True) - normed * inner)


def column_sum(entries):
    return jnp.sum(entries, axis=0, keepdims=True)


def own_pieces_kernel(place_ref, *refs):
    sources, vectors_ref, shift_ref = refs[:4], refs[4], refs[5]
    qkv_ref, mid_ref, fc2_ref = refs[6:9]
    scratch, sem = refs[9:13], refs[13]
    core, plane = place_ref[1], place_ref[2]
    copies = []
    for source, held in zip(sources, scratch):
        slots, rows, lanes = held.shape
        parts = (plane, 2) if slots == 2 else (0, 1, 2)
        column = pl.multiple_of(core * lanes, 128)
        for slot, part in enumerate(parts):
            start = pl.multiple_of(part * rows, rows)
            copies.append(
                pltpu.make_async_copy(
                    source.at[pl.ds(start, rows), pl.ds(column, lanes)],
                    held.at[slot],
                    sem.at[len(copies)],
                )
            )
    for copy in copies:
        copy.start()
    for copy in copies:
        copy.wait()
    qkv, out, fc1, fc2 = scratch
    width = qkv.shape[2]
    qkv_ref[:, :, :width] = qkv[...].astype(LOW)
    qkv_ref[:, :, width:] = jnp.zeros((2, qkv.shape[1], 128), LOW)
    qkv_ref[1, 0:8, width : width + vectors_ref.shape[1]] = vectors_ref[...].astype(LOW)
    qkv_ref[1, 8 : 8 + shift_ref.shape[0], width:] = shift_ref[...].astype(LOW)
    width = out.shape[2]
    mid_ref[:, :, :width] = out[...].astype(LOW)
    mid_ref[:, :, width:] = fc1[...].astype(LOW)
    fc2_ref[...] = fc2[...].astype(LOW)


def own_pieces(place, w_qkv, w_out, w_fc1, w_fc2, vectors, fc1_bias):
    weights = (w_qkv, w_out, w_fc1, w_fc2)
    dims = [
        (slots, entry.shape[0] // 3, entry.shape[1] // 2)
        for slots, entry in zip((2, 2, 2, 3), weights)
    ]
    rows = dims[0][1]
    return pl.pallas_call(
        own_pieces_kernel,
        out_shape=[
            shape((2, rows, dims[0][2] + 128)),
            shape((2, rows, dims[1][2] + dims[2][2])),
            shape(dims[3]),
        ],
        in_specs=[in_smem()] + [in_hbm()] * 4 + [in_vmem()] * 2,
        out_specs=[in_vmem()] * 3,
        scratch_shapes=[pltpu.VMEM(entry, WIDE) for entry in dims] + [pltpu.SemaphoreType.DMA((9,))],
        compiler_params=kernel_params(8),
    )(place, *hbm(weights), vectors, fc1_bias.reshape(-1, 128))


def after(entry, *others):
    return lax.optimization_barrier((entry, *others))[0]


def sync(*entries):
    leaves, tree = jax.tree.flatten(entries)
    return jax.tree.unflatten(tree, lax.optimization_barrier(leaves))


def gather_z(own, name):
    return [own] + [swap(own, "shard", mask, name) for mask in (2, 4, 6)]


def gather_x(near, name):
    return swap(near, "shard", 1, name)


def gather_y(near, far, name, lanes=None):
    return swap(jnp.concatenate([near[0, :, :, :lanes], far[0, :, :, :lanes]]), "dp", 2, name)


def gather_core(entry, name):
    return swap(entry, "dp", 1, name)


def load_weight(place_ref, pieces, first, width, full, sem):
    shard, core, plane = place_ref[0], place_ref[1], place_ref[2]
    rows = pieces[0].shape[2]
    lanes = pl.ds(first, width)

    def put(source, owner, part, which):
        row = pl.multiple_of((owner * 3 + part) * rows, rows)
        column = pl.multiple_of(which * width, 128)
        pltpu.make_async_copy(source, full.at[pl.ds(row, rows), pl.ds(column, width)], sem).start()

    count = len(pieces) // 2
    for which, half in ((core, pieces[:count]), (1 - core, pieces[count:])):
        for flip in range(2):
            for step in range(4):
                owner = shard ^ (2 * step + flip)
                if count == 2:
                    for part in range(3):
                        put(half[flip].at[part, step, :, lanes], owner, part, which)
                else:
                    put(half[flip].at[0, step, :, lanes], owner, plane, which)
                    put(half[flip].at[1, step, :, lanes], owner, 2, which)
                    put(half[2].at[4 * flip + step, :, lanes], owner, 1 - plane, which)
    return pltpu.make_async_copy(full, full, sem)


def gather_vectors(place_ref, near, far, held, sem, vec_ref, shift_ref):
    lane = near.shape[3] - 128
    owned = vec_ref.shape[1] // 8
    for flip, ref in ((0, near), (1, far)):
        for step in range(4):
            source = ref.at[1, step, pl.ds(0, 16), pl.ds(lane, 128)]
            pltpu.make_async_copy(source, held.at[4 * flip + step], sem).start()
    pltpu.make_async_copy(held, held, sem).wait()
    source = lax.broadcasted_iota(jnp.int32, (128, vec_ref.shape[1]), 0)
    target = lax.broadcasted_iota(jnp.int32, (128, vec_ref.shape[1]), 1)
    rows = jnp.zeros((16, vec_ref.shape[1]), WIDE)
    count = shift_ref.shape[1] // (8 * 128)
    for order in range(8):
        owner = place_ref[0] ^ (2 * (order % 4) + order // 4)
        move = (target == source + owner * owned) & (source < owned)
        rows = rows + dot(held[order], move.astype(WIDE).astype(LOW))
        for row in range(count):
            start = pl.multiple_of((owner * count + row) * 128, 128)
            shift_ref[0:1, pl.ds(start, 128)] = held[order, 8 + row : 9 + row, :].astype(WIDE)
    vec_ref[...] = rows[0:8]


def attention_kernel(place_ref, stream_ref, ids_column_ref, ids_row_ref, *refs):
    pieces = refs[:6]
    vec_ref, shift_ref, a1_t_ref, mix_ref, mix_t_ref, qkv_out, prob_out = refs[6:13]
    weight, qkv_ref, prob, bias, v_t, weight_sem, vec_held, vec_sem, out_sem = refs[13:]
    width = mix_ref.shape[1]
    pairs = width // 128
    loading = load_weight(place_ref, pieces, 0, weight.shape[1] // 2, weight, weight_sem)
    gather_vectors(place_ref, *pieces[:2], vec_held, vec_sem, vec_ref, shift_ref)
    normed, _ = normalize(stream_ref[...].astype(WIDE))
    a1 = (normed * vec_ref[0:1, :] + vec_ref[1:2, :]).astype(LOW)
    a1_t_ref[...] = a1.T
    bias[...] = jnp.where(ids_column_ref[...] == ids_row_ref[...], 0.0, MASKED)
    loading.wait()
    queries = dot(a1, weight[:, :width]) + vec_ref[2:3, :]
    qkv_ref[:, :width] = queries.astype(LOW)
    qkv_ref[:, width : 2 * width] = dot(a1, weight[:, width : 2 * width]).astype(LOW)
    values = (dot(a1, weight[:, 2 * width :]) + vec_ref[3:4, :]).astype(LOW)
    qkv_ref[:, 2 * width :] = values
    qkv_copy = pltpu.make_async_copy(qkv_ref, qkv_out, out_sem.at[pairs])
    qkv_copy.start()
    v_t[...] = values.T

    def out_copy(pair):
        heads = pl.ds(2 * pair, 2)
        return pltpu.make_async_copy(prob.at[heads], prob_out.at[heads], out_sem.at[pair])

    left = lax.broadcasted_iota(jnp.int32, (ROW, 128), 1) < HEAD_DIM

    @pl.loop(0, pairs)
    def _(pair):
        lane = pl.multiple_of(pair * 128, 128)
        scaled = qkv_ref[:, pl.ds(lane, 128)] * HEAD_DIM**-0.5
        keys = qkv_ref[:, pl.ds(width + lane, 128)]
        for half in range(2):
            key_half = jnp.where(left == (half == 0), keys, jnp.zeros_like(keys))
            v_rows = pl.ds(pl.multiple_of(lane + half * HEAD_DIM, HEAD_DIM), HEAD_DIM)
            for block in range(2):
                rows = slice(block * 256, block * 256 + 256)
                scores = dot_t(key_half, scaled[rows]) + bias[:, rows]
                weights = jnp.exp(scores - jnp.max(scores, axis=0, keepdims=True))
                weights = weights * (1.0 / jnp.sum(weights, axis=0, keepdims=True))
                low = weights.astype(LOW)
                prob[2 * pair + half, :, rows] = low
                mix_t_ref[v_rows, rows] = dot(v_t[v_rows, :], low).astype(LOW)
        out_copy(pair).start()

    mix_ref[...] = mix_t_ref[...].T
    qkv_copy.wait()

    @pl.loop(0, pairs)
    def _(pair):
        out_copy(pair).wait()


def attention(place, stream, ids, hidden, pieces):
    width = stream.shape[1]
    return pl.pallas_call(
        attention_kernel,
        out_shape=[
            shape((8, width), WIDE),
            shape((1, hidden), WIDE),
            shape((width, ROW)),
            shape((ROW, width)),
            shape((width, ROW)),
            pltpu.HBM((ROW, 3 * width), LOW),
            pltpu.HBM((HEADS, ROW, ROW), LOW),
        ],
        in_specs=[in_smem()] + [in_vmem()] * 3 + [in_hbm()] * 6,
        out_specs=[in_vmem()] * 5 + [in_hbm()] * 2,
        scratch_shapes=[
            pltpu.VMEM((width, 3 * width), LOW),
            pltpu.VMEM((ROW, 3 * width), LOW),
            pltpu.VMEM((HEADS, ROW, ROW), LOW),
            pltpu.VMEM((ROW, ROW), WIDE),
            pltpu.VMEM((width, ROW), LOW),
            pltpu.SemaphoreType.DMA,
            pltpu.VMEM((8, 16, 128), LOW),
            pltpu.SemaphoreType.DMA,
            pltpu.SemaphoreType.DMA((HEADS // 2 + 1,)),
        ],
        compiler_params=kernel_params(22),
        cost_estimate=cost(12e9, 24e6),
    )(place, stream, ids.reshape(ROW, 1), ids.reshape(1, ROW), *hbm(pieces))


def hidden_kernel(place_ref, tokens_ref, mix_ref, valid_ref, vec_ref, bias_ref, *refs):
    pieces = refs[:6]
    mid_ref, a2_t_ref, act_ref, act_t_ref, slope_ref, sums_ref, w_out, w_fc1 = refs[6:14]
    out_sem, fc1_sem = refs[14:]
    width = tokens_ref.shape[1]
    hidden = bias_ref.shape[1]
    out_ready = load_weight(place_ref, pieces, 0, width // 2, w_out, out_sem)
    fc1_ready = load_weight(place_ref, pieces, width // 2, hidden // 2, w_fc1, fc1_sem)
    stream = tokens_ref[...].astype(WIDE)
    valid = valid_ref[...]
    out_ready.wait()
    branch = dot(mix_ref[...], w_out[...]) + vec_ref[4:5, :]
    middle = stream + branch
    mid_ref[...] = middle
    sums_ref[0:1, :] = column_sum(valid * stream * stream)
    sums_ref[1:2, :] = column_sum(valid * branch * branch)
    sums_ref[2:3, :] = column_sum(valid * middle * middle)
    sums_ref[3:8, :] = jnp.zeros((5, width), WIDE)
    normed, _ = normalize(middle)
    a2 = (normed * vec_ref[5:6, :] + vec_ref[6:7, :]).astype(LOW)
    a2_t_ref[...] = a2.T
    fc1_ready.wait()
    step = 512
    for first in range(0, hidden, step):
        lanes = slice(first, first + step)
        pre = dot(a2, w_fc1[:, lanes]) + bias_ref[:, lanes]
        square = pre * pre
        turn = jnp.tanh(GELU_SCALE * (pre + GELU_CUBE * (square * pre)))
        half = 0.5 * (1.0 + turn)
        act = (pre * half).astype(LOW)
        act_ref[:, lanes] = act
        act_t_ref[lanes, :] = act.T
        bend = (1.0 - turn * turn) * (GELU_SCALE + 3.0 * GELU_SCALE * GELU_CUBE * square)
        slope_ref[:, lanes] = (half + 0.5 * pre * bend).astype(LOW)


def hidden_layer(place, tokens, mix, valid, vec, bias, pieces):
    width, hidden = tokens.shape[1], bias.shape[1]
    return pl.pallas_call(
        hidden_kernel,
        out_shape=[
            shape((ROW, width), WIDE),
            shape((width, ROW)),
            shape((ROW, hidden)),
            shape((hidden, ROW)),
            shape((ROW, hidden)),
            shape((8, width), WIDE),
            shape((width, width)),
            shape((width, hidden)),
        ],
        in_specs=[in_smem()] + [in_vmem()] * 5 + [in_hbm()] * 6,
        out_specs=[in_vmem()] * 8,
        scratch_shapes=[
            pltpu.SemaphoreType.DMA,
            pltpu.SemaphoreType.DMA,
        ],
        compiler_params=kernel_params(16),
        cost_estimate=cost(10e9, 20e6),
    )(place, tokens, mix, valid, vec, bias, *hbm(pieces))


def hidden_back_kernel(place_ref, cot_ref, slope_ref, *refs):
    pieces = refs[:4]
    d_pre_ref, shift_ref, w_fc2, sem = refs[4:]
    hidden = slope_ref.shape[1]
    loading = load_weight(place_ref, pieces, 0, w_fc2.shape[1] // 2, w_fc2, sem)
    cot = cot_ref[...]
    loading.wait()
    step = 512
    for first in range(0, hidden, step):
        lanes = slice(first, first + step)
        d_pre = dot_t(cot, w_fc2[lanes, :]) * slope_ref[:, lanes].astype(WIDE)
        shift_ref[:, lanes] = column_sum(d_pre)
        d_pre_ref[:, lanes] = d_pre.astype(LOW)


def hidden_back(place, cot, slope, pieces):
    width, hidden = cot.shape[1], slope.shape[1]
    return pl.pallas_call(
        hidden_back_kernel,
        out_shape=[shape((ROW, hidden)), shape((1, hidden), WIDE), shape((hidden, width))],
        in_specs=[in_smem()] + [in_vmem()] * 2 + [in_hbm()] * 4,
        out_specs=[in_vmem()] * 3,
        scratch_shapes=[pltpu.SemaphoreType.DMA],
        compiler_params=kernel_params(18),
        cost_estimate=cost(3e9, 14e6),
    )(place, cot, slope, *hbm(pieces))


def middle_kernel(mid_ref, act_ref, d_pre_ref, cot_ref, valid_ref, vec_ref, *refs):
    w_out, w_fc1, w_fc2 = refs[:3]
    layer_ref, d_mid_ref, d_mid_low_ref, d_mix_ref, sums_ref = refs[3:]
    middle = mid_ref[...]
    valid = valid_ref[...]
    mlp = dot(act_ref[...], w_fc2[...]) + vec_ref[7:8, :]
    result = middle + mlp
    layer_ref[...] = result.astype(LOW)
    sums_ref[4:5, :] = column_sum(valid * mlp * mlp)
    sums_ref[5:6, :] = column_sum(valid * result * result)
    sums_ref[6:8, :] = jnp.zeros((2, mid_ref.shape[1]), WIDE)
    d_a2 = dot_t(d_pre_ref[...], w_fc1[...])
    normed, scale = normalize(middle)
    dy = cot_ref[...].astype(WIDE)
    d_mid = dy + normalize_back(d_a2 * vec_ref[5:6, :], normed, scale)
    d_mid_ref[...] = d_mid
    low = d_mid.astype(LOW)
    d_mid_low_ref[...] = low
    sums_ref[0:1, :] = column_sum(d_mid)
    sums_ref[1:2, :] = column_sum(d_a2 * normed)
    sums_ref[2:3, :] = column_sum(d_a2)
    sums_ref[3:4, :] = column_sum(dy)
    d_mix_ref[...] = dot_t(low, w_out[...]).astype(LOW)


def middle_layer(mid, act, d_pre, cot, valid, vec, w_out, w_fc1, w_fc2):
    width = mid.shape[1]
    return pl.pallas_call(
        middle_kernel,
        out_shape=[
            shape((ROW, width)),
            shape((ROW, width), WIDE),
            shape((ROW, width)),
            shape((ROW, width)),
            shape((8, width), WIDE),
        ],
        in_specs=[in_vmem()] * 9,
        out_specs=[in_vmem()] * 5,
        compiler_params=kernel_params(20),
        cost_estimate=cost(14e9, 30e6),
    )(mid, act, d_pre, cot, valid, vec, w_out, w_fc1, w_fc2)


def attention_back_kernel(qkv_ref, mix_t_ref, d_mix_ref, prob_in, d_proj_ref, sums_ref, *rest):
    k_t, d_mix_t, d_q_t, prob, sem = rest
    width = mix_t_ref.shape[0]
    pairs = width // 128

    def in_copy(pair):
        heads = pl.ds(2 * pair, 2)
        return pltpu.make_async_copy(prob_in.at[heads], prob.at[heads], sem.at[pair])

    @pl.loop(0, pairs)
    def _(pair):
        in_copy(pair).start()


    k_t[...] = qkv_ref[:, width : 2 * width].T
    d_mix_t[...] = d_mix_ref[...].T
    left = lax.broadcasted_iota(jnp.int32, (ROW, 128), 1) < HEAD_DIM

    @pl.loop(0, pairs)
    def _(pair):
        lane = pl.multiple_of(pair * 128, 128)
        queries = qkv_ref[:, pl.ds(lane, 128)]
        values = qkv_ref[:, pl.ds(2 * width + lane, 128)]
        d_mix = d_mix_ref[:, pl.ds(lane, 128)]
        in_copy(pair).wait()
        d_keys, d_values = [], []
        for half in range(2):
            rows = pl.ds(pl.multiple_of(lane + half * HEAD_DIM, HEAD_DIM), HEAD_DIM)
            inner = column_sum(mix_t_ref[rows, :].astype(WIDE) * d_mix_t[rows, :].astype(WIDE))
            value_half = jnp.where(left == (half == 0), values, jnp.zeros_like(values))
            d_key, d_value = [], []
            for block in range(2):
                lanes = slice(block * 256, block * 256 + 256)
                low = prob[2 * pair + half, :, lanes]
                d_prob = dot_t(value_half, d_mix[lanes])
                d_score = (low.astype(WIDE) * (d_prob - inner[:, lanes])).astype(LOW)
                d_key.append(dot(d_score, queries[lanes]))
                d_value.append(dot(low, d_mix[lanes]))
                d_q_t[rows, lanes] = dot(k_t[rows, :], d_score)
            d_keys.append(d_key[0] + d_key[1])
            d_values.append(d_value[0] + d_value[1])
        d_k = jnp.where(left, d_keys[0], d_keys[1]) * HEAD_DIM**-0.5
        d_v = jnp.where(left, d_values[0], d_values[1])
        d_proj_ref[:, pl.ds(width + lane, 128)] = d_k.astype(LOW)
        d_proj_ref[:, pl.ds(2 * width + lane, 128)] = d_v.astype(LOW)
        sums_ref[1:2, pl.ds(lane, 128)] = column_sum(d_v)

    d_q = d_q_t[...].T * HEAD_DIM**-0.5
    d_proj_ref[:, :width] = d_q.astype(LOW)
    sums_ref[0:1, :] = column_sum(d_q)
    sums_ref[2:8, :] = jnp.zeros((6, width), WIDE)


def attention_back(qkv, mix_t, d_mix, prob):
    width = mix_t.shape[0]
    heads = prob.shape[0]
    return pl.pallas_call(
        attention_back_kernel,
        out_shape=[shape((ROW, 3 * width)), shape((8, width), WIDE)],
        in_specs=[in_vmem()] * 3 + [in_hbm()],
        out_specs=[in_vmem()] * 2,
        scratch_shapes=[
            pltpu.VMEM((width, ROW), LOW),
            pltpu.VMEM((width, ROW), LOW),
            pltpu.VMEM((width, ROW), WIDE),
            pltpu.VMEM((heads, ROW, ROW), LOW),
            pltpu.SemaphoreType.DMA((heads // 2,)),
        ],
        compiler_params=kernel_params(20),
        cost_estimate=cost(1.2e9 * heads, 2e6 * heads),
    )(qkv, mix_t, d_mix, *hbm([prob]))


def first_norm_kernel(place_ref, tokens_ref, d_proj_ref, d_mid_ref, vec_ref, *refs):
    pieces = refs[:6]
    grad_ref, sums_ref, weight, sem = refs[6:]
    loading = load_weight(place_ref, pieces, 0, weight.shape[1] // 2, weight, sem)
    normed, scale = normalize(tokens_ref[...].astype(WIDE))
    loading.wait()
    d_a1 = dot_t(d_proj_ref[...], weight[...])
    d_in = normalize_back(d_a1 * vec_ref[0:1, :], normed, scale)
    grad_ref[...] = (d_mid_ref[...] + d_in).astype(LOW)
    sums_ref[0:1, :] = column_sum(d_a1 * normed)
    sums_ref[1:2, :] = column_sum(d_a1)
    sums_ref[2:8, :] = jnp.zeros((6, d_a1.shape[1]), WIDE)


def first_norm_back(place, tokens, d_proj, d_mid, vec, pieces):
    width = tokens.shape[1]
    return pl.pallas_call(
        first_norm_kernel,
        out_shape=[shape((ROW, width)), shape((8, width), WIDE)],
        in_specs=[in_smem()] + [in_vmem()] * 4 + [in_hbm()] * 6,
        out_specs=[in_vmem()] * 2,
        scratch_shapes=[pltpu.VMEM((width, d_proj.shape[1]), LOW), pltpu.SemaphoreType.DMA],
        compiler_params=kernel_params(16),
        cost_estimate=pl.CostEstimate(flops=4_000_000_000, bytes_accessed=1, transcendentals=0),
    )(place, tokens, d_proj, d_mid, vec, *hbm(pieces))


def product_half(left_refs, right_ref, which, sums, first):
    half = right_ref.shape[1] // 2
    row = 0
    for left_ref in left_refs:
        count = left_ref.shape[0]
        for start in range(0, half, 384):
            lane = pl.multiple_of(which * half + start, 128)
            sums[row : row + count, first + start : first + start + 384] = dot(
                left_ref[...], right_ref[:, pl.ds(lane, 384)]
            )
        row += count


def products(groups, refs, which, sums):
    first = 0
    for count in groups:
        product_half(refs[:count], refs[count], which, sums, first)
        first += refs[count].shape[1] // 2
        refs = refs[count + 1 :]


def give_kernel(groups, place_ref, *refs):
    out_ref, sums = refs[-2:]
    shard, core = place_ref[0], place_ref[1]
    products(groups, refs[:-2], 1 - core, sums)
    rows = out_ref.shape[2]
    for order in range(8):
        owner = shard ^ (2 * (order % 4) + order // 4)
        for part in range(3):
            start = pl.multiple_of((owner * 3 + part) * rows, rows)
            out_ref[order, part] = sums[pl.ds(start, rows), :].astype(LOW)


def keep_kernel(groups, place_ref, received_ref, *refs):
    give_ref, keep_ref, sums = refs[-3:]
    shard, core, plane = place_ref[0], place_ref[1], place_ref[2]
    products(groups, refs[:-3], core, sums)
    rows = give_ref.shape[1]
    for order in range(8):
        owner = shard ^ (2 * (order % 4) + order // 4)

        def total(part):
            start = pl.multiple_of((owner * 3 + part) * rows, rows)
            mine = sums[pl.ds(start, rows), :]
            return (mine + received_ref[order, part].astype(WIDE)).astype(LOW)

        give_ref[order] = total(1 - plane)
        keep_ref[0, order] = total(plane)
        keep_ref[1, order] = total(2)


class Reduction:
    def __init__(self, place, groups):
        self.place = place
        self.counts = tuple(len(group) - 1 for group in groups)
        self.operands = [entry for group in groups for entry in group]
        self.height = sum(entry.shape[0] for entry in groups[0][:-1])
        self.half = sum(group[-1].shape[1] for group in groups) // 2
        self.rows = self.height // 24
        self.scratch = [pltpu.VMEM((self.height, self.half), WIDE)]
        self.cost = cost(2 * self.height * self.half * ROW, 4 * self.height * self.half)

    def give(self):
        return pl.pallas_call(
            partial(give_kernel, self.counts),
            out_shape=shape((8, 3, self.rows, self.half)),
            in_specs=[in_smem()] + [in_vmem()] * len(self.operands),
            out_specs=in_vmem(),
            scratch_shapes=self.scratch,
            compiler_params=kernel_params(10),
            cost_estimate=self.cost,
        )(self.place, *self.operands)

    def keep(self, received):
        return pl.pallas_call(
            partial(keep_kernel, self.counts),
            out_shape=[shape((8, self.rows, self.half)), shape((2, 8, self.rows, self.half))],
            in_specs=[in_smem()] + [in_vmem()] * (1 + len(self.operands)),
            out_specs=[in_vmem()] * 2,
            scratch_shapes=self.scratch,
            compiler_params=kernel_params(12),
            cost_estimate=self.cost,
        )(self.place, received, *self.operands)

    def after_y(self, kept, side):
        sent = jnp.stack([plus(kept[0, 4:], side[4:]), kept[1, 4:]])
        return sent, (kept[0, :4], side[:4], kept[1, :4])

    def after_x(self, stay, column):
        kept, side, shared = stay
        return [
            jnp.stack([plus(kept[step], side[step], column[0, step]), plus(shared[step], column[1, step])])
            for step in range(4)
        ]

    def over_z(self, columns, name):
        return [swap(columns[step], "shard", 2 * step, name) for step in (1, 2, 3)]

    def after_z(self, mine, pieces):
        piece = plus(mine, *pieces)
        for bit in range(2, lax.axis_size("dp").bit_length() - 1):
            piece = plus(piece, swap(piece, "dp", 2**bit))
        return piece

    def after_y2(self, piece, other):
        shared = plus(piece[1], other[1])
        even = self.place[2] == 0
        first = jnp.where(even, piece[0], other[0])
        second = jnp.where(even, other[0], piece[0])
        return jnp.stack([first, second, shared])

    def halves(self, mine, theirs):
        low_core = self.place[1] == 0
        low, high = jnp.where(low_core, mine, theirs), jnp.where(low_core, theirs, mine)
        return low.reshape(3 * self.rows, self.half), high.reshape(3 * self.rows, self.half)


def plus(*entries):
    return sum(entry.astype(WIDE) for entry in entries).astype(LOW)


def total(entry, axes):
    for axis in axes:
        for bit in range(lax.axis_size(axis).bit_length() - 1):
            entry = entry + swap(entry, axis, 2**bit)
    return entry


def body(
    tokens,
    picture_ids,
    cotangent,
    w_qkv,
    w_out,
    w_fc1,
    w_fc2,
    vectors,
    fc1_bias,
    moments_qkv,
    moments_out,
    moments_fc1,
    moments_fc2,
    moments_vectors,
    moments_fc1_bias,
):
    model_width = tokens.shape[1]
    masters = (w_qkv, w_out, w_fc1, w_fc2, vectors, fc1_bias)
    moments = (
        moments_qkv,
        moments_out,
        moments_fc1,
        moments_fc2,
        moments_vectors,
        moments_fc1_bias,
    )
    shard = lax.axis_index("shard")
    data = lax.axis_index("dp")
    place = jnp.stack([shard, data % 2, (data // 2) % 2]).astype(jnp.int32)
    model_owned = vectors.shape[1]
    hidden_owned = fc1_bias.shape[0]
    valid = (picture_ids != 0).astype(WIDE)[:, None]
    own_a, own_b, own_c = own_pieces(place, w_qkv, w_out, w_fc1, w_fc2, vectors, fc1_bias)
    near_a = jnp.stack(gather_z(own_a, "A"), axis=1)
    near_a, own_b, own_c = sync(near_a, own_b, own_c)
    far_a, near2_a = gather_x(near_a, "A"), gather_core(near_a, "A")
    near_b = jnp.stack(gather_z(own_b, "B"), axis=1)
    far_a, near_b = sync(far_a, near_b)
    side_a = gather_y(near_a, far_a, "A", w_qkv.shape[1] // 2)
    far_b, near2_b = gather_x(near_b, "B"), gather_core(near_b, "B")
    far2_a, side2_a = gather_core(far_a, "A"), gather_core(side_a, "A")
    near_c = jnp.stack(gather_z(own_c, "C"), axis=1)
    pieces_a = (near_a, far_a, side_a, near2_a, far2_a, side2_a)
    far_b, near_c, side2_a = sync(far_b, near_c, side2_a)
    side_b, far2_b = gather_y(near_b, far_b, "B"), gather_core(far_b, "B")
    far_c, near2_c = gather_x(near_c, "C"), gather_core(near_c, "C")
    vec, bias, a1_t, mix, mix_t, qkv, prob = attention(
        place, after(tokens, far_b, near_c), picture_ids, w_fc1.shape[1], pieces_a
    )
    side_b, far2_b, mix = sync(side_b, far2_b, mix)
    side2_b = gather_core(side_b, "B")
    pieces_b = (near_b, far_b, side_b, near2_b, far2_b, side2_b)
    mid, a2_t, act, act_t, slope, sums_in, wide_out, wide_fc1 = hidden_layer(
        place, tokens, mix, valid, vec, bias, pieces_b
    )
    far_c, near2_c, act_t = sync(far_c, near2_c, act_t)
    far2_c = gather_core(far_c, "C")
    fc2 = Reduction(place, [(act_t, cotangent)])
    given = fc2.give()
    far2_c, given = sync(far2_c, given)
    recv_f2 = gather_core(given, "F2")
    pieces_c = (near_c, far_c, near2_c, far2_c)
    d_pre, shift_sum, wide_fc2 = hidden_back(place, cotangent, after(slope, given), pieces_c)
    recv_f2, d_pre = sync(recv_f2, d_pre)
    give_f2, keep_f2 = fc2.keep(recv_f2)
    side_f2 = swap(give_f2, "dp", 2, "F2")
    fc1 = Reduction(place, [(a2_t, after(d_pre, give_f2))])
    given = fc1.give()
    recv_f1 = gather_core(given, "F1")
    layer_out, d_mid, d_mid_low, d_mix, sums_mid = middle_layer(
        mid, act, after(d_pre, given), cotangent, valid, vec, wide_out, wide_fc1, wide_fc2
    )
    recv_f1, d_mix = sync(recv_f1, d_mix)
    give_f1, keep_f1 = fc1.keep(recv_f1)
    side_f2, give_f1, d_mix = sync(side_f2, give_f1, d_mix)
    sent, stay_f2 = fc2.after_y(keep_f2, side_f2)
    column_f2 = swap(sent, "shard", 1, "F2")
    side_f1 = swap(give_f1, "dp", 2, "F1")
    d_proj, sums_att = attention_back(qkv, mix_t, after(d_mix, sent), prob)
    first = Reduction(place, [(a1_t, d_proj), (mix_t, d_mid_low)])
    given = first.give()
    column_f2, side_f1, given = sync(column_f2, side_f1, given)
    recv_a = gather_core(given, "RA")
    columns = fc2.after_x(stay_f2, column_f2)
    pieces_f2, mine_f2 = fc2.over_z(columns, "F2"), columns[0]
    sent, stay_f1 = fc1.after_y(keep_f1, side_f1)
    column_f1 = swap(sent, "shard", 1, "F1")
    tokens_grad, sums_first = first_norm_back(
        place, tokens, d_proj, after(d_mid, columns, sent), vec, pieces_a
    )
    recv_a, sums_first = sync(recv_a, sums_first)
    give_a, keep_a = first.keep(recv_a)
    side_ra = swap(give_a, "dp", 2, "RA")
    small_sums = jnp.concatenate(
        [
            sums_first[:2],
            sums_att[:2],
            sums_mid[:4],
            shift_sum.reshape(-1, model_width),
            sums_in[:3],
            sums_mid[4:6],
            jnp.full((1, model_width), jnp.sum(valid)),
        ]
    )
    small_more = swap(small_sums, "dp", 1)
    pieces_f2, column_f1, give_a, small_more = sync(pieces_f2, column_f1, give_a, small_more)
    small_sums = small_sums + small_more
    columns = fc1.after_x(stay_f1, column_f1)
    pieces_f1, mine_f1 = fc1.over_z(columns, "F1"), columns[0]
    piece_f2 = fc2.after_z(mine_f2, pieces_f2)
    other_f2 = swap(piece_f2, "dp", 2, "F2")
    small_more = swap(small_sums, "dp", 2)
    side_ra, other_f2, small_more = sync(side_ra, other_f2, small_more)
    small_sums = small_sums + small_more
    sent, stay_a = first.after_y(keep_a, side_ra)
    column_a = swap(sent, "shard", 1, "RA")
    owned_f2 = fc2.after_y2(piece_f2, other_f2)
    theirs_f2 = gather_core(owned_f2, "F2")
    small_more = swap(small_sums, "shard", 1)
    pieces_f1, column_a, theirs_f2, small_more = sync(pieces_f1, column_a, theirs_f2, small_more)
    small_sums = small_sums + small_more
    columns = first.after_x(stay_a, column_a)
    pieces_ra, mine_a = first.over_z(columns, "RA"), columns[0]
    piece_f1 = fc1.after_z(mine_f1, pieces_f1)
    other_f1 = swap(piece_f1, "dp", 2, "F1")
    small_more = swap(small_sums, "shard", 2)
    pieces_ra, other_f1, small_more = sync(pieces_ra, other_f1, small_more)
    small_sums = small_sums + small_more
    piece_a = first.after_z(mine_a, pieces_ra)
    other_a = swap(piece_a, "dp", 2, "RA")
    owned_f1 = fc1.after_y2(piece_f1, other_f1)
    theirs_f1 = gather_core(owned_f1, "F1")
    small_more = swap(small_sums, "shard", 4)
    other_a, theirs_f1, small_more = sync(other_a, theirs_f1, small_more)
    small_sums = small_sums + small_more
    owned_a = first.after_y2(piece_a, other_a)
    theirs_a = gather_core(owned_a, "RA")
    for bit in range(2, lax.axis_size("dp").bit_length() - 1):
        small_sums = small_sums + swap(small_sums, "dp", 2**bit)
    fc2_halves, fc1_halves = fc2.halves(owned_f2, theirs_f2), fc1.halves(owned_f1, theirs_f1)
    first_halves = first.halves(owned_a, theirs_a)
    split = w_qkv.shape[1] // 2
    owner_grads = [
        jnp.concatenate([half[:, :split] for half in first_halves], axis=1).astype(WIDE),
        jnp.concatenate([half[:, split:] for half in first_halves], axis=1).astype(WIDE),
        jnp.concatenate(fc1_halves, axis=1).astype(WIDE),
        jnp.concatenate(fc2_halves, axis=1).astype(WIDE),
    ]
    grad_vectors, grad_shift = small_sums[:8], small_sums[8:12].reshape(-1)
    stream_sums = jnp.sum(small_sums[12:17], axis=1)
    square_sum = total(sum(jnp.sum(entry * entry) for entry in owner_grads), ("shard",))
    square_sum = square_sum + jnp.sum(small_sums[:12] * small_sums[:12])
    owner_grads = (
        *owner_grads,
        lax.dynamic_slice_in_dim(grad_vectors, shard * model_owned, model_owned, 1),
        lax.dynamic_slice_in_dim(grad_shift, shard * hidden_owned, hidden_owned, 0),
    )
    stream_rms = jnp.sqrt(stream_sums / (small_sums[17, 0] * model_width))
    clip_factor = CLIP_NORM / jnp.maximum(jnp.sqrt(square_sum), CLIP_NORM)
    correction = 1.0 - ADAM_BETA**STEP
    updated = []
    for number in range(6):
        clipped = owner_grads[number] * clip_factor
        first_moment = ADAM_BETA * moments[number][0] + (1.0 - ADAM_BETA) * clipped
        second_moment = ADAM_BETA * moments[number][1] + (1.0 - ADAM_BETA) * clipped * clipped
        change = first_moment / correction / (jnp.sqrt(second_moment / correction) + ADAM_EPS)
        if number < 4:
            change = change + WEIGHT_DECAY * masters[number]
        if number == 4:
            updated.append(LEARN_RATE * change)
        else:
            updated.append(masters[number] - LEARN_RATE * change)
    return (layer_out, tokens_grad, *owner_grads, *updated, stream_rms)


def solution(mesh):
    placed = (
        P(("dp", "shard"), None),
        P(("dp", "shard")),
        P(("dp", "shard"), None),
        P("shard", None),
        P("shard", None),
        P("shard", None),
        P("shard", None),
        P(None, "shard"),
        P("shard"),
        P(None, "shard", None),
        P(None, "shard", None),
        P(None, "shard", None),
        P(None, "shard", None),
        P(None, None, "shard"),
        P(None, "shard"),
    )
    return jax.shard_map(
        body,
        mesh=mesh,
        in_specs=placed,
        out_specs=(
            P(("dp", "shard"), None),
            P(("dp", "shard"), None),
            P("shard", None),
            P("shard", None),
            P("shard", None),
            P("shard", None),
            P(None, "shard"),
            P("shard"),
            P("shard", None),
            P("shard", None),
            P("shard", None),
            P("shard", None),
            P(None, "shard"),
            P("shard"),
            P(),
        ),
        check_vma=False,
    )
```

```python
from functools import partial

import jax
import jax.numpy as jnp
from jax import lax
from jax.experimental import pallas as pl
from jax.experimental.pallas import tpu as pltpu
from jax.sharding import PartitionSpec as P

HEADS = 12
HEAD_DIM = 64
ROW = 512
STEP = 2

NORM_EPS = 1e-06
ADAM_BETA = 0.5
LEARN_RATE = 0.03
WEIGHT_DECAY = 0.1
ADAM_EPS = 1e-08
CLIP_NORM = 1.0
MASKED = -1e30
GELU_SCALE = 0.7978845608028654
GELU_CUBE = 0.044715

LOW = jnp.bfloat16
WIDE = jnp.float32


def swap(entry, axis, mask, name="sums"):
    count = lax.axis_size(axis)
    with jax.named_scope(name + "_" + axis + str(mask)):
        return lax.ppermute(entry, axis, [(place, place ^ mask) for place in range(count)])


def in_vmem():
    return pl.BlockSpec(memory_space=pltpu.VMEM)


def in_hbm():
    return pl.BlockSpec(memory_space=pltpu.HBM)


def hbm(entries):
    return [pltpu.with_memory_space_constraint(entry, pltpu.HBM) for entry in entries]


def in_smem():
    return pl.BlockSpec(memory_space=pltpu.SMEM)


def shape(dims, kind=LOW):
    return jax.ShapeDtypeStruct(dims, kind)


def cost(flops, moved):
    return pl.CostEstimate(flops=1, bytes_accessed=1, transcendentals=0)


def kernel_params(mib):
    return pltpu.CompilerParams(vmem_limit_bytes=mib * 2**20)


def dot(left, right):
    return jnp.dot(left, right, preferred_element_type=WIDE)


def dot_t(left, right):
    return lax.dot_general(left, right, (((1,), (1,)), ((), ())), preferred_element_type=WIDE)


def normalize(entries):
    center = entries - jnp.mean(entries, axis=-1, keepdims=True)
    scale = lax.rsqrt(jnp.mean(center * center, axis=-1, keepdims=True) + NORM_EPS)
    return center * scale, scale


def normalize_back(grad, normed, scale):
    inner = jnp.mean(grad * normed, axis=-1, keepdims=True)
    return scale * (grad - jnp.mean(grad, axis=-1, keepdims=True) - normed * inner)


def column_sum(entries):
    return jnp.sum(entries, axis=0, keepdims=True)


def own_pieces_kernel(place_ref, *refs):
    sources, vectors_ref, shift_ref = refs[:4], refs[4], refs[5]
    qkv_ref, mid_ref, fc2_ref = refs[6:9]
    scratch, sem = refs[9:13], refs[13]
    core, plane = place_ref[1], place_ref[2]
    copies = []
    for number, (source, held) in enumerate(zip(sources, scratch)):
        rows, lanes = held.shape
        column = pl.multiple_of(core * lanes, 128)
        size = rows if number == 0 else rows // 2
        starts = (plane * size,) if number == 0 else (plane * size, 2 * size)
        for slot, start in enumerate(starts):
            start = pl.multiple_of(start, size)
            copies.append(
                pltpu.make_async_copy(
                    source.at[pl.ds(start, size), pl.ds(column, lanes)],
                    held.at[pl.ds(slot * size, size)],
                    sem.at[len(copies)],
                )
            )
    for copy in copies:
        copy.start()
    qkv, out, fc1, fc2 = scratch
    width = qkv.shape[1]
    qkv_ref[:, width:] = jnp.zeros((qkv.shape[0], 128), LOW)
    qkv_ref[0:8, width : width + vectors_ref.shape[1]] = vectors_ref[...].astype(LOW)
    qkv_ref[8 : 8 + shift_ref.shape[0], width:] = shift_ref[...].astype(LOW)
    for copy in copies:
        copy.wait()
    qkv_ref[:, :width] = qkv[...].astype(LOW)
    width = out.shape[1]
    mid_ref[:, :width] = out[...].astype(LOW)
    mid_ref[:, width:] = fc1[...].astype(LOW)
    fc2_ref[...] = fc2[...].astype(LOW)


def own_pieces(place, w_qkv, w_out, w_fc1, w_fc2, vectors, fc1_bias):
    weights = (w_qkv, w_out, w_fc1, w_fc2)
    dims = [
        (entry.shape[0] * share // 6, entry.shape[1] // 2)
        for share, entry in zip((3, 4, 4, 4), weights)
    ]
    return pl.pallas_call(
        own_pieces_kernel,
        out_shape=[
            shape((dims[0][0], dims[0][1] + 128)),
            shape((dims[1][0], dims[1][1] + dims[2][1])),
            shape(dims[3]),
        ],
        in_specs=[in_smem()] + [in_hbm()] * 4 + [in_vmem()] * 2,
        out_specs=[in_vmem()] * 3,
        scratch_shapes=[pltpu.VMEM(entry, WIDE) for entry in dims] + [pltpu.SemaphoreType.DMA((7,))],
        compiler_params=kernel_params(8),
    )(place, *hbm(weights), vectors, fc1_bias.reshape(-1, 128))


def after(entry, *others):
    return sync(entry, *others)[0]


def sync(*entries):
    leaves, tree = jax.tree.flatten(entries)
    return jax.tree.unflatten(tree, lax.optimization_barrier(leaves))


def gather_z(own, name):
    return [own] + [swap(own, "shard", mask, name) for mask in (2, 4, 6)]


def gather_x(near, name):
    return swap(near, "shard", 1, name)


def gather_y(near, far, name, rows=None, lanes=None):
    return swap(jnp.concatenate([near[:, :rows, :lanes], far[:, :rows, :lanes]]), "dp", 2, name)


def gather_core(entry, name):
    return swap(entry, "dp", 1, name)


def load_weight(place_ref, pieces, first, width, full, sem):
    shard, core, plane = place_ref[0], place_ref[1], place_ref[2]
    lanes = pl.ds(first, width)
    count = len(pieces) // 2
    owned = full.shape[0] // 8
    rows = pieces[2].shape[1] if count == 3 else owned
    shared = pieces[0].shape[1] - rows

    def put(source, owner, start, which):
        row = pl.multiple_of(owner * owned + start, 16)
        column = pl.multiple_of(which * width, 128)
        target = full.at[pl.ds(row, source.shape[0]), pl.ds(column, width)]
        pltpu.make_async_copy(source, target, sem).start()

    for which, half in ((core, pieces[:count]), (1 - core, pieces[count:])):
        for flip in range(2):
            for step in range(4):
                owner = shard ^ (2 * step + flip)
                ref = half[flip].at[step]
                put(ref.at[pl.ds(0, rows), lanes], owner, plane * rows if count == 3 else 0, which)
                if shared:
                    put(ref.at[pl.ds(rows, shared), lanes], owner, 2 * rows, which)
                if count == 3:
                    side = half[2].at[4 * flip + step, :, lanes]
                    put(side, owner, (1 - plane) * rows, which)
    return pltpu.make_async_copy(full, full, sem)


def gather_vectors(place_ref, near, far, held, sem, vec_ref, shift_ref):
    lane = near.shape[2] - 128
    owned = vec_ref.shape[1] // 8
    for flip, ref in ((0, near), (1, far)):
        for step in range(4):
            source = ref.at[step, pl.ds(0, 16), pl.ds(lane, 128)]
            pltpu.make_async_copy(source, held.at[4 * flip + step], sem).start()
    pltpu.make_async_copy(held, held, sem).wait()
    source = lax.broadcasted_iota(jnp.int32, (128, vec_ref.shape[1]), 0)
    target = lax.broadcasted_iota(jnp.int32, (128, vec_ref.shape[1]), 1)
    rows = jnp.zeros((16, vec_ref.shape[1]), WIDE)
    count = shift_ref.shape[1] // (8 * 128)
    for order in range(8):
        owner = place_ref[0] ^ (2 * (order % 4) + order // 4)
        move = (target == source + owner * owned) & (source < owned)
        rows = rows + dot(held[order], move.astype(WIDE).astype(LOW))
        for row in range(count):
            start = pl.multiple_of((owner * count + row) * 128, 128)
            shift_ref[0:1, pl.ds(start, 128)] = held[order, 8 + row : 9 + row, :].astype(WIDE)
    vec_ref[...] = rows[0:8]


def attention_kernel(place_ref, stream_ref, ids_column_ref, ids_row_ref, *refs):
    pieces = refs[:6]
    vec_ref, shift_ref, a1_t_ref, mix_ref, mix_t_ref, qkv_out, prob_out = refs[6:13]
    weight, qkv_ref, prob, bias, v_t, weight_sem, vec_held, vec_sem, out_sem = refs[13:]
    width = mix_ref.shape[1]
    pairs = width // 128
    loading = load_weight(place_ref, pieces, 0, weight.shape[1] // 2, weight, weight_sem)
    gather_vectors(place_ref, *pieces[:2], vec_held, vec_sem, vec_ref, shift_ref)
    normed, _ = normalize(stream_ref[...].astype(WIDE))
    a1 = (normed * vec_ref[0:1, :] + vec_ref[1:2, :]).astype(LOW)
    a1_t_ref[...] = a1.T
    bias[...] = jnp.where(ids_column_ref[...] == ids_row_ref[...], 0.0, MASKED)
    loading.wait()
    queries = dot(a1, weight[:, :width]) + vec_ref[2:3, :]
    qkv_ref[:, :width] = queries.astype(LOW)
    qkv_ref[:, width : 2 * width] = dot(a1, weight[:, width : 2 * width]).astype(LOW)
    values = (dot(a1, weight[:, 2 * width :]) + vec_ref[3:4, :]).astype(LOW)
    qkv_ref[:, 2 * width :] = values
    qkv_copy = pltpu.make_async_copy(qkv_ref, qkv_out, out_sem.at[pairs])
    qkv_copy.start()
    v_t[...] = values.T

    def out_copy(pair):
        heads = pl.ds(2 * pair, 2)
        return pltpu.make_async_copy(prob.at[heads], prob_out.at[heads], out_sem.at[pair])

    left = lax.broadcasted_iota(jnp.int32, (ROW, 128), 1) < HEAD_DIM

    @pl.loop(0, pairs, unroll=2)
    def _(pair):
        lane = pl.multiple_of(pair * 128, 128)
        scaled = qkv_ref[:, pl.ds(lane, 128)] * HEAD_DIM**-0.5
        keys = qkv_ref[:, pl.ds(width + lane, 128)]
        blank = jnp.zeros_like(keys)
        halves = jnp.concatenate([jnp.where(left, keys, blank), jnp.where(left, blank, keys)])
        scores = dot_t(halves, scaled)
        for half in range(2):
            v_rows = pl.ds(pl.multiple_of(lane + half * HEAD_DIM, HEAD_DIM), HEAD_DIM)
            head = scores[half * ROW : (half + 1) * ROW] + bias[...]
            weights = jnp.exp(head - jnp.max(head, axis=0, keepdims=True))
            weights = weights * (1.0 / jnp.sum(weights, axis=0, keepdims=True))
            low = weights.astype(LOW)
            prob[2 * pair + half] = low
            mix_t_ref[v_rows, :] = dot(v_t[v_rows, :], low).astype(LOW)
        out_copy(pair).start()

    mix_ref[...] = mix_t_ref[...].T
    qkv_copy.wait()

    @pl.loop(0, pairs)
    def _(pair):
        out_copy(pair).wait()


def attention(place, stream, ids, hidden, pieces):
    width = stream.shape[1]
    return pl.pallas_call(
        attention_kernel,
        out_shape=[
            shape((8, width), WIDE),
            shape((1, hidden), WIDE),
            shape((width, ROW)),
            shape((ROW, width)),
            shape((width, ROW)),
            pltpu.HBM((ROW, 3 * width), LOW),
            pltpu.HBM((HEADS, ROW, ROW), LOW),
        ],
        in_specs=[in_smem()] + [in_vmem()] * 3 + [in_hbm()] * 6,
        out_specs=[in_vmem()] * 5 + [in_hbm()] * 2,
        scratch_shapes=[
            pltpu.VMEM((width, 3 * width), LOW),
            pltpu.VMEM((ROW, 3 * width), LOW),
            pltpu.VMEM((HEADS, ROW, ROW), LOW),
            pltpu.VMEM((ROW, ROW), WIDE),
            pltpu.VMEM((width, ROW), LOW),
            pltpu.SemaphoreType.DMA,
            pltpu.VMEM((8, 16, 128), LOW),
            pltpu.SemaphoreType.DMA,
            pltpu.SemaphoreType.DMA((HEADS // 2 + 1,)),
        ],
        compiler_params=kernel_params(22),
        cost_estimate=cost(12e9, 24e6),
    )(place, stream, ids.reshape(ROW, 1), ids.reshape(1, ROW), *hbm(pieces))


def hidden_kernel(place_ref, tokens_ref, mix_ref, valid_ref, vec_ref, bias_ref, *refs):
    pieces = refs[:6]
    mid_ref, a2_t_ref, act_ref, act_t_ref, slope_ref, sums_ref, w_out, w_fc1 = refs[6:14]
    out_sem, fc1_sem = refs[14:]
    width = tokens_ref.shape[1]
    hidden = bias_ref.shape[1]
    out_ready = load_weight(place_ref, pieces, 0, width // 2, w_out, out_sem)
    fc1_ready = load_weight(place_ref, pieces, width // 2, hidden // 2, w_fc1, fc1_sem)
    stream = tokens_ref[...].astype(WIDE)
    valid = valid_ref[...]
    out_ready.wait()
    branch = dot(mix_ref[...], w_out[...]) + vec_ref[4:5, :]
    middle = stream + branch
    mid_ref[...] = middle
    sums_ref[0:1, :] = column_sum(valid * stream * stream)
    sums_ref[1:2, :] = column_sum(valid * branch * branch)
    sums_ref[2:3, :] = column_sum(valid * middle * middle)
    sums_ref[3:8, :] = jnp.zeros((5, width), WIDE)
    normed, _ = normalize(middle)
    a2 = (normed * vec_ref[5:6, :] + vec_ref[6:7, :]).astype(LOW)
    a2_t_ref[...] = a2.T
    fc1_ready.wait()
    step = 512
    for first in range(0, hidden, step):
        lanes = slice(first, first + step)
        pre = dot(a2, w_fc1[:, lanes]) + bias_ref[:, lanes]
        square = pre * pre
        turn = jnp.tanh(GELU_SCALE * (pre + GELU_CUBE * (square * pre)))
        half = 0.5 * (1.0 + turn)
        act = (pre * half).astype(LOW)
        act_ref[:, lanes] = act
        act_t_ref[lanes, :] = act.T
        bend = (1.0 - turn * turn) * (GELU_SCALE + 3.0 * GELU_SCALE * GELU_CUBE * square)
        slope_ref[:, lanes] = (half + 0.5 * pre * bend).astype(LOW)


def hidden_layer(place, tokens, mix, valid, vec, bias, pieces):
    width, hidden = tokens.shape[1], bias.shape[1]
    return pl.pallas_call(
        hidden_kernel,
        out_shape=[
            shape((ROW, width), WIDE),
            shape((width, ROW)),
            shape((ROW, hidden)),
            shape((hidden, ROW)),
            shape((ROW, hidden)),
            shape((8, width), WIDE),
            shape((width, width)),
            shape((width, hidden)),
        ],
        in_specs=[in_smem()] + [in_vmem()] * 5 + [in_hbm()] * 6,
        out_specs=[in_vmem()] * 8,
        scratch_shapes=[
            pltpu.SemaphoreType.DMA,
            pltpu.SemaphoreType.DMA,
        ],
        compiler_params=kernel_params(22),
        cost_estimate=cost(10e9, 20e6),
    )(place, tokens, mix, valid, vec, bias, *hbm(pieces))


def hidden_back_kernel(place_ref, cot_ref, slope_ref, *refs):
    pieces = refs[:6]
    d_pre_ref, shift_ref, w_fc2, sem = refs[6:]
    hidden = slope_ref.shape[1]
    loading = load_weight(place_ref, pieces, 0, w_fc2.shape[1] // 2, w_fc2, sem)
    cot = cot_ref[...]
    loading.wait()
    step = 512
    for first in range(0, hidden, step):
        lanes = slice(first, first + step)
        d_pre = dot_t(cot, w_fc2[lanes, :]) * slope_ref[:, lanes].astype(WIDE)
        shift_ref[:, lanes] = column_sum(d_pre)
        d_pre_ref[:, lanes] = d_pre.astype(LOW)


def hidden_back(place, cot, slope, pieces):
    width, hidden = cot.shape[1], slope.shape[1]
    return pl.pallas_call(
        hidden_back_kernel,
        out_shape=[shape((ROW, hidden)), shape((1, hidden), WIDE), shape((hidden, width))],
        in_specs=[in_smem()] + [in_vmem()] * 2 + [in_hbm()] * 6,
        out_specs=[in_vmem()] * 3,
        scratch_shapes=[pltpu.SemaphoreType.DMA],
        compiler_params=kernel_params(18),
        cost_estimate=cost(3e9, 14e6),
    )(place, cot, slope, *hbm(pieces))


def middle_kernel(mid_ref, act_ref, d_pre_ref, cot_ref, valid_ref, vec_ref, *refs):
    w_out, w_fc1, w_fc2 = refs[:3]
    layer_ref, d_mid_ref, d_mid_low_ref, d_mix_ref, sums_ref = refs[3:]
    middle = mid_ref[...]
    valid = valid_ref[...]
    mlp = dot(act_ref[...], w_fc2[...]) + vec_ref[7:8, :]
    result = middle + mlp
    layer_ref[...] = result.astype(LOW)
    sums_ref[4:5, :] = column_sum(valid * mlp * mlp)
    sums_ref[5:6, :] = column_sum(valid * result * result)
    sums_ref[6:8, :] = jnp.zeros((2, mid_ref.shape[1]), WIDE)
    d_a2 = dot_t(d_pre_ref[...], w_fc1[...])
    normed, scale = normalize(middle)
    dy = cot_ref[...].astype(WIDE)
    d_mid = dy + normalize_back(d_a2 * vec_ref[5:6, :], normed, scale)
    d_mid_ref[...] = d_mid
    low = d_mid.astype(LOW)
    d_mid_low_ref[...] = low
    sums_ref[0:1, :] = column_sum(d_mid)
    sums_ref[1:2, :] = column_sum(d_a2 * normed)
    sums_ref[2:3, :] = column_sum(d_a2)
    sums_ref[3:4, :] = column_sum(dy)
    d_mix_ref[...] = dot_t(low, w_out[...]).astype(LOW)


def middle_layer(mid, act, d_pre, cot, valid, vec, w_out, w_fc1, w_fc2):
    width = mid.shape[1]
    return pl.pallas_call(
        middle_kernel,
        out_shape=[
            shape((ROW, width)),
            shape((ROW, width), WIDE),
            shape((ROW, width)),
            shape((ROW, width)),
            shape((8, width), WIDE),
        ],
        in_specs=[in_vmem()] * 9,
        out_specs=[in_vmem()] * 5,
        compiler_params=kernel_params(20),
        cost_estimate=cost(14e9, 30e6),
    )(mid, act, d_pre, cot, valid, vec, w_out, w_fc1, w_fc2)


def attention_back_kernel(qkv_ref, mix_t_ref, d_mix_ref, prob_in, d_proj_ref, sums_ref, *rest):
    k_t, d_mix_t, d_q_t, prob, sem = rest
    width = mix_t_ref.shape[0]
    pairs = width // 128

    def in_copy(pair):
        heads = pl.ds(2 * pair, 2)
        return pltpu.make_async_copy(prob_in.at[heads], prob.at[heads], sem.at[pair])

    @pl.loop(0, pairs)
    def _(pair):
        in_copy(pair).start()


    k_t[...] = qkv_ref[:, width : 2 * width].T
    d_mix_t[...] = d_mix_ref[...].T
    left = lax.broadcasted_iota(jnp.int32, (ROW, 128), 1) < HEAD_DIM

    @pl.loop(0, pairs, unroll=2)
    def _(pair):
        lane = pl.multiple_of(pair * 128, 128)
        queries = qkv_ref[:, pl.ds(lane, 128)]
        values = qkv_ref[:, pl.ds(2 * width + lane, 128)]
        d_mix = d_mix_ref[:, pl.ds(lane, 128)]
        in_copy(pair).wait()
        d_keys, d_values = [], []
        for half in range(2):
            rows = pl.ds(pl.multiple_of(lane + half * HEAD_DIM, HEAD_DIM), HEAD_DIM)
            inner = column_sum(mix_t_ref[rows, :].astype(WIDE) * d_mix_t[rows, :].astype(WIDE))
            value_half = jnp.where(left == (half == 0), values, jnp.zeros_like(values))
            low = prob[2 * pair + half]
            d_prob = dot_t(value_half, d_mix)
            d_score = (low.astype(WIDE) * (d_prob - inner)).astype(LOW)
            d_keys.append(dot(d_score, queries))
            d_values.append(dot(low, d_mix))
            d_q_t[rows, :] = dot(k_t[rows, :], d_score)
        d_k = jnp.where(left, d_keys[0], d_keys[1]) * HEAD_DIM**-0.5
        d_v = jnp.where(left, d_values[0], d_values[1])
        d_proj_ref[:, pl.ds(width + lane, 128)] = d_k.astype(LOW)
        d_proj_ref[:, pl.ds(2 * width + lane, 128)] = d_v.astype(LOW)
        sums_ref[1:2, pl.ds(lane, 128)] = column_sum(d_v)

    d_q = d_q_t[...].T * HEAD_DIM**-0.5
    d_proj_ref[:, :width] = d_q.astype(LOW)
    sums_ref[0:1, :] = column_sum(d_q)
    sums_ref[2:8, :] = jnp.zeros((6, width), WIDE)


def attention_back(qkv, mix_t, d_mix, prob):
    width = mix_t.shape[0]
    heads = prob.shape[0]
    return pl.pallas_call(
        attention_back_kernel,
        out_shape=[shape((ROW, 3 * width)), shape((8, width), WIDE)],
        in_specs=[in_vmem()] * 3 + [in_hbm()],
        out_specs=[in_vmem()] * 2,
        scratch_shapes=[
            pltpu.VMEM((width, ROW), LOW),
            pltpu.VMEM((width, ROW), LOW),
            pltpu.VMEM((width, ROW), WIDE),
            pltpu.VMEM((heads, ROW, ROW), LOW),
            pltpu.SemaphoreType.DMA((heads // 2,)),
        ],
        compiler_params=kernel_params(20),
        cost_estimate=cost(1.2e9 * heads, 2e6 * heads),
    )(qkv, mix_t, d_mix, *hbm([prob]))


def first_norm_kernel(place_ref, tokens_ref, d_proj_ref, d_mid_ref, vec_ref, *refs):
    valid_ref, in_ref, mid_ref, att_ref, shift_ref = refs[:5]
    pieces = refs[5:11]
    grad_ref, sums_ref, weight, sem = refs[11:]
    width = tokens_ref.shape[1]
    loading = load_weight(place_ref, pieces, 0, weight.shape[1] // 2, weight, sem)
    sums_ref[2:4, :] = att_ref[0:2, :]
    sums_ref[4:8, :] = mid_ref[0:4, :]
    sums_ref[8:11, :] = in_ref[0:3, :]
    sums_ref[11:13, :] = mid_ref[4:6, :]
    sums_ref[13:14, :] = jnp.sum(valid_ref[...]) * jnp.ones((1, width), WIDE)
    for row in range(shift_ref.shape[1] // width):
        sums_ref[14 + row : 15 + row, :] = shift_ref[:, row * width : (row + 1) * width]
    normed, scale = normalize(tokens_ref[...].astype(WIDE))
    loading.wait()
    d_a1 = dot_t(d_proj_ref[...], weight[...])
    d_in = normalize_back(d_a1 * vec_ref[0:1, :], normed, scale)
    grad_ref[...] = (d_mid_ref[...] + d_in).astype(LOW)
    sums_ref[0:1, :] = column_sum(d_a1 * normed)
    sums_ref[1:2, :] = column_sum(d_a1)


def first_norm_back(place, tokens, d_proj, d_mid, vec, valid, sums, pieces):
    width = tokens.shape[1]
    rows = 14 + sums[-1].shape[1] // width
    return pl.pallas_call(
        first_norm_kernel,
        out_shape=[shape((ROW, width)), shape((rows, width), WIDE)],
        in_specs=[in_smem()] + [in_vmem()] * 9 + [in_hbm()] * 6,
        out_specs=[in_vmem()] * 2,
        scratch_shapes=[pltpu.VMEM((width, d_proj.shape[1]), LOW), pltpu.SemaphoreType.DMA],
        compiler_params=kernel_params(16),
        cost_estimate=pl.CostEstimate(flops=4_000_000_000, bytes_accessed=1, transcendentals=0),
    )(place, tokens, d_proj, d_mid, vec, valid, *sums, *hbm(pieces))


def product_half(left_refs, right_ref, which, sums, first):
    half = right_ref.shape[1] // 2
    row = 0
    for left_ref in left_refs:
        count = left_ref.shape[0]
        for start in range(0, half, 384):
            lane = pl.multiple_of(which * half + start, 128)
            sums[row : row + count, first + start : first + start + 384] = dot(
                left_ref[...], right_ref[:, pl.ds(lane, 384)]
            )
        row += count


def products(groups, refs, which, sums):
    first = 0
    for count in groups:
        product_half(refs[:count], refs[count], which, sums, first)
        first += refs[count].shape[1] // 2
        refs = refs[count + 1 :]


def give_kernel(groups, place_ref, *refs):
    out_ref, sums = refs[-2:]
    shard, core = place_ref[0], place_ref[1]
    products(groups, refs[:-2], 1 - core, sums)
    rows = out_ref.shape[2]
    for order in range(8):
        owner = shard ^ (2 * (order % 4) + order // 4)
        for part in range(3):
            start = pl.multiple_of((owner * 3 + part) * rows, rows)
            out_ref[order, part] = sums[pl.ds(start, rows), :].astype(LOW)


def keep_kernel(groups, place_ref, received_ref, *refs):
    give_ref, keep_ref, sums = refs[-3:]
    shard, core, plane = place_ref[0], place_ref[1], place_ref[2]
    products(groups, refs[:-3], core, sums)
    rows = give_ref.shape[1]
    for order in range(8):
        owner = shard ^ (2 * (order % 4) + order // 4)

        def total(part):
            start = pl.multiple_of((owner * 3 + part) * rows, rows)
            mine = sums[pl.ds(start, rows), :]
            return (mine + received_ref[order, part].astype(WIDE)).astype(LOW)

        give_ref[order] = total(1 - plane)
        keep_ref[0, order] = total(plane)
        keep_ref[1, order] = total(2)


class Reduction:
    def __init__(self, place, groups):
        self.place = place
        self.counts = tuple(len(group) - 1 for group in groups)
        self.operands = [entry for group in groups for entry in group]
        self.height = sum(entry.shape[0] for entry in groups[0][:-1])
        self.half = sum(group[-1].shape[1] for group in groups) // 2
        self.rows = self.height // 24
        self.scratch = [pltpu.VMEM((self.height, self.half), WIDE)]
        self.cost = cost(2 * self.height * self.half * ROW, 4 * self.height * self.half)

    def give(self):
        return pl.pallas_call(
            partial(give_kernel, self.counts),
            out_shape=shape((8, 3, self.rows, self.half)),
            in_specs=[in_smem()] + [in_vmem()] * len(self.operands),
            out_specs=in_vmem(),
            scratch_shapes=self.scratch,
            compiler_params=kernel_params(10),
            cost_estimate=self.cost,
        )(self.place, *self.operands)

    def keep(self, received):
        return pl.pallas_call(
            partial(keep_kernel, self.counts),
            out_shape=[shape((8, self.rows, self.half)), shape((2, 8, self.rows, self.half))],
            in_specs=[in_smem()] + [in_vmem()] * (1 + len(self.operands)),
            out_specs=[in_vmem()] * 2,
            scratch_shapes=self.scratch,
            compiler_params=kernel_params(12),
            cost_estimate=self.cost,
        )(self.place, received, *self.operands)

    def after_y(self, kept, side):
        sent = jnp.stack([plus(kept[0, 4:], side[4:]), kept[1, 4:]])
        return sent, (kept[0, :4], side[:4], kept[1, :4])

    def after_x(self, stay, column):
        kept, side, shared = stay
        return [
            jnp.stack([plus(kept[step], side[step], column[0, step]), plus(shared[step], column[1, step])])
            for step in range(4)
        ]

    def over_z(self, columns, name):
        return [swap(columns[step], "shard", 2 * step, name) for step in (1, 2, 3)]

    def after_z(self, mine, pieces):
        piece = plus(mine, *pieces)
        for bit in range(2, lax.axis_size("dp").bit_length() - 1):
            piece = plus(piece, swap(piece, "dp", 2**bit))
        return piece

    def after_y2(self, piece, other):
        shared = plus(piece[1], other[1])
        even = self.place[2] == 0
        first = jnp.where(even, piece[0], other[0])
        second = jnp.where(even, other[0], piece[0])
        return jnp.stack([first, second, shared])

    def halves(self, mine, theirs):
        low_core = self.place[1] == 0
        low, high = jnp.where(low_core, mine, theirs), jnp.where(low_core, theirs, mine)
        return low.reshape(3 * self.rows, self.half), high.reshape(3 * self.rows, self.half)


def plus(*entries):
    return sum(entry.astype(WIDE) for entry in entries).astype(LOW)


def step_of(master, grad, first, second, clip, decay):
    correction = 1.0 / (1.0 - ADAM_BETA**STEP)
    clipped = grad * clip
    first = ADAM_BETA * first + (1.0 - ADAM_BETA) * clipped
    second = ADAM_BETA * second + (1.0 - ADAM_BETA) * clipped * clipped
    change = first * correction / (jnp.sqrt(second * correction) + ADAM_EPS)
    return LEARN_RATE * (change + decay * master)


def body(
    tokens,
    picture_ids,
    cotangent,
    w_qkv,
    w_out,
    w_fc1,
    w_fc2,
    vectors,
    fc1_bias,
    moments_qkv,
    moments_out,
    moments_fc1,
    moments_fc2,
    moments_vectors,
    moments_fc1_bias,
):
    model_width = tokens.shape[1]
    masters = (w_qkv, w_out, w_fc1, w_fc2, vectors, fc1_bias)
    moments = (
        moments_qkv,
        moments_out,
        moments_fc1,
        moments_fc2,
        moments_vectors,
        moments_fc1_bias,
    )
    shard = lax.axis_index("shard")
    data = lax.axis_index("dp")
    place = jnp.stack([shard, data % 2, (data // 2) % 2]).astype(jnp.int32)
    model_owned = vectors.shape[1]
    hidden_owned = fc1_bias.shape[0]
    valid = (picture_ids != 0).astype(WIDE)[:, None]
    own_a, own_b, own_c = own_pieces(place, w_qkv, w_out, w_fc1, w_fc2, vectors, fc1_bias)
    near_a = jnp.stack(gather_z(own_a, "A"))
    near_a, own_b, own_c = sync(near_a, own_b, own_c)
    far_a, near2_a = gather_x(near_a, "A"), gather_core(near_a, "A")
    near_b = jnp.stack(gather_z(own_b, "B"))
    far_a, near_b, near2_a, own_c = sync(far_a, near_b, near2_a, own_c)
    side_a = gather_y(near_a, far_a, "A", lanes=w_qkv.shape[1] // 2)
    far_b, near2_b = gather_x(near_b, "B"), gather_core(near_b, "B")
    far2_a = gather_core(far_a, "A")
    z_c = gather_z(own_c, "C")
    side2_a = gather_core(side_a, "A")
    far_b, near2_b, z_c = sync(far_b, near2_b, z_c)
    near_c = jnp.stack(z_c)
    pieces_a = (near_a, far_a, side_a, near2_a, far2_a, side2_a)
    side_b, far2_b = gather_y(near_b, far_b, "B", w_out.shape[0] // 3), gather_core(far_b, "B")
    far_c, near2_c = gather_x(near_c, "C"), gather_core(near_c, "C")
    vec, bias, a1_t, mix, mix_t, qkv, prob = attention(
        place, after(tokens, side2_a, near_c), picture_ids, w_fc1.shape[1], pieces_a
    )
    side_b, far2_b, far_c, near2_c, mix = sync(side_b, far2_b, far_c, near2_c, mix)
    side2_b = gather_core(side_b, "B")
    side_c, far2_c = gather_y(near_c, far_c, "C", w_fc2.shape[0] // 3), gather_core(far_c, "C")
    pieces_b = (near_b, far_b, side_b, near2_b, far2_b, side2_b)
    mid, a2_t, act, act_t, slope, sums_in, wide_out, wide_fc1 = hidden_layer(
        place, tokens, mix, valid, vec, bias, pieces_b
    )
    fc2 = Reduction(place, [(act_t, cotangent)])
    given = fc2.give()
    side_c, far2_c, given = sync(side_c, far2_c, given)
    recv_f2, side2_c = gather_core(given, "F2"), gather_core(side_c, "C")
    pieces_c = (near_c, far_c, side_c, near2_c, far2_c, side2_c)
    give_f2, keep_f2 = fc2.keep(recv_f2)
    side_f2 = swap(give_f2, "dp", 2, "F2")
    d_pre, shift_sum, wide_fc2 = hidden_back(place, cotangent, after(slope, give_f2), pieces_c)
    layer_out, d_mid, d_mid_low, d_mix, sums_mid = middle_layer(
        mid, act, d_pre, cotangent, valid, vec, wide_out, wide_fc1, wide_fc2
    )
    fc1 = Reduction(place, [(a2_t, after(d_pre, d_mix))])
    given = fc1.give()
    side_f2, given, d_mix = sync(side_f2, given, d_mix)
    sent, stay_f2 = fc2.after_y(keep_f2, side_f2)
    column_f2 = swap(sent, "shard", 1, "F2")
    recv_f1 = gather_core(given, "F1")
    d_proj, sums_att = attention_back(qkv, mix_t, after(d_mix, sent), prob)
    recv_f1, d_proj = sync(recv_f1, d_proj)
    give_f1, keep_f1 = fc1.keep(recv_f1)
    first = Reduction(place, [(a1_t, after(d_proj, give_f1)), (mix_t, d_mid_low)])
    given = first.give()
    column_f2, given, give_f1 = sync(column_f2, given, give_f1)
    side_f1 = swap(give_f1, "dp", 2, "F1")
    recv_a = gather_core(given, "RA")
    tokens_grad, small_sums = first_norm_back(
        place,
        tokens,
        d_proj,
        after(d_mid, given),
        vec,
        valid,
        (sums_in, sums_mid, sums_att, shift_sum),
        pieces_a,
    )
    recv_a, small_sums = sync(recv_a, small_sums)
    give_a, keep_a = first.keep(recv_a)
    small_more = swap(small_sums, "dp", 1)
    side_f1, give_a, small_more = sync(side_f1, give_a, small_more)
    side_ra = swap(give_a, "dp", 2, "RA")
    columns = fc2.after_x(stay_f2, column_f2)
    sent, stay_f1 = fc1.after_y(keep_f1, after(side_f1, columns))
    column_f1 = swap(sent, "shard", 1, "F1")
    pieces_f2, mine_f2 = fc2.over_z(columns, "F2"), columns[0]
    side_ra, column_f1, pieces_f2 = sync(side_ra, column_f1, pieces_f2)
    sent, stay_a = first.after_y(keep_a, side_ra)
    column_a = swap(sent, "shard", 1, "RA")
    columns = fc1.after_x(stay_f1, after(column_f1, sent))
    pieces_f1, mine_f1 = fc1.over_z(columns, "F1"), columns[0]
    piece_f2 = fc2.after_z(mine_f2, after(pieces_f2, columns))
    other_f2 = swap(piece_f2, "dp", 2, "F2")
    small_sums = small_sums + small_more
    small_more = swap(small_sums, "dp", 2)
    column_a, pieces_f1, other_f2, small_more = sync(column_a, pieces_f1, other_f2, small_more)
    columns = first.after_x(stay_a, column_a)
    pieces_ra, mine_a = first.over_z(columns, "RA"), columns[0]
    piece_f1 = fc1.after_z(mine_f1, after(pieces_f1, columns))
    other_f1 = swap(piece_f1, "dp", 2, "F1")
    owned_f2 = fc2.after_y2(piece_f2, after(other_f2, columns))
    theirs_f2 = gather_core(owned_f2, "F2")
    small_sums = small_sums + small_more
    small_more = swap(small_sums, "shard", 1)
    pieces_ra, other_f1, theirs_f2, small_more = sync(pieces_ra, other_f1, theirs_f2, small_more)
    piece_a = first.after_z(mine_a, pieces_ra)
    other_a = swap(piece_a, "dp", 2, "RA")
    owned_f1 = fc1.after_y2(piece_f1, after(other_f1, piece_a))
    theirs_f1 = gather_core(owned_f1, "F1")
    small_sums = small_sums + small_more
    small_more = swap(small_sums, "shard", 2)
    square_sum = sum(jnp.sum(jnp.square(entry.astype(WIDE))) for entry in (owned_f2, owned_f1))
    other_a, theirs_f1, small_more, square_sum = sync(other_a, theirs_f1, small_more, square_sum)
    owned_a = first.after_y2(piece_a, other_a)
    theirs_a = gather_core(owned_a, "RA")
    square_sum = square_sum + jnp.sum(jnp.square(owned_a.astype(WIDE)))
    square_more = swap(square_sum, "dp", 1)
    small_sums = small_sums + small_more
    small_more = swap(small_sums, "shard", 4)
    theirs_a, square_more, small_more = sync(theirs_a, square_more, small_more)
    square_sum = square_sum + square_more
    for mask in (1, 2, 4):
        square_sum = square_sum + swap(square_sum, "shard", mask)
    small_sums = small_sums + small_more
    for bit in range(2, lax.axis_size("dp").bit_length() - 1):
        small_sums = small_sums + swap(small_sums, "dp", 2**bit)
    fc2_halves, fc1_halves = fc2.halves(owned_f2, theirs_f2), fc1.halves(owned_f1, theirs_f1)
    first_halves = first.halves(owned_a, theirs_a)
    split = w_qkv.shape[1] // 2
    owner_grads = [
        jnp.concatenate([half[:, :split] for half in first_halves], axis=1).astype(WIDE),
        jnp.concatenate([half[:, split:] for half in first_halves], axis=1).astype(WIDE),
        jnp.concatenate(fc1_halves, axis=1).astype(WIDE),
        jnp.concatenate(fc2_halves, axis=1).astype(WIDE),
    ]
    grad_vectors, grad_shift = small_sums[:8], small_sums[14:].reshape(-1)
    stream_sums = jnp.sum(small_sums[8:13], axis=1)
    square_sum = square_sum + jnp.sum(small_sums[:8] * small_sums[:8])
    square_sum = square_sum + jnp.sum(small_sums[14:] * small_sums[14:])
    owner_grads = (
        *owner_grads,
        lax.dynamic_slice_in_dim(grad_vectors, shard * model_owned, model_owned, 1),
        lax.dynamic_slice_in_dim(grad_shift, shard * hidden_owned, hidden_owned, 0),
    )
    stream_rms = jnp.sqrt(stream_sums / (small_sums[13, 0] * model_width))
    clip_factor = CLIP_NORM / jnp.maximum(jnp.sqrt(square_sum), CLIP_NORM)
    steps = [
        step_of(
            masters[k],
            owner_grads[k],
            moments[k][0],
            moments[k][1],
            clip_factor,
            WEIGHT_DECAY if k < 4 else 0.0,
        )
        for k in range(6)
    ]
    updated = [steps[k] if k == 4 else masters[k] - steps[k] for k in range(6)]
    return (layer_out, tokens_grad, *owner_grads, *updated, stream_rms)


def solution(mesh):
    placed = (
        P(("dp", "shard"), None),
        P(("dp", "shard")),
        P(("dp", "shard"), None),
        P("shard", None),
        P("shard", None),
        P("shard", None),
        P("shard", None),
        P(None, "shard"),
        P("shard"),
        P(None, "shard", None),
        P(None, "shard", None),
        P(None, "shard", None),
        P(None, "shard", None),
        P(None, None, "shard"),
        P(None, "shard"),
    )
    return jax.shard_map(
        body,
        mesh=mesh,
        in_specs=placed,
        out_specs=(
            P(("dp", "shard"), None),
            P(("dp", "shard"), None),
            P("shard", None),
            P("shard", None),
            P("shard", None),
            P("shard", None),
            P(None, "shard"),
            P("shard"),
            P("shard", None),
            P("shard", None),
            P("shard", None),
            P("shard", None),
            P(None, "shard"),
            P("shard"),
            P(),
        ),
        check_vma=False,
    )
```

```python
from functools import partial

import jax
import jax.numpy as jnp
from jax import lax
from jax.experimental import pallas as pl
from jax.experimental.pallas import tpu as pltpu
from jax.sharding import PartitionSpec as P

HEADS = 12
HEAD_DIM = 64
ROW = 512
STEP = 2

NORM_EPS = 1e-06
ADAM_BETA = 0.5
LEARN_RATE = 0.03
WEIGHT_DECAY = 0.1
ADAM_EPS = 1e-08
CLIP_NORM = 1.0
MASKED = -1e30
GELU_SCALE = 0.7978845608028654
GELU_CUBE = 0.044715

LOW = jnp.bfloat16
WIDE = jnp.float32


def swap(entry, axis, mask, name="sums"):
    count = lax.axis_size(axis)
    with jax.named_scope(name + "_" + axis + str(mask)):
        return lax.ppermute(entry, axis, [(place, place ^ mask) for place in range(count)])


def in_vmem():
    return pl.BlockSpec(memory_space=pltpu.VMEM)


def in_hbm():
    return pl.BlockSpec(memory_space=pltpu.HBM)


def hbm(entries):
    return [pltpu.with_memory_space_constraint(entry, pltpu.HBM) for entry in entries]


def in_smem():
    return pl.BlockSpec(memory_space=pltpu.SMEM)


def shape(dims, kind=LOW):
    return jax.ShapeDtypeStruct(dims, kind)


def cost(flops, moved):
    return pl.CostEstimate(flops=1, bytes_accessed=1, transcendentals=0)


def kernel_params(mib):
    return pltpu.CompilerParams(vmem_limit_bytes=mib * 2**20)


def dot(left, right):
    return jnp.dot(left, right, preferred_element_type=WIDE)


def dot_t(left, right):
    return lax.dot_general(left, right, (((1,), (1,)), ((), ())), preferred_element_type=WIDE)


def normalize(entries):
    center = entries - jnp.mean(entries, axis=-1, keepdims=True)
    scale = lax.rsqrt(jnp.mean(center * center, axis=-1, keepdims=True) + NORM_EPS)
    return center * scale, scale


def normalize_back(grad, normed, scale):
    inner = jnp.mean(grad * normed, axis=-1, keepdims=True)
    return scale * (grad - jnp.mean(grad, axis=-1, keepdims=True) - normed * inner)


def column_sum(entries):
    return jnp.sum(entries, axis=0, keepdims=True)


def own_pieces_kernel(place_ref, *refs):
    sources, vectors_ref, shift_ref = refs[:4], refs[4], refs[5]
    qkv_ref, mid_ref, fc2_ref = refs[6:9]
    scratch, sem = refs[9:13], refs[13]
    core, plane = place_ref[1], place_ref[2]
    copies = []
    for number, (source, held) in enumerate(zip(sources, scratch)):
        rows, lanes = held.shape
        column = pl.multiple_of(core * lanes, 128)
        size = rows if number == 0 else rows // 2
        starts = (plane * size,) if number == 0 else (plane * size, 2 * size)
        for slot, start in enumerate(starts):
            start = pl.multiple_of(start, size)
            copies.append(
                pltpu.make_async_copy(
                    source.at[pl.ds(start, size), pl.ds(column, lanes)],
                    held.at[pl.ds(slot * size, size)],
                    sem.at[len(copies)],
                )
            )
    for copy in copies:
        copy.start()
    qkv, out, fc1, fc2 = scratch
    width = qkv.shape[1]
    qkv_ref[:, width:] = jnp.zeros((qkv.shape[0], 128), LOW)
    qkv_ref[0:8, width : width + vectors_ref.shape[1]] = vectors_ref[...].astype(LOW)
    qkv_ref[8 : 8 + shift_ref.shape[0], width:] = shift_ref[...].astype(LOW)
    for copy in copies:
        copy.wait()
    qkv_ref[:, :width] = qkv[...].astype(LOW)
    width = out.shape[1]
    mid_ref[:, :width] = out[...].astype(LOW)
    mid_ref[:, width:] = fc1[...].astype(LOW)
    fc2_ref[...] = fc2[...].astype(LOW)


def own_pieces(place, w_qkv, w_out, w_fc1, w_fc2, vectors, fc1_bias):
    weights = (w_qkv, w_out, w_fc1, w_fc2)
    dims = [
        (entry.shape[0] * share // 6, entry.shape[1] // 2)
        for share, entry in zip((3, 4, 4, 4), weights)
    ]
    return pl.pallas_call(
        own_pieces_kernel,
        out_shape=[
            shape((dims[0][0], dims[0][1] + 128)),
            shape((dims[1][0], dims[1][1] + dims[2][1])),
            shape(dims[3]),
        ],
        in_specs=[in_smem()] + [in_hbm()] * 4 + [in_vmem()] * 2,
        out_specs=[in_vmem()] * 3,
        scratch_shapes=[pltpu.VMEM(entry, WIDE) for entry in dims] + [pltpu.SemaphoreType.DMA((7,))],
        compiler_params=kernel_params(8),
    )(place, *hbm(weights), vectors, fc1_bias.reshape(-1, 128))


def after(entry, *others):
    return sync(entry, *others)[0]


def sync(*entries):
    leaves, tree = jax.tree.flatten(entries)
    return jax.tree.unflatten(tree, lax.optimization_barrier(leaves))


def gather_z(own, name):
    return [own] + [swap(own, "shard", mask, name) for mask in (2, 4, 6)]


def gather_x(near, name):
    return swap(near, "shard", 1, name)


def gather_y(near, far, name, rows=None, lanes=None):
    return swap(jnp.concatenate([near[:, :rows, :lanes], far[:, :rows, :lanes]]), "dp", 2, name)


def gather_core(entry, name):
    return swap(entry, "dp", 1, name)


def load_weight(place_ref, pieces, first, width, full, sem):
    shard, core, plane = place_ref[0], place_ref[1], place_ref[2]
    lanes = pl.ds(first, width)
    count = len(pieces) // 2
    owned = full.shape[0] // 8
    rows = pieces[2].shape[1] if count == 3 else owned
    shared = pieces[0].shape[1] - rows

    def put(source, owner, start, which):
        row = pl.multiple_of(owner * owned + start, 16)
        column = pl.multiple_of(which * width, 128)
        target = full.at[pl.ds(row, source.shape[0]), pl.ds(column, width)]
        pltpu.make_async_copy(source, target, sem).start()

    for which, half in ((core, pieces[:count]), (1 - core, pieces[count:])):
        for flip in range(2):
            for step in range(4):
                owner = shard ^ (2 * step + flip)
                ref = half[flip].at[step]
                put(ref.at[pl.ds(0, rows), lanes], owner, plane * rows if count == 3 else 0, which)
                if shared:
                    put(ref.at[pl.ds(rows, shared), lanes], owner, 2 * rows, which)
                if count == 3:
                    side = half[2].at[4 * flip + step, :, lanes]
                    put(side, owner, (1 - plane) * rows, which)
    return pltpu.make_async_copy(full, full, sem)


def gather_vectors(place_ref, near, far, held, sem, vec_ref, shift_ref):
    lane = near.shape[2] - 128
    owned = vec_ref.shape[1] // 8
    for flip, ref in ((0, near), (1, far)):
        for step in range(4):
            source = ref.at[step, pl.ds(0, 16), pl.ds(lane, 128)]
            pltpu.make_async_copy(source, held.at[4 * flip + step], sem).start()
    pltpu.make_async_copy(held, held, sem).wait()
    source = lax.broadcasted_iota(jnp.int32, (128, vec_ref.shape[1]), 0)
    target = lax.broadcasted_iota(jnp.int32, (128, vec_ref.shape[1]), 1)
    rows = jnp.zeros((16, vec_ref.shape[1]), WIDE)
    count = shift_ref.shape[1] // (8 * 128)
    for order in range(8):
        owner = place_ref[0] ^ (2 * (order % 4) + order // 4)
        move = (target == source + owner * owned) & (source < owned)
        rows = rows + dot(held[order], move.astype(WIDE).astype(LOW))
        for row in range(count):
            start = pl.multiple_of((owner * count + row) * 128, 128)
            shift_ref[0:1, pl.ds(start, 128)] = held[order, 8 + row : 9 + row, :].astype(WIDE)
    vec_ref[...] = rows[0:8]


def attention_kernel(place_ref, stream_ref, ids_column_ref, ids_row_ref, *refs):
    pieces = refs[:6]
    vec_ref, shift_ref, a1_t_ref, mix_ref, mix_t_ref, qkv_out, prob_out = refs[6:13]
    weight, qkv_ref, prob, bias, v_t, weight_sem, vec_held, vec_sem, out_sem = refs[13:]
    width = mix_ref.shape[1]
    pairs = width // 128
    loading = load_weight(place_ref, pieces, 0, weight.shape[1] // 2, weight, weight_sem)
    gather_vectors(place_ref, *pieces[:2], vec_held, vec_sem, vec_ref, shift_ref)
    normed, _ = normalize(stream_ref[...].astype(WIDE))
    a1 = (normed * vec_ref[0:1, :] + vec_ref[1:2, :]).astype(LOW)
    a1_t_ref[...] = a1.T
    bias[...] = jnp.where(ids_column_ref[...] == ids_row_ref[...], 0.0, MASKED)
    loading.wait()
    queries = dot(a1, weight[:, :width]) + vec_ref[2:3, :]
    qkv_ref[:, :width] = queries.astype(LOW)
    qkv_ref[:, width : 2 * width] = dot(a1, weight[:, width : 2 * width]).astype(LOW)
    values = (dot(a1, weight[:, 2 * width :]) + vec_ref[3:4, :]).astype(LOW)
    qkv_ref[:, 2 * width :] = values
    qkv_copy = pltpu.make_async_copy(qkv_ref, qkv_out, out_sem.at[pairs])
    qkv_copy.start()
    v_t[...] = values.T

    def out_copy(pair):
        heads = pl.ds(2 * pair, 2)
        return pltpu.make_async_copy(prob.at[heads], prob_out.at[heads], out_sem.at[pair])

    left = lax.broadcasted_iota(jnp.int32, (ROW, 128), 1) < HEAD_DIM

    @pl.loop(0, pairs, unroll=2)
    def _(pair):
        lane = pl.multiple_of(pair * 128, 128)
        scaled = qkv_ref[:, pl.ds(lane, 128)] * HEAD_DIM**-0.5
        keys = qkv_ref[:, pl.ds(width + lane, 128)]
        blank = jnp.zeros_like(keys)
        halves = jnp.concatenate([jnp.where(left, keys, blank), jnp.where(left, blank, keys)])
        scores = dot_t(halves, scaled)
        for half in range(2):
            v_rows = pl.ds(pl.multiple_of(lane + half * HEAD_DIM, HEAD_DIM), HEAD_DIM)
            head = scores[half * ROW : (half + 1) * ROW] + bias[...]
            weights = jnp.exp(head - jnp.max(head, axis=0, keepdims=True))
            weights = weights * (1.0 / jnp.sum(weights, axis=0, keepdims=True))
            low = weights.astype(LOW)
            prob[2 * pair + half] = low
            mix_t_ref[v_rows, :] = dot(v_t[v_rows, :], low).astype(LOW)
        out_copy(pair).start()

    mix_ref[...] = mix_t_ref[...].T
    qkv_copy.wait()

    @pl.loop(0, pairs)
    def _(pair):
        out_copy(pair).wait()


def attention(place, stream, ids, hidden, pieces):
    width = stream.shape[1]
    return pl.pallas_call(
        attention_kernel,
        out_shape=[
            shape((8, width), WIDE),
            shape((1, hidden), WIDE),
            shape((width, ROW)),
            shape((ROW, width)),
            shape((width, ROW)),
            pltpu.HBM((ROW, 3 * width), LOW),
            pltpu.HBM((HEADS, ROW, ROW), LOW),
        ],
        in_specs=[in_smem()] + [in_vmem()] * 3 + [in_hbm()] * 6,
        out_specs=[in_vmem()] * 5 + [in_hbm()] * 2,
        scratch_shapes=[
            pltpu.VMEM((width, 3 * width), LOW),
            pltpu.VMEM((ROW, 3 * width), LOW),
            pltpu.VMEM((HEADS, ROW, ROW), LOW),
            pltpu.VMEM((ROW, ROW), WIDE),
            pltpu.VMEM((width, ROW), LOW),
            pltpu.SemaphoreType.DMA,
            pltpu.VMEM((8, 16, 128), LOW),
            pltpu.SemaphoreType.DMA,
            pltpu.SemaphoreType.DMA((HEADS // 2 + 1,)),
        ],
        compiler_params=kernel_params(22),
        cost_estimate=cost(12e9, 24e6),
    )(place, stream, ids.reshape(ROW, 1), ids.reshape(1, ROW), *hbm(pieces))


def hidden_kernel(place_ref, tokens_ref, mix_ref, valid_ref, vec_ref, bias_ref, *refs):
    pieces = refs[:6]
    mid_ref, a2_t_ref, act_ref, act_t_ref, slope_ref, sums_ref, w_out, w_fc1 = refs[6:14]
    out_sem, fc1_sem = refs[14:]
    width = tokens_ref.shape[1]
    hidden = bias_ref.shape[1]
    out_ready = load_weight(place_ref, pieces, 0, width // 2, w_out, out_sem)
    fc1_ready = load_weight(place_ref, pieces, width // 2, hidden // 2, w_fc1, fc1_sem)
    stream = tokens_ref[...].astype(WIDE)
    valid = valid_ref[...]
    out_ready.wait()
    branch = dot(mix_ref[...], w_out[...]) + vec_ref[4:5, :]
    middle = stream + branch
    mid_ref[...] = middle
    sums_ref[0:1, :] = column_sum(valid * stream * stream)
    sums_ref[1:2, :] = column_sum(valid * branch * branch)
    sums_ref[2:3, :] = column_sum(valid * middle * middle)
    sums_ref[3:8, :] = jnp.zeros((5, width), WIDE)
    normed, _ = normalize(middle)
    a2 = (normed * vec_ref[5:6, :] + vec_ref[6:7, :]).astype(LOW)
    a2_t_ref[...] = a2.T
    fc1_ready.wait()
    step = 512
    for first in range(0, hidden, step):
        lanes = slice(first, first + step)
        pre = dot(a2, w_fc1[:, lanes]) + bias_ref[:, lanes]
        square = pre * pre
        turn = jnp.tanh(GELU_SCALE * (pre + GELU_CUBE * (square * pre)))
        half = 0.5 * (1.0 + turn)
        act = (pre * half).astype(LOW)
        act_ref[:, lanes] = act
        act_t_ref[lanes, :] = act.T
        bend = (1.0 - turn * turn) * (GELU_SCALE + 3.0 * GELU_SCALE * GELU_CUBE * square)
        slope_ref[:, lanes] = (half + 0.5 * pre * bend).astype(LOW)


def hidden_layer(place, tokens, mix, valid, vec, bias, pieces):
    width, hidden = tokens.shape[1], bias.shape[1]
    return pl.pallas_call(
        hidden_kernel,
        out_shape=[
            shape((ROW, width), WIDE),
            shape((width, ROW)),
            shape((ROW, hidden)),
            shape((hidden, ROW)),
            shape((ROW, hidden)),
            shape((8, width), WIDE),
            shape((width, width)),
            shape((width, hidden)),
        ],
        in_specs=[in_smem()] + [in_vmem()] * 5 + [in_hbm()] * 6,
        out_specs=[in_vmem()] * 8,
        scratch_shapes=[
            pltpu.SemaphoreType.DMA,
            pltpu.SemaphoreType.DMA,
        ],
        compiler_params=kernel_params(22),
        cost_estimate=cost(10e9, 20e6),
    )(place, tokens, mix, valid, vec, bias, *hbm(pieces))


def hidden_back_kernel(place_ref, cot_ref, slope_ref, *refs):
    pieces = refs[:6]
    d_pre_ref, shift_ref, w_fc2, sem = refs[6:]
    hidden = slope_ref.shape[1]
    loading = load_weight(place_ref, pieces, 0, w_fc2.shape[1] // 2, w_fc2, sem)
    cot = cot_ref[...]
    loading.wait()
    step = 512
    for first in range(0, hidden, step):
        lanes = slice(first, first + step)
        d_pre = dot_t(cot, w_fc2[lanes, :]) * slope_ref[:, lanes].astype(WIDE)
        shift_ref[:, lanes] = column_sum(d_pre)
        d_pre_ref[:, lanes] = d_pre.astype(LOW)


def hidden_back(place, cot, slope, pieces):
    width, hidden = cot.shape[1], slope.shape[1]
    return pl.pallas_call(
        hidden_back_kernel,
        out_shape=[shape((ROW, hidden)), shape((1, hidden), WIDE), shape((hidden, width))],
        in_specs=[in_smem()] + [in_vmem()] * 2 + [in_hbm()] * 6,
        out_specs=[in_vmem()] * 3,
        scratch_shapes=[pltpu.SemaphoreType.DMA],
        compiler_params=kernel_params(18),
        cost_estimate=cost(3e9, 14e6),
    )(place, cot, slope, *hbm(pieces))


def middle_kernel(mid_ref, act_ref, d_pre_ref, cot_ref, valid_ref, vec_ref, *refs):
    w_out, w_fc1, w_fc2 = refs[:3]
    layer_ref, d_mid_ref, d_mid_low_ref, d_mix_ref, sums_ref = refs[3:]
    middle = mid_ref[...]
    valid = valid_ref[...]
    mlp = dot(act_ref[...], w_fc2[...]) + vec_ref[7:8, :]
    result = middle + mlp
    layer_ref[...] = result.astype(LOW)
    sums_ref[4:5, :] = column_sum(valid * mlp * mlp)
    sums_ref[5:6, :] = column_sum(valid * result * result)
    sums_ref[6:8, :] = jnp.zeros((2, mid_ref.shape[1]), WIDE)
    d_a2 = dot_t(d_pre_ref[...], w_fc1[...])
    normed, scale = normalize(middle)
    dy = cot_ref[...].astype(WIDE)
    d_mid = dy + normalize_back(d_a2 * vec_ref[5:6, :], normed, scale)
    d_mid_ref[...] = d_mid
    low = d_mid.astype(LOW)
    d_mid_low_ref[...] = low
    sums_ref[0:1, :] = column_sum(d_mid)
    sums_ref[1:2, :] = column_sum(d_a2 * normed)
    sums_ref[2:3, :] = column_sum(d_a2)
    sums_ref[3:4, :] = column_sum(dy)
    d_mix_ref[...] = dot_t(low, w_out[...]).astype(LOW)


def middle_layer(mid, act, d_pre, cot, valid, vec, w_out, w_fc1, w_fc2):
    width = mid.shape[1]
    return pl.pallas_call(
        middle_kernel,
        out_shape=[
            shape((ROW, width)),
            shape((ROW, width), WIDE),
            shape((ROW, width)),
            shape((ROW, width)),
            shape((8, width), WIDE),
        ],
        in_specs=[in_vmem()] * 9,
        out_specs=[in_vmem()] * 5,
        compiler_params=kernel_params(20),
        cost_estimate=cost(14e9, 30e6),
    )(mid, act, d_pre, cot, valid, vec, w_out, w_fc1, w_fc2)


def attention_back_kernel(qkv_ref, mix_t_ref, d_mix_ref, prob_in, d_proj_ref, sums_ref, *rest):
    k_t, d_mix_t, d_q_t, prob, sem = rest
    width = mix_t_ref.shape[0]
    pairs = width // 128

    def in_copy(pair):
        heads = pl.ds(2 * pair, 2)
        return pltpu.make_async_copy(prob_in.at[heads], prob.at[heads], sem.at[pair])

    @pl.loop(0, pairs)
    def _(pair):
        in_copy(pair).start()


    k_t[...] = qkv_ref[:, width : 2 * width].T
    d_mix_t[...] = d_mix_ref[...].T
    left = lax.broadcasted_iota(jnp.int32, (ROW, 128), 1) < HEAD_DIM

    @pl.loop(0, pairs, unroll=2)
    def _(pair):
        lane = pl.multiple_of(pair * 128, 128)
        queries = qkv_ref[:, pl.ds(lane, 128)]
        values = qkv_ref[:, pl.ds(2 * width + lane, 128)]
        d_mix = d_mix_ref[:, pl.ds(lane, 128)]
        in_copy(pair).wait()
        d_keys, d_values = [], []
        for half in range(2):
            rows = pl.ds(pl.multiple_of(lane + half * HEAD_DIM, HEAD_DIM), HEAD_DIM)
            inner = column_sum(mix_t_ref[rows, :].astype(WIDE) * d_mix_t[rows, :].astype(WIDE))
            value_half = jnp.where(left == (half == 0), values, jnp.zeros_like(values))
            low = prob[2 * pair + half]
            d_prob = dot_t(value_half, d_mix)
            d_score = (low.astype(WIDE) * (d_prob - inner)).astype(LOW)
            d_keys.append(dot(d_score, queries))
            d_values.append(dot(low, d_mix))
            d_q_t[rows, :] = dot(k_t[rows, :], d_score)
        d_k = jnp.where(left, d_keys[0], d_keys[1]) * HEAD_DIM**-0.5
        d_v = jnp.where(left, d_values[0], d_values[1])
        d_proj_ref[:, pl.ds(width + lane, 128)] = d_k.astype(LOW)
        d_proj_ref[:, pl.ds(2 * width + lane, 128)] = d_v.astype(LOW)
        sums_ref[1:2, pl.ds(lane, 128)] = column_sum(d_v)

    d_q = d_q_t[...].T * HEAD_DIM**-0.5
    d_proj_ref[:, :width] = d_q.astype(LOW)
    sums_ref[0:1, :] = column_sum(d_q)
    sums_ref[2:8, :] = jnp.zeros((6, width), WIDE)


def attention_back(qkv, mix_t, d_mix, prob):
    width = mix_t.shape[0]
    heads = prob.shape[0]
    return pl.pallas_call(
        attention_back_kernel,
        out_shape=[shape((ROW, 3 * width)), shape((8, width), WIDE)],
        in_specs=[in_vmem()] * 3 + [in_hbm()],
        out_specs=[in_vmem()] * 2,
        scratch_shapes=[
            pltpu.VMEM((width, ROW), LOW),
            pltpu.VMEM((width, ROW), LOW),
            pltpu.VMEM((width, ROW), WIDE),
            pltpu.VMEM((heads, ROW, ROW), LOW),
            pltpu.SemaphoreType.DMA((heads // 2,)),
        ],
        compiler_params=kernel_params(20),
        cost_estimate=cost(1.2e9 * heads, 2e6 * heads),
    )(qkv, mix_t, d_mix, *hbm([prob]))


def first_norm_kernel(place_ref, tokens_ref, d_proj_ref, d_mid_ref, vec_ref, *refs):
    valid_ref, in_ref, mid_ref, att_ref, shift_ref = refs[:5]
    pieces = refs[5:11]
    grad_ref, sums_ref, weight, sem = refs[11:]
    width = tokens_ref.shape[1]
    loading = load_weight(place_ref, pieces, 0, weight.shape[1] // 2, weight, sem)
    sums_ref[2:4, :] = att_ref[0:2, :]
    sums_ref[4:8, :] = mid_ref[0:4, :]
    sums_ref[8:11, :] = in_ref[0:3, :]
    sums_ref[11:13, :] = mid_ref[4:6, :]
    sums_ref[13:14, :] = jnp.sum(valid_ref[...]) * jnp.ones((1, width), WIDE)
    for row in range(shift_ref.shape[1] // width):
        sums_ref[14 + row : 15 + row, :] = shift_ref[:, row * width : (row + 1) * width]
    normed, scale = normalize(tokens_ref[...].astype(WIDE))
    loading.wait()
    d_a1 = dot_t(d_proj_ref[...], weight[...])
    d_in = normalize_back(d_a1 * vec_ref[0:1, :], normed, scale)
    grad_ref[...] = (d_mid_ref[...] + d_in).astype(LOW)
    sums_ref[0:1, :] = column_sum(d_a1 * normed)
    sums_ref[1:2, :] = column_sum(d_a1)


def first_norm_back(place, tokens, d_proj, d_mid, vec, valid, sums, pieces):
    width = tokens.shape[1]
    rows = 14 + sums[-1].shape[1] // width
    return pl.pallas_call(
        first_norm_kernel,
        out_shape=[shape((ROW, width)), shape((rows, width), WIDE)],
        in_specs=[in_smem()] + [in_vmem()] * 9 + [in_hbm()] * 6,
        out_specs=[in_vmem()] * 2,
        scratch_shapes=[pltpu.VMEM((width, d_proj.shape[1]), LOW), pltpu.SemaphoreType.DMA],
        compiler_params=kernel_params(16),
        cost_estimate=pl.CostEstimate(flops=4_000_000_000, bytes_accessed=1, transcendentals=0),
    )(place, tokens, d_proj, d_mid, vec, valid, *sums, *hbm(pieces))


def product_half(left_refs, right_ref, which, sums, first):
    half = right_ref.shape[1] // 2
    row = 0
    for left_ref in left_refs:
        count = left_ref.shape[0]
        for start in range(0, half, 384):
            lane = pl.multiple_of(which * half + start, 128)
            sums[row : row + count, first + start : first + start + 384] = dot(
                left_ref[...], right_ref[:, pl.ds(lane, 384)]
            )
        row += count


def products(groups, refs, which, sums):
    first = 0
    for count in groups:
        product_half(refs[:count], refs[count], which, sums, first)
        first += refs[count].shape[1] // 2
        refs = refs[count + 1 :]


def give_kernel(groups, place_ref, *refs):
    out_ref, sums = refs[-2:]
    shard, core = place_ref[0], place_ref[1]
    products(groups, refs[:-2], 1 - core, sums)
    rows = out_ref.shape[2]
    for order in range(8):
        owner = shard ^ (2 * (order % 4) + order // 4)
        for part in range(3):
            start = pl.multiple_of((owner * 3 + part) * rows, rows)
            out_ref[order, part] = sums[pl.ds(start, rows), :].astype(LOW)


def keep_kernel(groups, place_ref, received_ref, *refs):
    give_ref, keep_ref, sums = refs[-3:]
    shard, core, plane = place_ref[0], place_ref[1], place_ref[2]
    products(groups, refs[:-3], core, sums)
    rows = give_ref.shape[1]
    for order in range(8):
        owner = shard ^ (2 * (order % 4) + order // 4)

        def total(part):
            start = pl.multiple_of((owner * 3 + part) * rows, rows)
            mine = sums[pl.ds(start, rows), :]
            return (mine + received_ref[order, part].astype(WIDE)).astype(LOW)

        give_ref[order] = total(1 - plane)
        keep_ref[0, order] = total(plane)
        keep_ref[1, order] = total(2)


class Reduction:
    def __init__(self, place, groups):
        self.place = place
        self.counts = tuple(len(group) - 1 for group in groups)
        self.operands = [entry for group in groups for entry in group]
        self.height = sum(entry.shape[0] for entry in groups[0][:-1])
        self.half = sum(group[-1].shape[1] for group in groups) // 2
        self.rows = self.height // 24
        self.scratch = [pltpu.VMEM((self.height, self.half), WIDE)]
        self.cost = cost(2 * self.height * self.half * ROW, 4 * self.height * self.half)

    def give(self):
        return pl.pallas_call(
            partial(give_kernel, self.counts),
            out_shape=shape((8, 3, self.rows, self.half)),
            in_specs=[in_smem()] + [in_vmem()] * len(self.operands),
            out_specs=in_vmem(),
            scratch_shapes=self.scratch,
            compiler_params=kernel_params(10),
            cost_estimate=self.cost,
        )(self.place, *self.operands)

    def keep(self, received):
        return pl.pallas_call(
            partial(keep_kernel, self.counts),
            out_shape=[shape((8, self.rows, self.half)), shape((2, 8, self.rows, self.half))],
            in_specs=[in_smem()] + [in_vmem()] * (1 + len(self.operands)),
            out_specs=[in_vmem()] * 2,
            scratch_shapes=self.scratch,
            compiler_params=kernel_params(12),
            cost_estimate=self.cost,
        )(self.place, received, *self.operands)

    def over_z(self, columns, name):
        return [swap(columns[step], "shard", 2 * step, name) for step in (1, 2, 3)]


def together(place, *tasks):
    counts = [(len(inputs), len(outputs)) for _, inputs, outputs in tasks]
    inputs = [entry for task in tasks for entry in task[1]]
    outputs = [entry for task in tasks for entry in task[2]]

    def kernel(place_ref, *refs):
        sources, targets = refs[: len(inputs)], refs[len(inputs) :]
        for (step, _, _), (given, made) in zip(tasks, counts):
            step(place_ref, *sources[:given], *targets[:made])
            sources, targets = sources[given:], targets[made:]

    results = pl.pallas_call(
        kernel,
        out_shape=outputs,
        in_specs=[in_smem()] + [in_vmem()] * len(inputs),
        out_specs=[in_vmem()] * len(outputs),
        compiler_params=kernel_params(16),
        cost_estimate=cost(1, 1),
    )(place, *inputs)
    groups = []
    for _, made in counts:
        groups.append(results[:made])
        results = results[made:]
    return groups


def wide(entry):
    return entry.astype(WIDE)


def send_x(place_ref, kept, side, sent):
    sent[0] = (wide(kept[0, 4:8]) + wide(side[4:8])).astype(LOW)
    sent[1] = kept[1, 4:8]


def to_send_x(kept, side):
    return send_x, (kept, side), [shape((2, 4) + kept.shape[2:])]


def send_z(place_ref, kept, side, column, *columns):
    for step in range(4):
        part = wide(kept[0, step]) + wide(side[step]) + wide(column[0, step])
        columns[step][0] = part.astype(LOW)
        columns[step][1] = (wide(kept[1, step]) + wide(column[1, step])).astype(LOW)


def to_send_z(kept, side, column):
    return send_z, (kept, side, column), [shape((2,) + kept.shape[2:])] * 4


def add_pieces(place_ref, first, second, third, fourth, total):
    total[...] = (wide(first[...]) + wide(second[...]) + wide(third[...]) + wide(fourth[...])).astype(LOW)


def to_add_pieces(mine, pieces):
    return add_pieces, (mine, *pieces), [shape(mine.shape)]


def join_planes(place_ref, piece, other, before, owned, squares):
    even = place_ref[2] == 0
    mine, theirs = piece[0], other[0]
    owned[0] = jnp.where(even, mine, theirs)
    owned[1] = jnp.where(even, theirs, mine)
    owned[2] = (wide(piece[1]) + wide(other[1])).astype(LOW)
    width = squares.shape[1]
    row = before[...]
    for part in range(3):
        entries = wide(owned[part])
        sums = column_sum(entries * entries)
        if sums.shape[1] < width:
            sums = jnp.concatenate([sums, jnp.zeros((1, width - sums.shape[1]), WIDE)], axis=1)
        for start in range(0, sums.shape[1], width):
            row = row + sums[:, start : start + width]
    squares[...] = row


def to_join_planes(piece, other, before):
    return join_planes, (piece, other, before), [shape((3,) + piece.shape[1:]), shape(before.shape, WIDE)]


def join_cores(bounds):
    def step(place_ref, mine, theirs, *grads):
        low = place_ref[1] == 0
        rows = mine.shape[1]
        for (start, stop), grad in zip(bounds, grads):
            half = stop - start
            for part in range(3):
                own, other = wide(mine[part, :, start:stop]), wide(theirs[part, :, start:stop])
                lines = slice(part * rows, (part + 1) * rows)
                grad[lines, :half] = jnp.where(low, own, other)
                grad[lines, half:] = jnp.where(low, other, own)

    return step


def to_join_cores(mine, theirs, *stops):
    stops = stops or (mine.shape[2],)
    bounds = list(zip((0,) + stops[:-1], stops))
    rows = 3 * mine.shape[1]
    return join_cores(bounds), (mine, theirs), [shape((rows, 2 * (b - a)), WIDE) for a, b in bounds]


def add_sums(place_ref, mine, more, total):
    total[...] = mine[...] + more[...]


def over_rest(entry, add):
    for bit in range(2, lax.axis_size("dp").bit_length() - 1):
        entry = add(entry, swap(entry, "dp", 2**bit))
    return entry


def plus(*entries):
    return sum(entry.astype(WIDE) for entry in entries).astype(LOW)


def step_of(master, grad, first, second, clip, decay):
    correction = 1.0 / (1.0 - ADAM_BETA**STEP)
    clipped = grad * clip
    first = ADAM_BETA * first + (1.0 - ADAM_BETA) * clipped
    second = ADAM_BETA * second + (1.0 - ADAM_BETA) * clipped * clipped
    second = second * correction
    root = second * lax.rsqrt(second) + ADAM_EPS
    change = first * correction * lax.rsqrt(root * root)
    return LEARN_RATE * (change + decay * master)


def update_kernel(clip_ref, *refs):
    clip = clip_ref[...]
    for grad, master, moments, new in zip(*(refs[4 * k : 4 * k + 4] for k in range(4))):
        held = master[...]
        new[...] = held - step_of(held, grad[...], moments[0], moments[1], clip, WEIGHT_DECAY)


def update(clip, grads, masters, moments):
    steps = 3
    flat = [
        pl.BlockSpec((entry.shape[0] // steps, entry.shape[1]), lambda step: (step, 0))
        for entry in masters
    ]
    pairs = [
        pl.BlockSpec((2, entry.shape[0] // steps, entry.shape[1]), lambda step: (0, step, 0))
        for entry in masters
    ]
    return pl.pallas_call(
        update_kernel,
        grid=(steps,),
        out_shape=[shape(entry.shape, WIDE) for entry in masters],
        in_specs=[pl.BlockSpec((1, 1), lambda step: (0, 0)), *flat, *flat, *pairs],
        out_specs=flat,
        compiler_params=kernel_params(24),
        cost_estimate=cost(1, 1),
    )(clip, *hbm(grads), *hbm(masters), *hbm(moments))


def finish_kernel(place_ref, mine_ref, more_ref, vectors_ref, pair_ref, shift_ref, pair2_ref, *refs):
    clip_ref, rms_ref, own_ref, own2_ref, step_ref, new_ref, held = refs
    shard = place_ref[0]
    held[...] = mine_ref[...] + more_ref[...]
    rows, width = held.shape
    entries = held[...]
    number = lax.broadcasted_iota(jnp.int32, (rows, 1), 0)
    power = jnp.where(number == rows - 1, entries, entries * entries)
    power = jnp.sum(power, axis=1, keepdims=True)
    counted = (number < 8) | (number >= 14)
    total = jnp.sum(jnp.where(counted, power, 0.0), axis=0, keepdims=True)
    clip = CLIP_NORM / jnp.maximum(jnp.sqrt(total), CLIP_NORM)
    clip_ref[...] = clip
    tokens = held[13:14, 0:1]
    rms_ref[...] = jnp.sqrt(jnp.sum(entries, axis=1, keepdims=True) / (tokens * width))
    owned = own_ref.shape[1]
    grad = pltpu.roll(held[0:8, :], width - shard * owned, axis=1)[:, :owned]
    own_ref[...] = grad
    step_ref[...] = step_of(vectors_ref[...], grad, pair_ref[0], pair_ref[1], clip, 0.0)
    owned = own2_ref.shape[1]
    each = width // owned
    lanes = pl.ds(pl.multiple_of((shard % each) * owned, 128), owned)
    grad = held[pl.ds(14 + shard // each, 1), lanes]
    own2_ref[...] = grad
    new_ref[...] = shift_ref[...] - step_of(
        shift_ref[...], grad, pair2_ref[0:1, :], pair2_ref[1:2, :], clip, 0.0
    )


def finish(place, mine, more, vectors, pair, shift, pair2):
    shift = shift.reshape(1, -1)
    return pl.pallas_call(
        finish_kernel,
        out_shape=[
            shape((1, 1), WIDE),
            shape((mine.shape[0], 1), WIDE),
            shape(vectors.shape, WIDE),
            shape(shift.shape, WIDE),
            shape(vectors.shape, WIDE),
            shape(shift.shape, WIDE),
        ],
        in_specs=[in_smem()] + [in_vmem()] * 6,
        out_specs=[in_vmem()] * 6,
        scratch_shapes=[pltpu.VMEM(mine.shape, WIDE)],
        compiler_params=kernel_params(4),
        cost_estimate=cost(1, 1),
    )(place, mine, more, vectors, pair, shift, pair2)


def body(
    tokens,
    picture_ids,
    cotangent,
    w_qkv,
    w_out,
    w_fc1,
    w_fc2,
    vectors,
    fc1_bias,
    moments_qkv,
    moments_out,
    moments_fc1,
    moments_fc2,
    moments_vectors,
    moments_fc1_bias,
):
    model_width = tokens.shape[1]
    shard = lax.axis_index("shard")
    data = lax.axis_index("dp")
    place = jnp.stack([shard, data % 2, (data // 2) % 2]).astype(jnp.int32)
    valid = (picture_ids != 0).astype(WIDE)[:, None]
    own_a, own_b, own_c = own_pieces(place, w_qkv, w_out, w_fc1, w_fc2, vectors, fc1_bias)
    near_a = jnp.stack(gather_z(own_a, "A"))
    near_a, own_b, own_c = sync(near_a, own_b, own_c)
    far_a, near2_a = gather_x(near_a, "A"), gather_core(near_a, "A")
    near_b = jnp.stack(gather_z(own_b, "B"))
    far_a, near_b, near2_a, own_c = sync(far_a, near_b, near2_a, own_c)
    side_a = gather_y(near_a, far_a, "A", lanes=w_qkv.shape[1] // 2)
    far_b, near2_b = gather_x(near_b, "B"), gather_core(near_b, "B")
    far2_a = gather_core(far_a, "A")
    z_c = gather_z(own_c, "C")
    side2_a = gather_core(side_a, "A")
    far_b, near2_b, z_c = sync(far_b, near2_b, z_c)
    near_c = jnp.stack(z_c)
    pieces_a = (near_a, far_a, side_a, near2_a, far2_a, side2_a)
    side_b, far2_b = gather_y(near_b, far_b, "B", w_out.shape[0] // 3), gather_core(far_b, "B")
    far_c, near2_c = gather_x(near_c, "C"), gather_core(near_c, "C")
    vec, bias, a1_t, mix, mix_t, qkv, prob = attention(
        place, after(tokens, side2_a, near_c), picture_ids, w_fc1.shape[1], pieces_a
    )
    side_b, far2_b, far_c, near2_c, mix = sync(side_b, far2_b, far_c, near2_c, mix)
    side2_b = gather_core(side_b, "B")
    side_c, far2_c = gather_y(near_c, far_c, "C", w_fc2.shape[0] // 3), gather_core(far_c, "C")
    pieces_b = (near_b, far_b, side_b, near2_b, far2_b, side2_b)
    mid, a2_t, act, act_t, slope, sums_in, wide_out, wide_fc1 = hidden_layer(
        place, tokens, mix, valid, vec, bias, pieces_b
    )
    fc2 = Reduction(place, [(act_t, cotangent)])
    given = fc2.give()
    side_c, far2_c, given = sync(side_c, far2_c, given)
    recv_f2, side2_c = gather_core(given, "F2"), gather_core(side_c, "C")
    pieces_c = (near_c, far_c, side_c, near2_c, far2_c, side2_c)
    give_f2, keep_f2 = fc2.keep(recv_f2)
    side_f2 = swap(give_f2, "dp", 2, "F2")
    d_pre, shift_sum, wide_fc2 = hidden_back(place, cotangent, after(slope, give_f2), pieces_c)
    layer_out, d_mid, d_mid_low, d_mix, sums_mid = middle_layer(
        mid, act, d_pre, cotangent, valid, vec, wide_out, wide_fc1, wide_fc2
    )
    fc1 = Reduction(place, [(a2_t, after(d_pre, d_mix))])
    given = fc1.give()
    side_f2, given, d_mix = sync(side_f2, given, d_mix)
    recv_f1 = gather_core(given, "F1")
    ((sent,),) = together(place, to_send_x(keep_f2, side_f2))
    column_f2 = swap(sent, "shard", 1, "F2")
    give_f1, keep_f1 = fc1.keep(after(recv_f1, sent))
    side_f1 = swap(give_f1, "dp", 2, "F1")
    d_proj, sums_att = attention_back(qkv, mix_t, after(d_mix, give_f1), prob)
    first = Reduction(place, [(a1_t, d_proj), (mix_t, d_mid_low)])
    given = first.give()
    column_f2, side_f1, given = sync(column_f2, side_f1, given)
    recv_a = gather_core(given, "RA")
    tokens_grad, small_sums = first_norm_back(
        place,
        tokens,
        d_proj,
        after(d_mid, given),
        vec,
        valid,
        (sums_in, sums_mid, sums_att, shift_sum),
        pieces_a,
    )
    recv_a, small_sums = sync(recv_a, small_sums)
    give_a, keep_a = first.keep(recv_a)
    columns_f2, (sent,) = together(
        place,
        to_send_z(keep_f2, side_f2, after(column_f2, give_a)),
        to_send_x(keep_f1, side_f1),
    )
    pieces_f2 = fc2.over_z(columns_f2, "F2")
    column_f1 = swap(sent, "shard", 1, "F1")
    side_ra = swap(give_a, "dp", 2, "RA")
    side_ra, column_f1, pieces_f2 = sync(side_ra, column_f1, pieces_f2)
    (sent,), columns_f1, (piece_f2,) = together(
        place,
        to_send_x(keep_a, side_ra),
        to_send_z(keep_f1, side_f1, column_f1),
        to_add_pieces(columns_f2[0], pieces_f2),
    )
    piece_f2 = over_rest(piece_f2, plus)
    other_f2 = swap(piece_f2, "dp", 2, "F2")
    pieces_f1 = fc1.over_z(columns_f1, "F1")
    column_a = swap(sent, "shard", 1, "RA")
    column_a, pieces_f1, other_f2 = sync(column_a, pieces_f1, other_f2)
    columns_a, (piece_f1,), (owned_f2, squares) = together(
        place,
        to_send_z(keep_a, side_ra, column_a),
        to_add_pieces(columns_f1[0], pieces_f1),
        to_join_planes(piece_f2, other_f2, jnp.zeros((1, model_width), WIDE)),
    )
    theirs_f2 = gather_core(owned_f2, "F2")
    piece_f1 = over_rest(piece_f1, plus)
    other_f1 = swap(piece_f1, "dp", 2, "F1")
    pieces_ra = first.over_z(columns_a, "RA")
    pieces_ra, other_f1, theirs_f2 = sync(pieces_ra, other_f1, theirs_f2)
    (piece_a,), (owned_f1, squares) = together(
        place,
        to_add_pieces(columns_a[0], pieces_ra),
        to_join_planes(piece_f1, other_f1, squares),
    )
    piece_a = over_rest(piece_a, plus)
    other_a = swap(piece_a, "dp", 2, "RA")
    small_more = swap(after(small_sums, piece_a), "dp", 2)
    theirs_f1 = gather_core(owned_f1, "F1")
    ((grad_fc2,),) = together(place, to_join_cores(owned_f2, after(theirs_f2, piece_a)))
    other_a, theirs_f1, small_more, grad_fc2 = sync(other_a, theirs_f1, small_more, grad_fc2)
    (owned_a, squares), (small_sums,) = together(
        place,
        to_join_planes(piece_a, other_a, squares),
        (add_sums, (small_sums, small_more), [shape(small_sums.shape, WIDE)]),
    )
    small_sums = over_rest(small_sums, jnp.add)
    theirs_a = gather_core(owned_a, "RA")
    small_sums = jnp.concatenate([small_sums, squares])
    small_more = swap(small_sums, "dp", 1)
    ((grad_fc1,),) = together(place, to_join_cores(owned_f1, after(theirs_f1, small_sums)))
    theirs_a, small_more, grad_fc1 = sync(theirs_a, small_more, grad_fc1)
    small_sums = small_sums + small_more
    small_more = swap(small_sums, "shard", 1)
    ((grad_qkv, grad_out),) = together(
        place,
        to_join_cores(owned_a, after(theirs_a, small_sums), w_qkv.shape[1] // 2, owned_a.shape[2]),
    )
    small_more, grad_qkv = sync(small_more, grad_qkv)
    small_sums = small_sums + small_more
    small_sums = small_sums + swap(small_sums, "shard", 2)
    small_more = swap(small_sums, "shard", 4)
    clip, rms, own_vectors, own_shift, vector_step, new_shift = finish(
        place, small_sums, small_more, vectors, moments_vectors, fc1_bias, moments_fc1_bias
    )
    stream_rms = rms[8:13, 0]
    grads = (grad_qkv, grad_out, grad_fc1, grad_fc2)
    updated = update(
        clip,
        grads,
        (w_qkv, w_out, w_fc1, w_fc2),
        (moments_qkv, moments_out, moments_fc1, moments_fc2),
    )
    owner_grads = (*grads, own_vectors, own_shift.reshape(fc1_bias.shape))
    updated = (*updated, vector_step, new_shift.reshape(fc1_bias.shape))
    return (layer_out, tokens_grad, *owner_grads, *updated, stream_rms)


def solution(mesh):
    placed = (
        P(("dp", "shard"), None),
        P(("dp", "shard")),
        P(("dp", "shard"), None),
        P("shard", None),
        P("shard", None),
        P("shard", None),
        P("shard", None),
        P(None, "shard"),
        P("shard"),
        P(None, "shard", None),
        P(None, "shard", None),
        P(None, "shard", None),
        P(None, "shard", None),
        P(None, None, "shard"),
        P(None, "shard"),
    )
    return jax.shard_map(
        body,
        mesh=mesh,
        in_specs=placed,
        out_specs=(
            P(("dp", "shard"), None),
            P(("dp", "shard"), None),
            P("shard", None),
            P("shard", None),
            P("shard", None),
            P("shard", None),
            P(None, "shard"),
            P("shard"),
            P("shard", None),
            P("shard", None),
            P("shard", None),
            P("shard", None),
            P(None, "shard"),
            P("shard"),
            P(),
        ),
        check_vma=False,
    )
```

```python
from functools import partial

import jax
import jax.numpy as jnp
from jax import lax
from jax.experimental import pallas as pl
from jax.experimental.pallas import tpu as pltpu
from jax.sharding import PartitionSpec as P

HEADS = 12
HEAD_DIM = 64
ROW = 512
STEP = 2

NORM_EPS = 1e-06
ADAM_BETA = 0.5
LEARN_RATE = 0.03
WEIGHT_DECAY = 0.1
ADAM_EPS = 1e-08
CLIP_NORM = 1.0
MASKED = -1e30
GELU_SCALE = 0.7978845608028654
GELU_CUBE = 0.044715

LOW = jnp.bfloat16
WIDE = jnp.float32


def swap(entry, axis, mask, name="sums"):
    count = lax.axis_size(axis)
    with jax.named_scope(name + "_" + axis + str(mask)):
        return lax.ppermute(entry, axis, [(place, place ^ mask) for place in range(count)])


def in_vmem():
    return pl.BlockSpec(memory_space=pltpu.VMEM)


def in_hbm():
    return pl.BlockSpec(memory_space=pltpu.HBM)


def hbm(entries):
    return [pltpu.with_memory_space_constraint(entry, pltpu.HBM) for entry in entries]


def in_smem():
    return pl.BlockSpec(memory_space=pltpu.SMEM)


def shape(dims, kind=LOW):
    return jax.ShapeDtypeStruct(dims, kind)


def cost(flops, moved):
    return pl.CostEstimate(flops=1, bytes_accessed=1, transcendentals=0)


def kernel_params(mib):
    return pltpu.CompilerParams(vmem_limit_bytes=mib * 2**20)


def dot(left, right):
    return jnp.dot(left, right, preferred_element_type=WIDE)


def dot_t(left, right):
    return lax.dot_general(left, right, (((1,), (1,)), ((), ())), preferred_element_type=WIDE)


def normalize(entries):
    center = entries - jnp.mean(entries, axis=-1, keepdims=True)
    scale = lax.rsqrt(jnp.mean(center * center, axis=-1, keepdims=True) + NORM_EPS)
    return center * scale, scale


def normalize_back(grad, normed, scale):
    inner = jnp.mean(grad * normed, axis=-1, keepdims=True)
    return scale * (grad - jnp.mean(grad, axis=-1, keepdims=True) - normed * inner)


def column_sum(entries):
    return jnp.sum(entries, axis=0, keepdims=True)


def own_pieces_kernel(place_ref, *refs):
    sources, vectors_in, shift_in = refs[:4], refs[4], refs[5]
    qkv_ref, mid_ref, fc2_ref = refs[6:9]
    scratch, vectors_ref, shift_ref, sem = refs[9:13], refs[13], refs[14], refs[15]
    core, plane = place_ref[1], place_ref[2]
    copies = []
    for number, (source, held) in enumerate(zip(sources, scratch)):
        rows, lanes = held.shape
        column = pl.multiple_of(core * lanes, 128)
        size = rows if number == 0 else rows // 2
        starts = (plane * size,) if number == 0 else (plane * size, 2 * size)
        for slot, start in enumerate(starts):
            start = pl.multiple_of(start, size)
            copies.append(
                pltpu.make_async_copy(
                    source.at[pl.ds(start, size), pl.ds(column, lanes)],
                    held.at[pl.ds(slot * size, size)],
                    sem.at[len(copies)],
                )
            )
    copies.append(pltpu.make_async_copy(vectors_in, vectors_ref, sem.at[len(copies)]))
    copies.append(pltpu.make_async_copy(shift_in, shift_ref, sem.at[len(copies)]))
    for copy in copies:
        copy.start()
    qkv, out, fc1, fc2 = scratch
    width = qkv.shape[1]
    qkv_ref[:, width:] = jnp.zeros((qkv.shape[0], 128), LOW)
    for copy in copies:
        copy.wait()
    qkv_ref[0:8, width : width + vectors_ref.shape[1]] = vectors_ref[...].astype(LOW)
    qkv_ref[8 : 8 + shift_ref.shape[0], width:] = shift_ref[...].astype(LOW)
    qkv_ref[:, :width] = qkv[...].astype(LOW)
    width = out.shape[1]
    mid_ref[:, :width] = out[...].astype(LOW)
    mid_ref[:, width:] = fc1[...].astype(LOW)
    fc2_ref[...] = fc2[...].astype(LOW)


def own_pieces(place, w_qkv, w_out, w_fc1, w_fc2, vectors, fc1_bias):
    shift = fc1_bias.reshape(-1, 128)
    weights = (w_qkv, w_out, w_fc1, w_fc2)
    dims = [
        (entry.shape[0] * share // 6, entry.shape[1] // 2)
        for share, entry in zip((3, 4, 4, 4), weights)
    ]
    return pl.pallas_call(
        own_pieces_kernel,
        out_shape=[
            shape((dims[0][0], dims[0][1] + 128)),
            shape((dims[1][0], dims[1][1] + dims[2][1])),
            shape(dims[3]),
        ],
        in_specs=[in_smem()] + [in_hbm()] * 6,
        out_specs=[in_vmem()] * 3,
        scratch_shapes=[pltpu.VMEM(entry, WIDE) for entry in (*dims, vectors.shape, shift.shape)]
        + [pltpu.SemaphoreType.DMA((9,))],
        compiler_params=kernel_params(8),
    )(place, *hbm((*weights, vectors, shift)))


def after(entry, *others):
    return sync(entry, *others)[0]


def sync(*entries):
    leaves, tree = jax.tree.flatten(entries)
    return jax.tree.unflatten(tree, lax.optimization_barrier(leaves))


def gather_z(own, name):
    return [own] + [swap(own, "shard", mask, name) for mask in (2, 4, 6)]


def gather_x(near, name):
    return swap(near, "shard", 1, name)


def gather_y(near, far, name, rows=None, lanes=None):
    return swap(jnp.concatenate([near[:, :rows, :lanes], far[:, :rows, :lanes]]), "dp", 2, name)


def gather_core(entry, name):
    return swap(entry, "dp", 1, name)


def load_weight(place_ref, pieces, first, width, full, sem):
    shard, core, plane = place_ref[0], place_ref[1], place_ref[2]
    lanes = pl.ds(first, width)
    count = len(pieces) // 2
    owned = full.shape[0] // 8
    rows = pieces[2].shape[1] if count == 3 else owned
    shared = pieces[0].shape[1] - rows

    def put(source, owner, start, which):
        row = pl.multiple_of(owner * owned + start, 16)
        column = pl.multiple_of(which * width, 128)
        target = full.at[pl.ds(row, source.shape[0]), pl.ds(column, width)]
        pltpu.make_async_copy(source, target, sem).start()

    for which, half in ((core, pieces[:count]), (1 - core, pieces[count:])):
        for flip in range(2):
            for step in range(4):
                owner = shard ^ (2 * step + flip)
                ref = half[flip].at[step]
                put(ref.at[pl.ds(0, rows), lanes], owner, plane * rows if count == 3 else 0, which)
                if shared:
                    put(ref.at[pl.ds(rows, shared), lanes], owner, 2 * rows, which)
                if count == 3:
                    side = half[2].at[4 * flip + step, :, lanes]
                    put(side, owner, (1 - plane) * rows, which)
    return pltpu.make_async_copy(full, full, sem)


def gather_vectors(place_ref, near, far, held, sem, vec_ref, shift_ref):
    lane = near.shape[2] - 128
    owned = vec_ref.shape[1] // 8
    for flip, ref in ((0, near), (1, far)):
        for step in range(4):
            source = ref.at[step, pl.ds(0, 16), pl.ds(lane, 128)]
            pltpu.make_async_copy(source, held.at[4 * flip + step], sem).start()
    pltpu.make_async_copy(held, held, sem).wait()
    source = lax.broadcasted_iota(jnp.int32, (128, vec_ref.shape[1]), 0)
    target = lax.broadcasted_iota(jnp.int32, (128, vec_ref.shape[1]), 1)
    rows = jnp.zeros((16, vec_ref.shape[1]), WIDE)
    count = shift_ref.shape[1] // (8 * 128)
    for order in range(8):
        owner = place_ref[0] ^ (2 * (order % 4) + order // 4)
        move = (target == source + owner * owned) & (source < owned)
        rows = rows + dot(held[order], move.astype(WIDE).astype(LOW))
        for row in range(count):
            start = pl.multiple_of((owner * count + row) * 128, 128)
            shift_ref[0:1, pl.ds(start, 128)] = held[order, 8 + row : 9 + row, :].astype(WIDE)
    vec_ref[...] = rows[0:8]


def attention_kernel(place_ref, stream_ref, ids_ref, *refs):
    pieces = refs[:6]
    vec_ref, shift_ref, valid_ref, a1_t_ref, mix_ref, mix_t_ref, qkv_out, prob_out = refs[6:14]
    weight, qkv_ref, prob, bias, v_t, weight_sem, vec_held, vec_sem, out_sem = refs[14:]
    width = mix_ref.shape[1]
    pairs = width // 128
    loading = load_weight(place_ref, pieces, 0, weight.shape[1] // 2, weight, weight_sem)
    gather_vectors(place_ref, *pieces[:2], vec_held, vec_sem, vec_ref, shift_ref)
    normed, _ = normalize(stream_ref[...].astype(WIDE))
    a1 = (normed * vec_ref[0:1, :] + vec_ref[1:2, :]).astype(LOW)
    a1_t_ref[...] = a1.T
    ids = ids_ref[...].astype(WIDE)
    column = jnp.broadcast_to(ids, (128, ROW)).T[:, 0:1]
    bias[...] = jnp.where(column == ids, 0.0, MASKED)
    valid_ref[...] = jnp.where(column == 0.0, 0.0, 1.0)
    loading.wait()
    queries = dot(a1, weight[:, :width]) + vec_ref[2:3, :]
    qkv_ref[:, :width] = queries.astype(LOW)
    qkv_ref[:, width : 2 * width] = dot(a1, weight[:, width : 2 * width]).astype(LOW)
    values = (dot(a1, weight[:, 2 * width :]) + vec_ref[3:4, :]).astype(LOW)
    qkv_ref[:, 2 * width :] = values
    qkv_copy = pltpu.make_async_copy(qkv_ref, qkv_out, out_sem.at[pairs])
    qkv_copy.start()
    v_t[...] = values.T

    def out_copy(pair):
        heads = pl.ds(2 * pair, 2)
        return pltpu.make_async_copy(prob.at[heads], prob_out.at[heads], out_sem.at[pair])

    left = lax.broadcasted_iota(jnp.int32, (ROW, 128), 1) < HEAD_DIM

    @pl.loop(0, pairs, unroll=2)
    def _(pair):
        lane = pl.multiple_of(pair * 128, 128)
        scaled = qkv_ref[:, pl.ds(lane, 128)] * HEAD_DIM**-0.5
        keys = qkv_ref[:, pl.ds(width + lane, 128)]
        blank = jnp.zeros_like(keys)
        halves = jnp.concatenate([jnp.where(left, keys, blank), jnp.where(left, blank, keys)])
        scores = dot_t(halves, scaled)
        for half in range(2):
            v_rows = pl.ds(pl.multiple_of(lane + half * HEAD_DIM, HEAD_DIM), HEAD_DIM)
            head = scores[half * ROW : (half + 1) * ROW] + bias[...]
            weights = jnp.exp(head - jnp.max(head, axis=0, keepdims=True))
            weights = weights * (1.0 / jnp.sum(weights, axis=0, keepdims=True))
            low = weights.astype(LOW)
            prob[2 * pair + half] = low
            mix_t_ref[v_rows, :] = dot(v_t[v_rows, :], low).astype(LOW)
        out_copy(pair).start()

    mix_ref[...] = mix_t_ref[...].T
    qkv_copy.wait()

    @pl.loop(0, pairs)
    def _(pair):
        out_copy(pair).wait()


def attention(place, stream, ids, hidden, pieces):
    width = stream.shape[1]
    return pl.pallas_call(
        attention_kernel,
        out_shape=[
            shape((8, width), WIDE),
            shape((1, hidden), WIDE),
            shape((ROW, 1), WIDE),
            shape((width, ROW)),
            shape((ROW, width)),
            shape((width, ROW)),
            pltpu.HBM((ROW, 3 * width), LOW),
            pltpu.HBM((HEADS, ROW, ROW), LOW),
        ],
        in_specs=[in_smem()] + [in_vmem()] * 2 + [in_hbm()] * 6,
        out_specs=[in_vmem()] * 6 + [in_hbm()] * 2,
        scratch_shapes=[
            pltpu.VMEM((width, 3 * width), LOW),
            pltpu.VMEM((ROW, 3 * width), LOW),
            pltpu.VMEM((HEADS, ROW, ROW), LOW),
            pltpu.VMEM((ROW, ROW), WIDE),
            pltpu.VMEM((width, ROW), LOW),
            pltpu.SemaphoreType.DMA,
            pltpu.VMEM((8, 16, 128), LOW),
            pltpu.SemaphoreType.DMA,
            pltpu.SemaphoreType.DMA((HEADS // 2 + 1,)),
        ],
        compiler_params=kernel_params(22),
        cost_estimate=cost(12e9, 24e6),
    )(place, stream, ids.reshape(1, ROW), *hbm(pieces))


def hidden_kernel(place_ref, tokens_ref, mix_ref, valid_ref, vec_ref, bias_ref, *refs):
    pieces = refs[:6]
    mid_ref, a2_t_ref, act_ref, act_t_ref, slope_ref, sums_ref, w_out, w_fc1 = refs[6:14]
    out_sem, fc1_sem = refs[14:]
    width = tokens_ref.shape[1]
    hidden = bias_ref.shape[1]
    out_ready = load_weight(place_ref, pieces, 0, width // 2, w_out, out_sem)
    fc1_ready = load_weight(place_ref, pieces, width // 2, hidden // 2, w_fc1, fc1_sem)
    stream = tokens_ref[...].astype(WIDE)
    valid = valid_ref[...]
    out_ready.wait()
    branch = dot(mix_ref[...], w_out[...]) + vec_ref[4:5, :]
    middle = stream + branch
    mid_ref[...] = middle
    sums_ref[0:1, :] = column_sum(valid * stream * stream)
    sums_ref[1:2, :] = column_sum(valid * branch * branch)
    sums_ref[2:3, :] = column_sum(valid * middle * middle)
    sums_ref[3:8, :] = jnp.zeros((5, width), WIDE)
    normed, _ = normalize(middle)
    a2 = (normed * vec_ref[5:6, :] + vec_ref[6:7, :]).astype(LOW)
    a2_t_ref[...] = a2.T
    fc1_ready.wait()
    step = 512
    for first in range(0, hidden, step):
        lanes = slice(first, first + step)
        pre = dot(a2, w_fc1[:, lanes]) + bias_ref[:, lanes]
        square = pre * pre
        turn = jnp.tanh(GELU_SCALE * (pre + GELU_CUBE * (square * pre)))
        half = 0.5 * (1.0 + turn)
        act = (pre * half).astype(LOW)
        act_ref[:, lanes] = act
        act_t_ref[lanes, :] = act.T
        bend = (1.0 - turn * turn) * (GELU_SCALE + 3.0 * GELU_SCALE * GELU_CUBE * square)
        slope_ref[:, lanes] = (half + 0.5 * pre * bend).astype(LOW)


def hidden_layer(place, tokens, mix, valid, vec, bias, pieces):
    width, hidden = tokens.shape[1], bias.shape[1]
    return pl.pallas_call(
        hidden_kernel,
        out_shape=[
            shape((ROW, width), WIDE),
            shape((width, ROW)),
            shape((ROW, hidden)),
            shape((hidden, ROW)),
            shape((ROW, hidden)),
            shape((8, width), WIDE),
            shape((width, width)),
            shape((width, hidden)),
        ],
        in_specs=[in_smem()] + [in_vmem()] * 5 + [in_hbm()] * 6,
        out_specs=[in_vmem()] * 8,
        scratch_shapes=[
            pltpu.SemaphoreType.DMA,
            pltpu.SemaphoreType.DMA,
        ],
        compiler_params=kernel_params(22),
        cost_estimate=cost(10e9, 20e6),
    )(place, tokens, mix, valid, vec, bias, *hbm(pieces))


def hidden_back_kernel(place_ref, cot_ref, slope_ref, *refs):
    pieces = refs[:6]
    d_pre_ref, shift_ref, w_fc2, sem = refs[6:]
    hidden = slope_ref.shape[1]
    loading = load_weight(place_ref, pieces, 0, w_fc2.shape[1] // 2, w_fc2, sem)
    cot = cot_ref[...]
    loading.wait()
    step = 512
    for first in range(0, hidden, step):
        lanes = slice(first, first + step)
        d_pre = dot_t(cot, w_fc2[lanes, :]) * slope_ref[:, lanes].astype(WIDE)
        shift_ref[:, lanes] = column_sum(d_pre)
        d_pre_ref[:, lanes] = d_pre.astype(LOW)


def hidden_back(place, cot, slope, pieces):
    width, hidden = cot.shape[1], slope.shape[1]
    return pl.pallas_call(
        hidden_back_kernel,
        out_shape=[shape((ROW, hidden)), shape((1, hidden), WIDE), shape((hidden, width))],
        in_specs=[in_smem()] + [in_vmem()] * 2 + [in_hbm()] * 6,
        out_specs=[in_vmem()] * 3,
        scratch_shapes=[pltpu.SemaphoreType.DMA],
        compiler_params=kernel_params(18),
        cost_estimate=cost(3e9, 14e6),
    )(place, cot, slope, *hbm(pieces))


def middle_kernel(mid_ref, act_ref, d_pre_ref, cot_ref, valid_ref, vec_ref, *refs):
    w_out, w_fc1, w_fc2 = refs[:3]
    layer_ref, d_mid_ref, d_mid_low_ref, d_mix_ref, sums_ref = refs[3:]
    middle = mid_ref[...]
    valid = valid_ref[...]
    mlp = dot(act_ref[...], w_fc2[...]) + vec_ref[7:8, :]
    result = middle + mlp
    layer_ref[...] = result.astype(LOW)
    sums_ref[4:5, :] = column_sum(valid * mlp * mlp)
    sums_ref[5:6, :] = column_sum(valid * result * result)
    sums_ref[6:8, :] = jnp.zeros((2, mid_ref.shape[1]), WIDE)
    d_a2 = dot_t(d_pre_ref[...], w_fc1[...])
    normed, scale = normalize(middle)
    dy = cot_ref[...].astype(WIDE)
    d_mid = dy + normalize_back(d_a2 * vec_ref[5:6, :], normed, scale)
    d_mid_ref[...] = d_mid
    low = d_mid.astype(LOW)
    d_mid_low_ref[...] = low
    sums_ref[0:1, :] = column_sum(d_mid)
    sums_ref[1:2, :] = column_sum(d_a2 * normed)
    sums_ref[2:3, :] = column_sum(d_a2)
    sums_ref[3:4, :] = column_sum(dy)
    d_mix_ref[...] = dot_t(low, w_out[...]).astype(LOW)


def middle_layer(mid, act, d_pre, cot, valid, vec, w_out, w_fc1, w_fc2):
    width = mid.shape[1]
    return pl.pallas_call(
        middle_kernel,
        out_shape=[
            shape((ROW, width)),
            shape((ROW, width), WIDE),
            shape((ROW, width)),
            shape((ROW, width)),
            shape((8, width), WIDE),
        ],
        in_specs=[in_vmem()] * 9,
        out_specs=[in_vmem()] * 5,
        compiler_params=kernel_params(20),
        cost_estimate=cost(14e9, 30e6),
    )(mid, act, d_pre, cot, valid, vec, w_out, w_fc1, w_fc2)


def attention_back_kernel(qkv_ref, mix_t_ref, d_mix_ref, prob_in, d_proj_ref, sums_ref, *rest):
    k_t, d_mix_t, d_q_t, prob, sem = rest
    width = mix_t_ref.shape[0]
    pairs = width // 128

    def in_copy(pair):
        heads = pl.ds(2 * pair, 2)
        return pltpu.make_async_copy(prob_in.at[heads], prob.at[heads], sem.at[pair])

    @pl.loop(0, pairs)
    def _(pair):
        in_copy(pair).start()


    k_t[...] = qkv_ref[:, width : 2 * width].T
    d_mix_t[...] = d_mix_ref[...].T
    left = lax.broadcasted_iota(jnp.int32, (ROW, 128), 1) < HEAD_DIM

    @pl.loop(0, pairs, unroll=2)
    def _(pair):
        lane = pl.multiple_of(pair * 128, 128)
        queries = qkv_ref[:, pl.ds(lane, 128)]
        values = qkv_ref[:, pl.ds(2 * width + lane, 128)]
        d_mix = d_mix_ref[:, pl.ds(lane, 128)]
        in_copy(pair).wait()
        d_keys, d_values = [], []
        for half in range(2):
            rows = pl.ds(pl.multiple_of(lane + half * HEAD_DIM, HEAD_DIM), HEAD_DIM)
            inner = column_sum(mix_t_ref[rows, :].astype(WIDE) * d_mix_t[rows, :].astype(WIDE))
            value_half = jnp.where(left == (half == 0), values, jnp.zeros_like(values))
            low = prob[2 * pair + half]
            d_prob = dot_t(value_half, d_mix)
            d_score = (low.astype(WIDE) * (d_prob - inner)).astype(LOW)
            d_keys.append(dot(d_score, queries))
            d_values.append(dot(low, d_mix))
            d_q_t[rows, :] = dot(k_t[rows, :], d_score)
        d_k = jnp.where(left, d_keys[0], d_keys[1]) * HEAD_DIM**-0.5
        d_v = jnp.where(left, d_values[0], d_values[1])
        d_proj_ref[:, pl.ds(width + lane, 128)] = d_k.astype(LOW)
        d_proj_ref[:, pl.ds(2 * width + lane, 128)] = d_v.astype(LOW)
        sums_ref[1:2, pl.ds(lane, 128)] = column_sum(d_v)

    d_q = d_q_t[...].T * HEAD_DIM**-0.5
    d_proj_ref[:, :width] = d_q.astype(LOW)
    sums_ref[0:1, :] = column_sum(d_q)
    sums_ref[2:8, :] = jnp.zeros((6, width), WIDE)


def attention_back(qkv, mix_t, d_mix, prob):
    width = mix_t.shape[0]
    heads = prob.shape[0]
    return pl.pallas_call(
        attention_back_kernel,
        out_shape=[shape((ROW, 3 * width)), shape((8, width), WIDE)],
        in_specs=[in_vmem()] * 3 + [in_hbm()],
        out_specs=[in_vmem()] * 2,
        scratch_shapes=[
            pltpu.VMEM((width, ROW), LOW),
            pltpu.VMEM((width, ROW), LOW),
            pltpu.VMEM((width, ROW), WIDE),
            pltpu.VMEM((heads, ROW, ROW), LOW),
            pltpu.SemaphoreType.DMA((heads // 2,)),
        ],
        compiler_params=kernel_params(20),
        cost_estimate=cost(1.2e9 * heads, 2e6 * heads),
    )(qkv, mix_t, d_mix, *hbm([prob]))


def first_norm_kernel(place_ref, tokens_ref, d_proj_ref, d_mid_ref, vec_ref, *refs):
    valid_ref, in_ref, mid_ref, att_ref, shift_ref = refs[:5]
    pieces = refs[5:11]
    grad_ref, sums_ref, weight, sem = refs[11:]
    width = tokens_ref.shape[1]
    loading = load_weight(place_ref, pieces, 0, weight.shape[1] // 2, weight, sem)
    sums_ref[2:4, :] = att_ref[0:2, :]
    sums_ref[4:8, :] = mid_ref[0:4, :]
    sums_ref[8:11, :] = in_ref[0:3, :]
    sums_ref[11:13, :] = mid_ref[4:6, :]
    sums_ref[13:14, :] = jnp.sum(valid_ref[...]) * jnp.ones((1, width), WIDE)
    for row in range(shift_ref.shape[1] // width):
        sums_ref[14 + row : 15 + row, :] = shift_ref[:, row * width : (row + 1) * width]
    normed, scale = normalize(tokens_ref[...].astype(WIDE))
    loading.wait()
    d_a1 = dot_t(d_proj_ref[...], weight[...])
    d_in = normalize_back(d_a1 * vec_ref[0:1, :], normed, scale)
    grad_ref[...] = (d_mid_ref[...] + d_in).astype(LOW)
    sums_ref[0:1, :] = column_sum(d_a1 * normed)
    sums_ref[1:2, :] = column_sum(d_a1)


def first_norm_back(place, tokens, d_proj, d_mid, vec, valid, sums, pieces):
    width = tokens.shape[1]
    rows = 14 + sums[-1].shape[1] // width
    return pl.pallas_call(
        first_norm_kernel,
        out_shape=[shape((ROW, width)), shape((rows, width), WIDE)],
        in_specs=[in_smem()] + [in_vmem()] * 9 + [in_hbm()] * 6,
        out_specs=[in_vmem()] * 2,
        scratch_shapes=[pltpu.VMEM((width, d_proj.shape[1]), LOW), pltpu.SemaphoreType.DMA],
        compiler_params=kernel_params(16),
        cost_estimate=pl.CostEstimate(flops=4_000_000_000, bytes_accessed=1, transcendentals=0),
    )(place, tokens, d_proj, d_mid, vec, valid, *sums, *hbm(pieces))


def product_half(left_refs, right_ref, which, sums, first):
    half = right_ref.shape[1] // 2
    row = 0
    for left_ref in left_refs:
        count = left_ref.shape[0]
        for start in range(0, half, 384):
            lane = pl.multiple_of(which * half + start, 128)
            sums[row : row + count, first + start : first + start + 384] = dot(
                left_ref[...], right_ref[:, pl.ds(lane, 384)]
            )
        row += count


def products(groups, refs, which, sums):
    first = 0
    for count in groups:
        product_half(refs[:count], refs[count], which, sums, first)
        first += refs[count].shape[1] // 2
        refs = refs[count + 1 :]


def give_kernel(groups, place_ref, *refs):
    out_ref, sums = refs[-2:]
    shard, core = place_ref[0], place_ref[1]
    products(groups, refs[:-2], 1 - core, sums)
    rows = out_ref.shape[2]
    for order in range(8):
        owner = shard ^ (2 * (order % 4) + order // 4)
        for part in range(3):
            start = pl.multiple_of((owner * 3 + part) * rows, rows)
            out_ref[order, part] = sums[pl.ds(start, rows), :].astype(LOW)


def keep_kernel(groups, place_ref, received_ref, *refs):
    give_ref, keep_ref, sums = refs[-3:]
    shard, core, plane = place_ref[0], place_ref[1], place_ref[2]
    products(groups, refs[:-3], core, sums)
    rows = give_ref.shape[1]
    for order in range(8):
        owner = shard ^ (2 * (order % 4) + order // 4)

        def total(part):
            start = pl.multiple_of((owner * 3 + part) * rows, rows)
            mine = sums[pl.ds(start, rows), :]
            return (mine + received_ref[order, part].astype(WIDE)).astype(LOW)

        give_ref[order] = total(1 - plane)
        keep_ref[0, order] = total(plane)
        keep_ref[1, order] = total(2)


class Reduction:
    def __init__(self, place, groups):
        self.place = place
        self.counts = tuple(len(group) - 1 for group in groups)
        self.operands = [entry for group in groups for entry in group]
        self.height = sum(entry.shape[0] for entry in groups[0][:-1])
        self.half = sum(group[-1].shape[1] for group in groups) // 2
        self.rows = self.height // 24
        self.scratch = [pltpu.VMEM((self.height, self.half), WIDE)]
        self.cost = cost(2 * self.height * self.half * ROW, 4 * self.height * self.half)

    def give(self):
        return pl.pallas_call(
            partial(give_kernel, self.counts),
            out_shape=shape((8, 3, self.rows, self.half)),
            in_specs=[in_smem()] + [in_vmem()] * len(self.operands),
            out_specs=in_vmem(),
            scratch_shapes=self.scratch,
            compiler_params=kernel_params(10),
            cost_estimate=self.cost,
        )(self.place, *self.operands)

    def keep(self, received):
        return pl.pallas_call(
            partial(keep_kernel, self.counts),
            out_shape=[shape((8, self.rows, self.half)), shape((2, 8, self.rows, self.half))],
            in_specs=[in_smem()] + [in_vmem()] * (1 + len(self.operands)),
            out_specs=[in_vmem()] * 2,
            scratch_shapes=self.scratch,
            compiler_params=kernel_params(12),
            cost_estimate=self.cost,
        )(self.place, received, *self.operands)

    def over_z(self, columns, name):
        return [swap(columns[step], "shard", 2 * step, name) for step in (1, 2, 3)]


def together(place, *tasks):
    counts = [(len(inputs), len(outputs)) for _, inputs, outputs in tasks]
    inputs = [entry for task in tasks for entry in task[1]]
    outputs = [entry for task in tasks for entry in task[2]]

    def kernel(place_ref, *refs):
        sources, targets = refs[: len(inputs)], refs[len(inputs) :]
        for (step, _, _), (given, made) in zip(tasks, counts):
            step(place_ref, *sources[:given], *targets[:made])
            sources, targets = sources[given:], targets[made:]

    results = pl.pallas_call(
        kernel,
        out_shape=outputs,
        in_specs=[in_smem()] + [in_vmem()] * len(inputs),
        out_specs=[in_vmem()] * len(outputs),
        compiler_params=kernel_params(16),
        cost_estimate=cost(1, 1),
    )(place, *inputs)
    groups = []
    for _, made in counts:
        groups.append(results[:made])
        results = results[made:]
    return groups


def wide(entry):
    return entry.astype(WIDE)


def stack_four(place_ref, first, second, third, fourth, stacked):
    for number, entry in enumerate((first, second, third, fourth)):
        stacked[number] = entry[...]


def to_stack(entries):
    return stack_four, tuple(entries), [shape((4,) + entries[0].shape)]


def send_y(place_ref, near, far, sent):
    rows = sent.shape[1]
    for step in range(4):
        sent[step] = near[step, 0:rows]
        sent[4 + step] = far[step, 0:rows]


def to_send_y(near, far, rows):
    return send_y, (near, far), [shape((8, rows, near.shape[2]))]


def send_x(place_ref, kept, side, sent):
    sent[0] = (wide(kept[0, 4:8]) + wide(side[4:8])).astype(LOW)
    sent[1] = kept[1, 4:8]


def to_send_x(kept, side):
    return send_x, (kept, side), [shape((2, 4) + kept.shape[2:])]


def send_z(place_ref, kept, side, column, *columns):
    for step in range(4):
        part = wide(kept[0, step]) + wide(side[step]) + wide(column[0, step])
        columns[step][0] = part.astype(LOW)
        columns[step][1] = (wide(kept[1, step]) + wide(column[1, step])).astype(LOW)


def to_send_z(kept, side, column):
    return send_z, (kept, side, column), [shape((2,) + kept.shape[2:])] * 4


def add_pieces(place_ref, first, second, third, fourth, total):
    total[...] = (wide(first[...]) + wide(second[...]) + wide(third[...]) + wide(fourth[...])).astype(LOW)


def to_add_pieces(mine, pieces):
    return add_pieces, (mine, *pieces), [shape(mine.shape)]


def join_planes(place_ref, piece, other, before, owned, squares):
    even = place_ref[2] == 0
    mine, theirs = piece[0], other[0]
    owned[0] = jnp.where(even, mine, theirs)
    owned[1] = jnp.where(even, theirs, mine)
    owned[2] = (wide(piece[1]) + wide(other[1])).astype(LOW)
    width = squares.shape[1]
    row = before[...]
    for part in range(3):
        entries = wide(owned[part])
        sums = column_sum(entries * entries)
        if sums.shape[1] < width:
            sums = jnp.concatenate([sums, jnp.zeros((1, width - sums.shape[1]), WIDE)], axis=1)
        for start in range(0, sums.shape[1], width):
            row = row + sums[:, start : start + width]
    squares[...] = row


def to_join_planes(piece, other, before):
    return join_planes, (piece, other, before), [shape((3,) + piece.shape[1:]), shape(before.shape, WIDE)]


def join_cores(bounds):
    def step(place_ref, mine, theirs, *grads):
        low = place_ref[1] == 0
        rows = mine.shape[1]
        for (start, stop), grad in zip(bounds, grads):
            half = stop - start
            for part in range(3):
                own, other = wide(mine[part, :, start:stop]), wide(theirs[part, :, start:stop])
                lines = slice(part * rows, (part + 1) * rows)
                grad[lines, :half] = jnp.where(low, own, other)
                grad[lines, half:] = jnp.where(low, other, own)

    return step


def to_join_cores(mine, theirs, *stops):
    stops = stops or (mine.shape[2],)
    bounds = list(zip((0,) + stops[:-1], stops))
    rows = 3 * mine.shape[1]
    return join_cores(bounds), (mine, theirs), [shape((rows, 2 * (b - a)), WIDE) for a, b in bounds]


def add_sums(place_ref, mine, more, total):
    total[...] = mine[...] + more[...]


def over_rest(entry, add):
    for bit in range(2, lax.axis_size("dp").bit_length() - 1):
        entry = add(entry, swap(entry, "dp", 2**bit))
    return entry


def plus(*entries):
    return sum(entry.astype(WIDE) for entry in entries).astype(LOW)


def step_of(master, grad, first, second, clip, decay):
    correction = 1.0 / (1.0 - ADAM_BETA**STEP)
    clipped = grad * clip
    first = ADAM_BETA * first + (1.0 - ADAM_BETA) * clipped
    second = ADAM_BETA * second + (1.0 - ADAM_BETA) * clipped * clipped
    second = second * correction
    root = second * lax.rsqrt(second) + ADAM_EPS
    change = first * correction * lax.rsqrt(root * root)
    return LEARN_RATE * (change + decay * master)


def update_kernel(clip_ref, *refs):
    clip = clip_ref[...]
    for grad, master, moments, new in zip(*(refs[4 * k : 4 * k + 4] for k in range(4))):
        held = master[...]
        new[...] = held - step_of(held, grad[...], moments[0], moments[1], clip, WEIGHT_DECAY)


def update(clip, grads, masters, moments):
    steps = 3
    flat = [
        pl.BlockSpec((entry.shape[0] // steps, entry.shape[1]), lambda step: (step, 0))
        for entry in masters
    ]
    pairs = [
        pl.BlockSpec((2, entry.shape[0] // steps, entry.shape[1]), lambda step: (0, step, 0))
        for entry in masters
    ]
    return pl.pallas_call(
        update_kernel,
        grid=(steps,),
        out_shape=[shape(entry.shape, WIDE) for entry in masters],
        in_specs=[pl.BlockSpec((1, 1), lambda step: (0, 0)), *flat, *flat, *pairs],
        out_specs=flat,
        compiler_params=kernel_params(24),
        cost_estimate=cost(1, 1),
    )(clip, *hbm(grads), *hbm(masters), *hbm(moments))


def finish_kernel(place_ref, mine_ref, more_ref, vectors_ref, pair_ref, shift_ref, pair2_ref, *refs):
    clip_ref, rms_ref, own_ref, own2_ref, step_ref, new_ref, held = refs
    shard = place_ref[0]
    held[...] = mine_ref[...] + more_ref[...]
    rows, width = held.shape
    entries = held[...]
    number = lax.broadcasted_iota(jnp.int32, (rows, 1), 0)
    power = jnp.where(number == rows - 1, entries, entries * entries)
    power = jnp.sum(power, axis=1, keepdims=True)
    counted = (number < 8) | (number >= 14)
    total = jnp.sum(jnp.where(counted, power, 0.0), axis=0, keepdims=True)
    clip = CLIP_NORM / jnp.maximum(jnp.sqrt(total), CLIP_NORM)
    clip_ref[...] = clip
    tokens = held[13:14, 0:1]
    means = jnp.sqrt(jnp.sum(entries, axis=1, keepdims=True) / (tokens * width))
    lane = lax.broadcasted_iota(jnp.int32, (rows, 128), 1)
    line = jnp.sum(jnp.where(number == lane + 8, means, 0.0), axis=0, keepdims=True)
    rms_ref[...] = line[0, 0:5]
    owned = own_ref.shape[1]
    grad = pltpu.roll(held[0:8, :], width - shard * owned, axis=1)[:, :owned]
    own_ref[...] = grad
    step_ref[...] = step_of(vectors_ref[...], grad, pair_ref[0], pair_ref[1], clip, 0.0)
    owned = own2_ref.shape[0]
    each = width // owned
    lanes = pl.ds(pl.multiple_of((shard % each) * owned, 128), owned)
    grad = held[pl.ds(14 + shard // each, 1), lanes]
    own2_ref[...] = grad[0]
    new = shift_ref[...] - step_of(
        shift_ref[...], grad, pair2_ref[0:1, :], pair2_ref[1:2, :], clip, 0.0
    )
    new_ref[...] = new[0]


def finish(place, mine, more, vectors, pair, shift, pair2):
    count = shift.shape[0]
    shift = shift.reshape(1, count)
    return pl.pallas_call(
        finish_kernel,
        out_shape=[
            shape((1, 1), WIDE),
            shape((5,), WIDE),
            shape(vectors.shape, WIDE),
            shape((count,), WIDE),
            shape(vectors.shape, WIDE),
            shape((count,), WIDE),
        ],
        in_specs=[in_smem()] + [in_vmem()] * 6,
        out_specs=[in_vmem()] * 6,
        scratch_shapes=[pltpu.VMEM(mine.shape, WIDE)],
        compiler_params=kernel_params(4),
        cost_estimate=cost(1, 1),
    )(place, mine, more, vectors, pair, shift, pair2)


def body(
    tokens,
    picture_ids,
    cotangent,
    w_qkv,
    w_out,
    w_fc1,
    w_fc2,
    vectors,
    fc1_bias,
    moments_qkv,
    moments_out,
    moments_fc1,
    moments_fc2,
    moments_vectors,
    moments_fc1_bias,
):
    model_width = tokens.shape[1]
    shard = lax.axis_index("shard")
    data = lax.axis_index("dp")
    place = jnp.stack([shard, data % 2, (data // 2) % 2]).astype(jnp.int32)
    own_a, own_b, own_c = own_pieces(place, w_qkv, w_out, w_fc1, w_fc2, vectors, fc1_bias)
    near_a = jnp.stack(gather_z(own_a, "A"))
    near_a, own_b, own_c = sync(near_a, own_b, own_c)
    far_a, near2_a = gather_x(near_a, "A"), gather_core(near_a, "A")
    near_b = jnp.stack(gather_z(own_b, "B"))
    far_a, near_b, near2_a, own_c = sync(far_a, near_b, near2_a, own_c)
    side_a = gather_y(near_a, far_a, "A", lanes=w_qkv.shape[1] // 2)
    far_b = gather_x(near_b, "B")
    z_c = gather_z(own_c, "C")
    side_a, far_b, z_c = sync(side_a, far_b, z_c)
    far2_a, side2_a = gather_core(far_a, "A"), gather_core(side_a, "A")
    (near_c,), (sent,) = together(
        place, to_stack(z_c), to_send_y(near_b, far_b, w_out.shape[0] // 3)
    )
    pieces_a = (near_a, far_a, side_a, near2_a, far2_a, side2_a)
    side_b, near2_b = swap(sent, "dp", 2, "B"), gather_core(near_b, "B")
    far_c = gather_x(near_c, "C")
    far2_b = gather_core(after(far_b, side2_a), "B")
    vec, bias, valid, a1_t, mix, mix_t, qkv, prob = attention(
        place, after(tokens, side2_a, near_c), picture_ids, w_fc1.shape[1], pieces_a
    )
    side_b, far2_b, near2_b, far_c, mix = sync(side_b, far2_b, near2_b, far_c, mix)
    side2_b, near2_c = gather_core(side_b, "B"), gather_core(near_c, "C")
    ((sent,),) = together(place, to_send_y(near_c, far_c, w_fc2.shape[0] // 3))
    side_c, far2_c = swap(sent, "dp", 2, "C"), gather_core(far_c, "C")
    pieces_b = (near_b, far_b, side_b, near2_b, far2_b, side2_b)
    mid, a2_t, act, act_t, slope, sums_in, wide_out, wide_fc1 = hidden_layer(
        place, tokens, mix, valid, vec, bias, pieces_b
    )
    fc2 = Reduction(place, [(act_t, cotangent)])
    given = fc2.give()
    side_c, far2_c, near2_c, given = sync(side_c, far2_c, near2_c, given)
    recv_f2, side2_c = gather_core(given, "F2"), gather_core(side_c, "C")
    pieces_c = (near_c, far_c, side_c, near2_c, far2_c, side2_c)
    give_f2, keep_f2 = fc2.keep(recv_f2)
    side_f2 = swap(give_f2, "dp", 2, "F2")
    d_pre, shift_sum, wide_fc2 = hidden_back(place, cotangent, after(slope, give_f2), pieces_c)
    layer_out, d_mid, d_mid_low, d_mix, sums_mid = middle_layer(
        mid, act, d_pre, cotangent, valid, vec, wide_out, wide_fc1, wide_fc2
    )
    fc1 = Reduction(place, [(a2_t, after(d_pre, d_mix))])
    given = fc1.give()
    side_f2, given, d_mix = sync(side_f2, given, d_mix)
    recv_f1 = gather_core(given, "F1")
    ((sent,),) = together(place, to_send_x(keep_f2, side_f2))
    column_f2 = swap(sent, "shard", 1, "F2")
    give_f1, keep_f1 = fc1.keep(after(recv_f1, sent))
    side_f1 = swap(give_f1, "dp", 2, "F1")
    d_proj, sums_att = attention_back(qkv, mix_t, after(d_mix, give_f1), prob)
    first = Reduction(place, [(a1_t, d_proj), (mix_t, d_mid_low)])
    given = first.give()
    column_f2, side_f1, given = sync(column_f2, side_f1, given)
    recv_a = gather_core(given, "RA")
    tokens_grad, small_sums = first_norm_back(
        place,
        tokens,
        d_proj,
        after(d_mid, given),
        vec,
        valid,
        (sums_in, sums_mid, sums_att, shift_sum),
        pieces_a,
    )
    recv_a, small_sums = sync(recv_a, small_sums)
    give_a, keep_a = first.keep(recv_a)
    columns_f2, (sent,) = together(
        place,
        to_send_z(keep_f2, side_f2, after(column_f2, give_a)),
        to_send_x(keep_f1, side_f1),
    )
    pieces_f2 = fc2.over_z(columns_f2, "F2")
    column_f1 = swap(sent, "shard", 1, "F1")
    side_ra = swap(give_a, "dp", 2, "RA")
    side_ra, column_f1, pieces_f2 = sync(side_ra, column_f1, pieces_f2)
    (sent,), columns_f1, (piece_f2,) = together(
        place,
        to_send_x(keep_a, side_ra),
        to_send_z(keep_f1, side_f1, column_f1),
        to_add_pieces(columns_f2[0], pieces_f2),
    )
    piece_f2 = over_rest(piece_f2, plus)
    other_f2 = swap(piece_f2, "dp", 2, "F2")
    pieces_f1 = fc1.over_z(columns_f1, "F1")
    column_a = swap(sent, "shard", 1, "RA")
    column_a, pieces_f1, other_f2 = sync(column_a, pieces_f1, other_f2)
    columns_a, (piece_f1,), (owned_f2, squares) = together(
        place,
        to_send_z(keep_a, side_ra, column_a),
        to_add_pieces(columns_f1[0], pieces_f1),
        to_join_planes(piece_f2, other_f2, jnp.zeros((1, model_width), WIDE)),
    )
    theirs_f2 = gather_core(owned_f2, "F2")
    piece_f1 = over_rest(piece_f1, plus)
    other_f1 = swap(piece_f1, "dp", 2, "F1")
    pieces_ra = first.over_z(columns_a, "RA")
    pieces_ra, other_f1, theirs_f2 = sync(pieces_ra, other_f1, theirs_f2)
    (piece_a,), (owned_f1, squares) = together(
        place,
        to_add_pieces(columns_a[0], pieces_ra),
        to_join_planes(piece_f1, other_f1, squares),
    )
    piece_a = over_rest(piece_a, plus)
    other_a = swap(piece_a, "dp", 2, "RA")
    small_more = swap(after(small_sums, piece_a), "dp", 2)
    theirs_f1 = gather_core(owned_f1, "F1")
    ((grad_fc2,),) = together(place, to_join_cores(owned_f2, after(theirs_f2, piece_a)))
    other_a, theirs_f1, small_more, grad_fc2 = sync(other_a, theirs_f1, small_more, grad_fc2)
    (owned_a, squares), (small_sums,) = together(
        place,
        to_join_planes(piece_a, other_a, squares),
        (add_sums, (small_sums, small_more), [shape(small_sums.shape, WIDE)]),
    )
    small_sums = over_rest(small_sums, jnp.add)
    theirs_a = gather_core(owned_a, "RA")
    small_sums = jnp.concatenate([small_sums, squares])
    small_more = swap(small_sums, "dp", 1)
    ((grad_fc1,),) = together(place, to_join_cores(owned_f1, after(theirs_f1, small_sums)))
    theirs_a, small_more, grad_fc1 = sync(theirs_a, small_more, grad_fc1)
    small_sums = small_sums + small_more
    small_more = swap(small_sums, "shard", 1)
    ((grad_qkv, grad_out),) = together(
        place,
        to_join_cores(owned_a, after(theirs_a, small_sums), w_qkv.shape[1] // 2, owned_a.shape[2]),
    )
    small_more, grad_qkv = sync(small_more, grad_qkv)
    small_sums = small_sums + small_more
    small_sums = small_sums + swap(small_sums, "shard", 2)
    small_more = swap(small_sums, "shard", 4)
    clip, stream_rms, own_vectors, own_shift, vector_step, new_shift = finish(
        place, small_sums, small_more, vectors, moments_vectors, fc1_bias, moments_fc1_bias
    )
    grads = (grad_qkv, grad_out, grad_fc1, grad_fc2)
    updated = update(
        clip,
        grads,
        (w_qkv, w_out, w_fc1, w_fc2),
        (moments_qkv, moments_out, moments_fc1, moments_fc2),
    )
    owner_grads = (*grads, own_vectors, own_shift)
    updated = (*updated, vector_step, new_shift)
    return (layer_out, tokens_grad, *owner_grads, *updated, stream_rms)


def solution(mesh):
    placed = (
        P(("dp", "shard"), None),
        P(("dp", "shard")),
        P(("dp", "shard"), None),
        P("shard", None),
        P("shard", None),
        P("shard", None),
        P("shard", None),
        P(None, "shard"),
        P("shard"),
        P(None, "shard", None),
        P(None, "shard", None),
        P(None, "shard", None),
        P(None, "shard", None),
        P(None, None, "shard"),
        P(None, "shard"),
    )
    return jax.shard_map(
        body,
        mesh=mesh,
        in_specs=placed,
        out_specs=(
            P(("dp", "shard"), None),
            P(("dp", "shard"), None),
            P("shard", None),
            P("shard", None),
            P("shard", None),
            P("shard", None),
            P(None, "shard"),
            P("shard"),
            P("shard", None),
            P("shard", None),
            P("shard", None),
            P("shard", None),
            P(None, "shard"),
            P("shard"),
            P(),
        ),
        check_vma=False,
    )
```

```python
from functools import partial

import jax
import jax.numpy as jnp
from jax import lax
from jax.experimental import pallas as pl
from jax.experimental.pallas import tpu as pltpu
from jax.sharding import PartitionSpec as P

HEADS = 12
HEAD_DIM = 64
ROW = 512
STEP = 2

NORM_EPS = 1e-06
ADAM_BETA = 0.5
LEARN_RATE = 0.03
WEIGHT_DECAY = 0.1
ADAM_EPS = 1e-08
CLIP_NORM = 1.0
MASKED = -1e30
GELU_SCALE = 0.7978845608028654
GELU_CUBE = 0.044715

LOW = jnp.bfloat16
WIDE = jnp.float32


def swap(entry, axis, mask, name="sums"):
    count = lax.axis_size(axis)
    with jax.named_scope(name + "_" + axis + str(mask)):
        return lax.ppermute(entry, axis, [(place, place ^ mask) for place in range(count)])


def in_vmem():
    return pl.BlockSpec(memory_space=pltpu.VMEM)


def in_hbm():
    return pl.BlockSpec(memory_space=pltpu.HBM)


def hbm(entries):
    return [pltpu.with_memory_space_constraint(entry, pltpu.HBM) for entry in entries]


def in_smem():
    return pl.BlockSpec(memory_space=pltpu.SMEM)


def shape(dims, kind=LOW):
    return jax.ShapeDtypeStruct(dims, kind)


def cost(flops, moved):
    return pl.CostEstimate(flops=1, bytes_accessed=1, transcendentals=0)


def kernel_params(mib):
    return pltpu.CompilerParams(vmem_limit_bytes=mib * 2**20)


def dot(left, right):
    return jnp.dot(left, right, preferred_element_type=WIDE)


def dot_t(left, right):
    return lax.dot_general(left, right, (((1,), (1,)), ((), ())), preferred_element_type=WIDE)


def normalize(entries):
    center = entries - jnp.mean(entries, axis=-1, keepdims=True)
    scale = lax.rsqrt(jnp.mean(center * center, axis=-1, keepdims=True) + NORM_EPS)
    return center * scale, scale


def normalize_back(grad, normed, scale):
    inner = jnp.mean(grad * normed, axis=-1, keepdims=True)
    return scale * (grad - jnp.mean(grad, axis=-1, keepdims=True) - normed * inner)


def column_sum(entries):
    return jnp.sum(entries, axis=0, keepdims=True)


def own_pieces_kernel(place_ref, *refs):
    sources, vectors_in, shift_in = refs[:4], refs[4], refs[5]
    qkv_ref, mid_ref, fc2_ref = refs[6:9]
    scratch, vectors_ref, shift_ref, sem = refs[9:13], refs[13], refs[14], refs[15]
    core, plane = place_ref[1], place_ref[2]
    copies = []
    for number, (source, held) in enumerate(zip(sources, scratch)):
        rows, lanes = held.shape
        column = pl.multiple_of(core * lanes, 128)
        size = rows // (1, 2, 2, 3)[number]
        spans = [(plane * size, 0, size)]
        if number > 0:
            spans.append((2 * size, size, rows - size))
        for start, at, length in spans:
            copies.append(
                pltpu.make_async_copy(
                    source.at[pl.ds(pl.multiple_of(start, size), length), pl.ds(column, lanes)],
                    held.at[pl.ds(at, length)],
                    sem.at[len(copies)],
                )
            )
    copies.append(pltpu.make_async_copy(vectors_in, vectors_ref, sem.at[len(copies)]))
    copies.append(pltpu.make_async_copy(shift_in, shift_ref, sem.at[len(copies)]))
    for copy in copies:
        copy.start()
    qkv, out, fc1, fc2 = scratch
    width = qkv.shape[1]
    qkv_ref[:, width:] = jnp.zeros((qkv.shape[0], 128), LOW)
    for copy in copies:
        copy.wait()
    qkv_ref[0:8, width : width + vectors_ref.shape[1]] = vectors_ref[...].astype(LOW)
    qkv_ref[8 : 8 + shift_ref.shape[0], width:] = shift_ref[...].astype(LOW)
    qkv_ref[:, :width] = qkv[...].astype(LOW)
    width = out.shape[1]
    mid_ref[:, :width] = out[...].astype(LOW)
    mid_ref[:, width:] = fc1[...].astype(LOW)
    fc2_ref[...] = fc2[...].astype(LOW)


def own_pieces(place, w_qkv, w_out, w_fc1, w_fc2, vectors, fc1_bias):
    shift = fc1_bias.reshape(-1, 128)
    weights = (w_qkv, w_out, w_fc1, w_fc2)
    dims = [
        (entry.shape[0] * share // 12, entry.shape[1] // 2)
        for share, entry in zip((6, 8, 8, 9), weights)
    ]
    return pl.pallas_call(
        own_pieces_kernel,
        out_shape=[
            shape((dims[0][0], dims[0][1] + 128)),
            shape((dims[1][0], dims[1][1] + dims[2][1])),
            shape(dims[3]),
        ],
        in_specs=[in_smem()] + [in_hbm()] * 6,
        out_specs=[in_vmem()] * 3,
        scratch_shapes=[pltpu.VMEM(entry, WIDE) for entry in (*dims, vectors.shape, shift.shape)]
        + [pltpu.SemaphoreType.DMA((9,))],
        compiler_params=kernel_params(8),
    )(place, *hbm((*weights, vectors, shift)))


def after(entry, *others):
    return sync(entry, *others)[0]


def sync(*entries):
    leaves, tree = jax.tree.flatten(entries)
    return jax.tree.unflatten(tree, lax.optimization_barrier(leaves))


def gather_z(own, name):
    return [own] + [swap(own, "shard", mask, name) for mask in (2, 4, 6)]


def gather_x(near, name):
    return swap(near, "shard", 1, name)


def gather_y(near, far, name, rows=None, lanes=None):
    return swap(jnp.concatenate([near[:, :rows, :lanes], far[:, :rows, :lanes]]), "dp", 2, name)


def gather_core(entry, name):
    return swap(entry, "dp", 1, name)


def load_weight(place_ref, pieces, first, width, full, sem):
    shard, core, plane = place_ref[0], place_ref[1], place_ref[2]
    lanes = pl.ds(first, width)
    count = len(pieces) // 2
    owned = full.shape[0] // 8
    rows = pieces[2].shape[1] if count == 3 else owned
    shared = pieces[0].shape[1] - rows

    def put(source, owner, start, which):
        row = pl.multiple_of(owner * owned + start, 16)
        column = pl.multiple_of(which * width, 128)
        target = full.at[pl.ds(row, source.shape[0]), pl.ds(column, width)]
        pltpu.make_async_copy(source, target, sem).start()

    for which, half in ((core, pieces[:count]), (1 - core, pieces[count:])):
        for flip in range(2):
            for step in range(4):
                owner = shard ^ (2 * step + flip)
                ref = half[flip].at[step]
                put(ref.at[pl.ds(0, rows), lanes], owner, plane * rows if count == 3 else 0, which)
                if shared:
                    put(ref.at[pl.ds(rows, shared), lanes], owner, 2 * rows, which)
                if count == 3:
                    side = half[2].at[4 * flip + step, :, lanes]
                    put(side, owner, (1 - plane) * rows, which)
    return pltpu.make_async_copy(full, full, sem)


def gather_vectors(place_ref, near, far, held, sem, vec_ref, shift_ref):
    lane = near.shape[2] - 128
    owned = vec_ref.shape[1] // 8
    for flip, ref in ((0, near), (1, far)):
        for step in range(4):
            source = ref.at[step, pl.ds(0, 16), pl.ds(lane, 128)]
            pltpu.make_async_copy(source, held.at[4 * flip + step], sem).start()
    pltpu.make_async_copy(held, held, sem).wait()
    source = lax.broadcasted_iota(jnp.int32, (128, vec_ref.shape[1]), 0)
    target = lax.broadcasted_iota(jnp.int32, (128, vec_ref.shape[1]), 1)
    rows = jnp.zeros((16, vec_ref.shape[1]), WIDE)
    count = shift_ref.shape[1] // (8 * 128)
    for order in range(8):
        owner = place_ref[0] ^ (2 * (order % 4) + order // 4)
        move = (target == source + owner * owned) & (source < owned)
        rows = rows + dot(held[order], move.astype(WIDE).astype(LOW))
        for row in range(count):
            start = pl.multiple_of((owner * count + row) * 128, 128)
            shift_ref[0:1, pl.ds(start, 128)] = held[order, 8 + row : 9 + row, :].astype(WIDE)
    vec_ref[...] = rows[0:8]


def attention_kernel(place_ref, stream_ref, ids_ref, *refs):
    pieces = refs[:6]
    vec_ref, shift_ref, valid_ref, a1_t_ref, mix_ref, mix_t_ref, qkv_out, prob_out = refs[6:14]
    weight, qkv_ref, prob, bias, v_t, weight_sem, vec_held, vec_sem, out_sem = refs[14:]
    width = mix_ref.shape[1]
    pairs = width // 128
    loading = load_weight(place_ref, pieces, 0, weight.shape[1] // 2, weight, weight_sem)
    gather_vectors(place_ref, *pieces[:2], vec_held, vec_sem, vec_ref, shift_ref)
    normed, _ = normalize(stream_ref[...].astype(WIDE))
    a1 = (normed * vec_ref[0:1, :] + vec_ref[1:2, :]).astype(LOW)
    a1_t_ref[...] = a1.T
    ids = ids_ref[...].astype(WIDE)
    column = jnp.broadcast_to(ids, (128, ROW)).T[:, 0:1]
    bias[...] = jnp.where(column == ids, 0.0, MASKED)
    valid_ref[...] = jnp.where(column == 0.0, 0.0, 1.0)
    loading.wait()
    queries = dot(a1, weight[:, :width]) + vec_ref[2:3, :]
    qkv_ref[:, :width] = queries.astype(LOW)
    qkv_ref[:, width : 2 * width] = dot(a1, weight[:, width : 2 * width]).astype(LOW)
    values = (dot(a1, weight[:, 2 * width :]) + vec_ref[3:4, :]).astype(LOW)
    qkv_ref[:, 2 * width :] = values
    qkv_copy = pltpu.make_async_copy(qkv_ref, qkv_out, out_sem.at[pairs])
    qkv_copy.start()
    v_t[...] = values.T

    def out_copy(pair):
        heads = pl.ds(2 * pair, 2)
        return pltpu.make_async_copy(prob.at[heads], prob_out.at[heads], out_sem.at[pair])

    left = lax.broadcasted_iota(jnp.int32, (ROW, 128), 1) < HEAD_DIM

    @pl.loop(0, pairs, unroll=2)
    def _(pair):
        lane = pl.multiple_of(pair * 128, 128)
        scaled = qkv_ref[:, pl.ds(lane, 128)] * HEAD_DIM**-0.5
        keys = qkv_ref[:, pl.ds(width + lane, 128)]
        blank = jnp.zeros_like(keys)
        halves = jnp.concatenate([jnp.where(left, keys, blank), jnp.where(left, blank, keys)])
        scores = dot_t(halves, scaled)
        for half in range(2):
            v_rows = pl.ds(pl.multiple_of(lane + half * HEAD_DIM, HEAD_DIM), HEAD_DIM)
            head = scores[half * ROW : (half + 1) * ROW] + bias[...]
            weights = jnp.exp(head - jnp.max(head, axis=0, keepdims=True))
            weights = weights * (1.0 / jnp.sum(weights, axis=0, keepdims=True))
            low = weights.astype(LOW)
            prob[2 * pair + half] = low
            mix_t_ref[v_rows, :] = dot(v_t[v_rows, :], low).astype(LOW)
        out_copy(pair).start()

    mix_ref[...] = mix_t_ref[...].T
    qkv_copy.wait()

    @pl.loop(0, pairs)
    def _(pair):
        out_copy(pair).wait()


def attention(place, stream, ids, hidden, pieces):
    width = stream.shape[1]
    return pl.pallas_call(
        attention_kernel,
        out_shape=[
            shape((8, width), WIDE),
            shape((1, hidden), WIDE),
            shape((ROW, 1), WIDE),
            shape((width, ROW)),
            shape((ROW, width)),
            shape((width, ROW)),
            pltpu.HBM((ROW, 3 * width), LOW),
            pltpu.HBM((HEADS, ROW, ROW), LOW),
        ],
        in_specs=[in_smem()] + [in_vmem()] * 2 + [in_hbm()] * 6,
        out_specs=[in_vmem()] * 6 + [in_hbm()] * 2,
        scratch_shapes=[
            pltpu.VMEM((width, 3 * width), LOW),
            pltpu.VMEM((ROW, 3 * width), LOW),
            pltpu.VMEM((HEADS, ROW, ROW), LOW),
            pltpu.VMEM((ROW, ROW), WIDE),
            pltpu.VMEM((width, ROW), LOW),
            pltpu.SemaphoreType.DMA,
            pltpu.VMEM((8, 16, 128), LOW),
            pltpu.SemaphoreType.DMA,
            pltpu.SemaphoreType.DMA((HEADS // 2 + 1,)),
        ],
        compiler_params=kernel_params(22),
        cost_estimate=cost(12e9, 24e6),
    )(place, stream, ids.reshape(1, ROW), *hbm(pieces))


def hidden_kernel(place_ref, tokens_ref, mix_ref, valid_ref, vec_ref, bias_ref, *refs):
    pieces = refs[:6]
    mid_ref, a2_t_ref, act_ref, act_t_ref, slope_ref, sums_ref, w_out, w_fc1 = refs[6:14]
    out_sem, fc1_sem = refs[14:]
    width = tokens_ref.shape[1]
    hidden = bias_ref.shape[1]
    out_ready = load_weight(place_ref, pieces, 0, width // 2, w_out, out_sem)
    fc1_ready = load_weight(place_ref, pieces, width // 2, hidden // 2, w_fc1, fc1_sem)
    stream = tokens_ref[...].astype(WIDE)
    valid = valid_ref[...]
    out_ready.wait()
    branch = dot(mix_ref[...], w_out[...]) + vec_ref[4:5, :]
    middle = stream + branch
    mid_ref[...] = middle
    sums_ref[0:1, :] = column_sum(valid * stream * stream)
    sums_ref[1:2, :] = column_sum(valid * branch * branch)
    sums_ref[2:3, :] = column_sum(valid * middle * middle)
    sums_ref[3:8, :] = jnp.zeros((5, width), WIDE)
    normed, _ = normalize(middle)
    a2 = (normed * vec_ref[5:6, :] + vec_ref[6:7, :]).astype(LOW)
    a2_t_ref[...] = a2.T
    fc1_ready.wait()
    step = 512
    for first in range(0, hidden, step):
        lanes = slice(first, first + step)
        pre = dot(a2, w_fc1[:, lanes]) + bias_ref[:, lanes]
        square = pre * pre
        turn = jnp.tanh(GELU_SCALE * (pre + GELU_CUBE * (square * pre)))
        half = 0.5 * (1.0 + turn)
        act = (pre * half).astype(LOW)
        act_ref[:, lanes] = act
        act_t_ref[lanes, :] = act.T
        bend = (1.0 - turn * turn) * (GELU_SCALE + 3.0 * GELU_SCALE * GELU_CUBE * square)
        slope_ref[:, lanes] = (half + 0.5 * pre * bend).astype(LOW)


def hidden_layer(place, tokens, mix, valid, vec, bias, pieces):
    width, hidden = tokens.shape[1], bias.shape[1]
    return pl.pallas_call(
        hidden_kernel,
        out_shape=[
            shape((ROW, width), WIDE),
            shape((width, ROW)),
            shape((ROW, hidden)),
            shape((hidden, ROW)),
            shape((ROW, hidden)),
            shape((8, width), WIDE),
            shape((width, width)),
            shape((width, hidden)),
        ],
        in_specs=[in_smem()] + [in_vmem()] * 5 + [in_hbm()] * 6,
        out_specs=[in_vmem()] * 8,
        scratch_shapes=[
            pltpu.SemaphoreType.DMA,
            pltpu.SemaphoreType.DMA,
        ],
        compiler_params=kernel_params(22),
        cost_estimate=cost(10e9, 20e6),
    )(place, tokens, mix, valid, vec, bias, *hbm(pieces))


def hidden_back_kernel(place_ref, cot_ref, slope_ref, *refs):
    pieces = refs[:6]
    d_pre_ref, shift_ref, w_fc2, sem = refs[6:]
    hidden = slope_ref.shape[1]
    loading = load_weight(place_ref, pieces, 0, w_fc2.shape[1] // 2, w_fc2, sem)
    cot = cot_ref[...]
    loading.wait()
    step = 512
    for first in range(0, hidden, step):
        lanes = slice(first, first + step)
        d_pre = dot_t(cot, w_fc2[lanes, :]) * slope_ref[:, lanes].astype(WIDE)
        shift_ref[:, lanes] = column_sum(d_pre)
        d_pre_ref[:, lanes] = d_pre.astype(LOW)


def hidden_back(place, cot, slope, pieces):
    width, hidden = cot.shape[1], slope.shape[1]
    return pl.pallas_call(
        hidden_back_kernel,
        out_shape=[shape((ROW, hidden)), shape((1, hidden), WIDE), shape((hidden, width))],
        in_specs=[in_smem()] + [in_vmem()] * 2 + [in_hbm()] * 6,
        out_specs=[in_vmem()] * 3,
        scratch_shapes=[pltpu.SemaphoreType.DMA],
        compiler_params=kernel_params(18),
        cost_estimate=cost(3e9, 14e6),
    )(place, cot, slope, *hbm(pieces))


def middle_kernel(mid_ref, act_ref, d_pre_ref, cot_ref, valid_ref, vec_ref, *refs):
    w_out, w_fc1, w_fc2 = refs[:3]
    layer_ref, d_mid_ref, d_mid_low_ref, d_mix_ref, sums_ref = refs[3:]
    middle = mid_ref[...]
    valid = valid_ref[...]
    mlp = dot(act_ref[...], w_fc2[...]) + vec_ref[7:8, :]
    result = middle + mlp
    layer_ref[...] = result.astype(LOW)
    sums_ref[4:5, :] = column_sum(valid * mlp * mlp)
    sums_ref[5:6, :] = column_sum(valid * result * result)
    sums_ref[6:8, :] = jnp.zeros((2, mid_ref.shape[1]), WIDE)
    d_a2 = dot_t(d_pre_ref[...], w_fc1[...])
    normed, scale = normalize(middle)
    dy = cot_ref[...].astype(WIDE)
    d_mid = dy + normalize_back(d_a2 * vec_ref[5:6, :], normed, scale)
    d_mid_ref[...] = d_mid
    low = d_mid.astype(LOW)
    d_mid_low_ref[...] = low
    sums_ref[0:1, :] = column_sum(d_mid)
    sums_ref[1:2, :] = column_sum(d_a2 * normed)
    sums_ref[2:3, :] = column_sum(d_a2)
    sums_ref[3:4, :] = column_sum(dy)
    d_mix_ref[...] = dot_t(low, w_out[...]).astype(LOW)


def middle_layer(mid, act, d_pre, cot, valid, vec, w_out, w_fc1, w_fc2):
    width = mid.shape[1]
    return pl.pallas_call(
        middle_kernel,
        out_shape=[
            shape((ROW, width)),
            shape((ROW, width), WIDE),
            shape((ROW, width)),
            shape((ROW, width)),
            shape((8, width), WIDE),
        ],
        in_specs=[in_vmem()] * 9,
        out_specs=[in_vmem()] * 5,
        compiler_params=kernel_params(20),
        cost_estimate=cost(14e9, 30e6),
    )(mid, act, d_pre, cot, valid, vec, w_out, w_fc1, w_fc2)


def attention_back_kernel(qkv_ref, mix_t_ref, d_mix_ref, prob_in, d_proj_ref, sums_ref, *rest):
    k_t, d_mix_t, d_q_t, prob, sem = rest
    width = mix_t_ref.shape[0]
    pairs = width // 128

    def in_copy(pair):
        heads = pl.ds(2 * pair, 2)
        return pltpu.make_async_copy(prob_in.at[heads], prob.at[heads], sem.at[pair])

    @pl.loop(0, pairs)
    def _(pair):
        in_copy(pair).start()


    k_t[...] = qkv_ref[:, width : 2 * width].T
    d_mix_t[...] = d_mix_ref[...].T
    left = lax.broadcasted_iota(jnp.int32, (ROW, 128), 1) < HEAD_DIM

    @pl.loop(0, pairs, unroll=2)
    def _(pair):
        lane = pl.multiple_of(pair * 128, 128)
        queries = qkv_ref[:, pl.ds(lane, 128)]
        values = qkv_ref[:, pl.ds(2 * width + lane, 128)]
        d_mix = d_mix_ref[:, pl.ds(lane, 128)]
        in_copy(pair).wait()
        d_keys, d_values = [], []
        for half in range(2):
            rows = pl.ds(pl.multiple_of(lane + half * HEAD_DIM, HEAD_DIM), HEAD_DIM)
            inner = column_sum(mix_t_ref[rows, :].astype(WIDE) * d_mix_t[rows, :].astype(WIDE))
            value_half = jnp.where(left == (half == 0), values, jnp.zeros_like(values))
            low = prob[2 * pair + half]
            d_prob = dot_t(value_half, d_mix)
            d_score = (low.astype(WIDE) * (d_prob - inner)).astype(LOW)
            d_keys.append(dot(d_score, queries))
            d_values.append(dot(low, d_mix))
            d_q_t[rows, :] = dot(k_t[rows, :], d_score)
        d_k = jnp.where(left, d_keys[0], d_keys[1]) * HEAD_DIM**-0.5
        d_v = jnp.where(left, d_values[0], d_values[1])
        d_proj_ref[:, pl.ds(width + lane, 128)] = d_k.astype(LOW)
        d_proj_ref[:, pl.ds(2 * width + lane, 128)] = d_v.astype(LOW)
        sums_ref[1:2, pl.ds(lane, 128)] = column_sum(d_v)

    d_q = d_q_t[...].T * HEAD_DIM**-0.5
    d_proj_ref[:, :width] = d_q.astype(LOW)
    sums_ref[0:1, :] = column_sum(d_q)
    sums_ref[2:8, :] = jnp.zeros((6, width), WIDE)


def attention_back(qkv, mix_t, d_mix, prob):
    width = mix_t.shape[0]
    heads = prob.shape[0]
    return pl.pallas_call(
        attention_back_kernel,
        out_shape=[shape((ROW, 3 * width)), shape((8, width), WIDE)],
        in_specs=[in_vmem()] * 3 + [in_hbm()],
        out_specs=[in_vmem()] * 2,
        scratch_shapes=[
            pltpu.VMEM((width, ROW), LOW),
            pltpu.VMEM((width, ROW), LOW),
            pltpu.VMEM((width, ROW), WIDE),
            pltpu.VMEM((heads, ROW, ROW), LOW),
            pltpu.SemaphoreType.DMA((heads // 2,)),
        ],
        compiler_params=kernel_params(20),
        cost_estimate=cost(1.2e9 * heads, 2e6 * heads),
    )(qkv, mix_t, d_mix, *hbm([prob]))


def first_norm_kernel(place_ref, tokens_ref, d_proj_ref, d_mid_ref, vec_ref, *refs):
    valid_ref, in_ref, mid_ref, att_ref, shift_ref = refs[:5]
    pieces = refs[5:11]
    grad_ref, sums_ref, weight, sem = refs[11:]
    width = tokens_ref.shape[1]
    loading = load_weight(place_ref, pieces, 0, weight.shape[1] // 2, weight, sem)
    sums_ref[2:4, :] = att_ref[0:2, :]
    sums_ref[4:8, :] = mid_ref[0:4, :]
    sums_ref[8:11, :] = in_ref[0:3, :]
    sums_ref[11:13, :] = mid_ref[4:6, :]
    sums_ref[13:14, :] = jnp.sum(valid_ref[...]) * jnp.ones((1, width), WIDE)
    for row in range(shift_ref.shape[1] // width):
        sums_ref[14 + row : 15 + row, :] = shift_ref[:, row * width : (row + 1) * width]
    normed, scale = normalize(tokens_ref[...].astype(WIDE))
    loading.wait()
    d_a1 = dot_t(d_proj_ref[...], weight[...])
    d_in = normalize_back(d_a1 * vec_ref[0:1, :], normed, scale)
    grad_ref[...] = (d_mid_ref[...] + d_in).astype(LOW)
    sums_ref[0:1, :] = column_sum(d_a1 * normed)
    sums_ref[1:2, :] = column_sum(d_a1)


def first_norm_back(place, tokens, d_proj, d_mid, vec, valid, sums, pieces):
    width = tokens.shape[1]
    rows = 14 + sums[-1].shape[1] // width
    return pl.pallas_call(
        first_norm_kernel,
        out_shape=[shape((ROW, width)), shape((rows, width), WIDE)],
        in_specs=[in_smem()] + [in_vmem()] * 9 + [in_hbm()] * 6,
        out_specs=[in_vmem()] * 2,
        scratch_shapes=[pltpu.VMEM((width, d_proj.shape[1]), LOW), pltpu.SemaphoreType.DMA],
        compiler_params=kernel_params(16),
        cost_estimate=pl.CostEstimate(flops=4_000_000_000, bytes_accessed=1, transcendentals=0),
    )(place, tokens, d_proj, d_mid, vec, valid, *sums, *hbm(pieces))


def product_half(left_refs, right_ref, which, sums, first):
    half = right_ref.shape[1] // 2
    row = 0
    for left_ref in left_refs:
        count = left_ref.shape[0]
        for start in range(0, half, 384):
            lane = pl.multiple_of(which * half + start, 128)
            sums[row : row + count, first + start : first + start + 384] = dot(
                left_ref[...], right_ref[:, pl.ds(lane, 384)]
            )
        row += count


def products(groups, refs, which, sums):
    first = 0
    for count in groups:
        product_half(refs[:count], refs[count], which, sums, first)
        first += refs[count].shape[1] // 2
        refs = refs[count + 1 :]


def give_kernel(groups, place_ref, *refs):
    out_ref, sums = refs[-2:]
    shard, core = place_ref[0], place_ref[1]
    products(groups, refs[:-2], 1 - core, sums)
    rows = out_ref.shape[2]
    for order in range(8):
        owner = shard ^ (2 * (order % 4) + order // 4)
        for part in range(3):
            start = pl.multiple_of((owner * 3 + part) * rows, rows)
            out_ref[order, part] = sums[pl.ds(start, rows), :].astype(LOW)


def keep_kernel(groups, place_ref, received_ref, *refs):
    give_ref, keep_ref, sums = refs[-3:]
    shard, core, plane = place_ref[0], place_ref[1], place_ref[2]
    products(groups, refs[:-3], core, sums)
    rows = give_ref.shape[1]
    for order in range(8):
        owner = shard ^ (2 * (order % 4) + order // 4)

        def total(part):
            start = pl.multiple_of((owner * 3 + part) * rows, rows)
            mine = sums[pl.ds(start, rows), :]
            return (mine + received_ref[order, part].astype(WIDE)).astype(LOW)

        give_ref[order] = total(1 - plane)
        keep_ref[0, order] = total(plane)
        keep_ref[1, order] = total(2)


class Reduction:
    def __init__(self, place, groups):
        self.place = place
        self.counts = tuple(len(group) - 1 for group in groups)
        self.operands = [entry for group in groups for entry in group]
        self.height = sum(entry.shape[0] for entry in groups[0][:-1])
        self.half = sum(group[-1].shape[1] for group in groups) // 2
        self.rows = self.height // 24
        self.scratch = [pltpu.VMEM((self.height, self.half), WIDE)]
        self.cost = cost(2 * self.height * self.half * ROW, 4 * self.height * self.half)

    def give(self):
        return pl.pallas_call(
            partial(give_kernel, self.counts),
            out_shape=shape((8, 3, self.rows, self.half)),
            in_specs=[in_smem()] + [in_vmem()] * len(self.operands),
            out_specs=in_vmem(),
            scratch_shapes=self.scratch,
            compiler_params=kernel_params(10),
            cost_estimate=self.cost,
        )(self.place, *self.operands)

    def keep(self, received):
        return pl.pallas_call(
            partial(keep_kernel, self.counts),
            out_shape=[shape((8, self.rows, self.half)), shape((2, 8, self.rows, self.half))],
            in_specs=[in_smem()] + [in_vmem()] * (1 + len(self.operands)),
            out_specs=[in_vmem()] * 2,
            scratch_shapes=self.scratch,
            compiler_params=kernel_params(12),
            cost_estimate=self.cost,
        )(self.place, received, *self.operands)

    def over_z(self, columns, name):
        return [swap(columns[step], "shard", 2 * step, name) for step in (1, 2, 3)]


def together(place, *tasks):
    counts = [(len(inputs), len(outputs)) for _, inputs, outputs in tasks]
    inputs = [entry for task in tasks for entry in task[1]]
    outputs = [entry for task in tasks for entry in task[2]]

    def kernel(place_ref, *refs):
        sources, targets = refs[: len(inputs)], refs[len(inputs) :]
        for (step, _, _), (given, made) in zip(tasks, counts):
            step(place_ref, *sources[:given], *targets[:made])
            sources, targets = sources[given:], targets[made:]

    results = pl.pallas_call(
        kernel,
        out_shape=outputs,
        in_specs=[in_smem()] + [in_vmem()] * len(inputs),
        out_specs=[in_vmem()] * len(outputs),
        compiler_params=kernel_params(16),
        cost_estimate=cost(1, 1),
    )(place, *inputs)
    groups = []
    for _, made in counts:
        groups.append(results[:made])
        results = results[made:]
    return groups


def wide(entry):
    return entry.astype(WIDE)


def stack_four(place_ref, first, second, third, fourth, stacked):
    for number, entry in enumerate((first, second, third, fourth)):
        stacked[number] = entry[...]


def to_stack(entries):
    return stack_four, tuple(entries), [shape((4,) + entries[0].shape)]


def send_y(place_ref, near, far, sent):
    rows = sent.shape[1]
    for step in range(4):
        sent[step] = near[step, 0:rows]
        sent[4 + step] = far[step, 0:rows]


def to_send_y(near, far, rows):
    return send_y, (near, far), [shape((8, rows, near.shape[2]))]


def send_x(place_ref, kept, side, sent):
    sent[0] = (wide(kept[0, 4:8]) + wide(side[4:8])).astype(LOW)
    sent[1] = kept[1, 4:8]


def to_send_x(kept, side):
    return send_x, (kept, side), [shape((2, 4) + kept.shape[2:])]


def send_z(place_ref, kept, side, column, *columns):
    for step in range(4):
        part = wide(kept[0, step]) + wide(side[step]) + wide(column[0, step])
        columns[step][0] = part.astype(LOW)
        columns[step][1] = (wide(kept[1, step]) + wide(column[1, step])).astype(LOW)


def to_send_z(kept, side, column):
    return send_z, (kept, side, column), [shape((2,) + kept.shape[2:])] * 4


def add_pieces(place_ref, first, second, third, fourth, total):
    total[...] = (wide(first[...]) + wide(second[...]) + wide(third[...]) + wide(fourth[...])).astype(LOW)


def to_add_pieces(mine, pieces):
    return add_pieces, (mine, *pieces), [shape(mine.shape)]


def join_planes(place_ref, piece, other, before, owned, squares):
    even = place_ref[2] == 0
    mine, theirs = piece[0], other[0]
    owned[0] = jnp.where(even, mine, theirs)
    owned[1] = jnp.where(even, theirs, mine)
    owned[2] = (wide(piece[1]) + wide(other[1])).astype(LOW)
    width = squares.shape[1]
    row = before[...]
    for part in range(3):
        entries = wide(owned[part])
        sums = column_sum(entries * entries)
        if sums.shape[1] < width:
            sums = jnp.concatenate([sums, jnp.zeros((1, width - sums.shape[1]), WIDE)], axis=1)
        for start in range(0, sums.shape[1], width):
            row = row + sums[:, start : start + width]
    squares[...] = row


def to_join_planes(piece, other, before):
    return join_planes, (piece, other, before), [shape((3,) + piece.shape[1:]), shape(before.shape, WIDE)]


def join_cores(bounds):
    def step(place_ref, mine, theirs, *grads):
        low = place_ref[1] == 0
        rows = mine.shape[1]
        for (start, stop), grad in zip(bounds, grads):
            half = stop - start
            for part in range(3):
                own, other = wide(mine[part, :, start:stop]), wide(theirs[part, :, start:stop])
                lines = slice(part * rows, (part + 1) * rows)
                grad[lines, :half] = jnp.where(low, own, other)
                grad[lines, half:] = jnp.where(low, other, own)

    return step


def to_join_cores(mine, theirs, *stops):
    stops = stops or (mine.shape[2],)
    bounds = list(zip((0,) + stops[:-1], stops))
    rows = 3 * mine.shape[1]
    return join_cores(bounds), (mine, theirs), [shape((rows, 2 * (b - a)), WIDE) for a, b in bounds]


def add_sums(place_ref, mine, more, total):
    total[...] = mine[...] + more[...]


def over_rest(entry, add):
    for bit in range(2, lax.axis_size("dp").bit_length() - 1):
        entry = add(entry, swap(entry, "dp", 2**bit))
    return entry


def plus(*entries):
    return sum(entry.astype(WIDE) for entry in entries).astype(LOW)


def step_of(master, grad, first, second, clip, decay):
    correction = 1.0 / (1.0 - ADAM_BETA**STEP)
    clipped = grad * clip
    first = ADAM_BETA * first + (1.0 - ADAM_BETA) * clipped
    second = ADAM_BETA * second + (1.0 - ADAM_BETA) * clipped * clipped
    second = second * correction
    root = second * lax.rsqrt(second) + ADAM_EPS
    change = first * correction * lax.rsqrt(root * root)
    return LEARN_RATE * (change + decay * master)


def update_kernel(clip_ref, *refs):
    clip = clip_ref[...]
    for grad, master, moments, new in zip(*(refs[4 * k : 4 * k + 4] for k in range(4))):
        held = master[...]
        new[...] = held - step_of(held, grad[...], moments[0], moments[1], clip, WEIGHT_DECAY)


def update(clip, grads, masters, moments):
    steps = 3
    flat = [
        pl.BlockSpec((entry.shape[0] // steps, entry.shape[1]), lambda step: (step, 0))
        for entry in masters
    ]
    pairs = [
        pl.BlockSpec((2, entry.shape[0] // steps, entry.shape[1]), lambda step: (0, step, 0))
        for entry in masters
    ]
    return pl.pallas_call(
        update_kernel,
        grid=(steps,),
        out_shape=[shape(entry.shape, WIDE) for entry in masters],
        in_specs=[pl.BlockSpec((1, 1), lambda step: (0, 0)), *flat, *flat, *pairs],
        out_specs=flat,
        compiler_params=kernel_params(24),
        cost_estimate=cost(1, 1),
    )(clip, *hbm(grads), *hbm(masters), *hbm(moments))


def finish_kernel(place_ref, mine_ref, more_ref, vectors_ref, pair_ref, shift_ref, pair2_ref, *refs):
    clip_ref, rms_ref, own_ref, own2_ref, step_ref, new_ref, held = refs
    shard = place_ref[0]
    held[...] = mine_ref[...] + more_ref[...]
    rows, width = held.shape
    entries = held[...]
    number = lax.broadcasted_iota(jnp.int32, (rows, 1), 0)
    power = jnp.where(number == rows - 1, entries, entries * entries)
    power = jnp.sum(power, axis=1, keepdims=True)
    counted = (number < 8) | (number >= 14)
    total = jnp.sum(jnp.where(counted, power, 0.0), axis=0, keepdims=True)
    clip = CLIP_NORM / jnp.maximum(jnp.sqrt(total), CLIP_NORM)
    clip_ref[...] = clip
    tokens = held[13:14, 0:1]
    means = jnp.sqrt(jnp.sum(entries, axis=1, keepdims=True) / (tokens * width))
    lane = lax.broadcasted_iota(jnp.int32, (rows, 128), 1)
    line = jnp.sum(jnp.where(number == lane + 8, means, 0.0), axis=0, keepdims=True)
    rms_ref[...] = line[0, 0:5]
    owned = own_ref.shape[1]
    grad = pltpu.roll(held[0:8, :], width - shard * owned, axis=1)[:, :owned]
    own_ref[...] = grad
    step_ref[...] = step_of(vectors_ref[...], grad, pair_ref[0], pair_ref[1], clip, 0.0)
    owned = own2_ref.shape[0]
    each = width // owned
    lanes = pl.ds(pl.multiple_of((shard % each) * owned, 128), owned)
    grad = held[pl.ds(14 + shard // each, 1), lanes]
    own2_ref[...] = grad[0]
    new = shift_ref[...] - step_of(
        shift_ref[...], grad, pair2_ref[0:1, :], pair2_ref[1:2, :], clip, 0.0
    )
    new_ref[...] = new[0]


def finish(place, mine, more, vectors, pair, shift, pair2):
    count = shift.shape[0]
    shift = shift.reshape(1, count)
    return pl.pallas_call(
        finish_kernel,
        out_shape=[
            shape((1, 1), WIDE),
            shape((5,), WIDE),
            shape(vectors.shape, WIDE),
            shape((count,), WIDE),
            shape(vectors.shape, WIDE),
            shape((count,), WIDE),
        ],
        in_specs=[in_smem()] + [in_vmem()] * 6,
        out_specs=[in_vmem()] * 6,
        scratch_shapes=[pltpu.VMEM(mine.shape, WIDE)],
        compiler_params=kernel_params(4),
        cost_estimate=cost(1, 1),
    )(place, mine, more, vectors, pair, shift, pair2)


def body(
    tokens,
    picture_ids,
    cotangent,
    w_qkv,
    w_out,
    w_fc1,
    w_fc2,
    vectors,
    fc1_bias,
    moments_qkv,
    moments_out,
    moments_fc1,
    moments_fc2,
    moments_vectors,
    moments_fc1_bias,
):
    model_width = tokens.shape[1]
    shard = lax.axis_index("shard")
    data = lax.axis_index("dp")
    place = jnp.stack([shard, data % 2, (data // 2) % 2]).astype(jnp.int32)
    own_a, own_b, own_c = own_pieces(place, w_qkv, w_out, w_fc1, w_fc2, vectors, fc1_bias)
    near_a = jnp.stack(gather_z(own_a, "A"))
    near_a, own_b, own_c = sync(near_a, own_b, own_c)
    far_a, near2_a = gather_x(near_a, "A"), gather_core(near_a, "A")
    near_b = jnp.stack(gather_z(own_b, "B"))
    far_a, near_b, near2_a, own_c = sync(far_a, near_b, near2_a, own_c)
    side_a = gather_y(near_a, far_a, "A", lanes=w_qkv.shape[1] // 2)
    far_b = gather_x(near_b, "B")
    z_c = gather_z(own_c, "C")
    side_a, far_b, z_c = sync(side_a, far_b, z_c)
    far2_a, side2_a = gather_core(far_a, "A"), gather_core(side_a, "A")
    (near_c,), (sent,) = together(
        place, to_stack(z_c), to_send_y(near_b, far_b, w_out.shape[0] // 3)
    )
    pieces_a = (near_a, far_a, side_a, near2_a, far2_a, side2_a)
    side_b, near2_b = swap(sent, "dp", 2, "B"), gather_core(near_b, "B")
    far_c = gather_x(near_c, "C")
    far2_b = gather_core(after(far_b, side2_a), "B")
    vec, bias, valid, a1_t, mix, mix_t, qkv, prob = attention(
        place, after(tokens, side2_a, near_c), picture_ids, w_fc1.shape[1], pieces_a
    )
    side_b, far2_b, near2_b, far_c, mix = sync(side_b, far2_b, near2_b, far_c, mix)
    side2_b, near2_c = gather_core(side_b, "B"), gather_core(near_c, "C")
    ((sent,),) = together(place, to_send_y(near_c, far_c, w_fc2.shape[0] // 4))
    side_c, far2_c = swap(sent, "dp", 2, "C"), gather_core(far_c, "C")
    pieces_b = (near_b, far_b, side_b, near2_b, far2_b, side2_b)
    mid, a2_t, act, act_t, slope, sums_in, wide_out, wide_fc1 = hidden_layer(
        place, tokens, mix, valid, vec, bias, pieces_b
    )
    fc2 = Reduction(place, [(act_t, cotangent)])
    given = fc2.give()
    side_c, far2_c, near2_c, given = sync(side_c, far2_c, near2_c, given)
    recv_f2, side2_c = gather_core(given, "F2"), gather_core(side_c, "C")
    pieces_c = (near_c, far_c, side_c, near2_c, far2_c, side2_c)
    give_f2, keep_f2 = fc2.keep(recv_f2)
    side_f2 = swap(give_f2, "dp", 2, "F2")
    d_pre, shift_sum, wide_fc2 = hidden_back(place, cotangent, after(slope, give_f2), pieces_c)
    layer_out, d_mid, d_mid_low, d_mix, sums_mid = middle_layer(
        mid, act, d_pre, cotangent, valid, vec, wide_out, wide_fc1, wide_fc2
    )
    fc1 = Reduction(place, [(a2_t, after(d_pre, d_mix))])
    given = fc1.give()
    side_f2, given, d_mix = sync(side_f2, given, d_mix)
    recv_f1 = gather_core(given, "F1")
    ((sent,),) = together(place, to_send_x(keep_f2, side_f2))
    column_f2 = swap(sent, "shard", 1, "F2")
    give_f1, keep_f1 = fc1.keep(after(recv_f1, sent))
    side_f1 = swap(give_f1, "dp", 2, "F1")
    d_proj, sums_att = attention_back(qkv, mix_t, after(d_mix, give_f1), prob)
    first = Reduction(place, [(a1_t, d_proj), (mix_t, d_mid_low)])
    given = first.give()
    column_f2, side_f1, given = sync(column_f2, side_f1, given)
    recv_a = gather_core(given, "RA")
    tokens_grad, small_sums = first_norm_back(
        place,
        tokens,
        d_proj,
        after(d_mid, given),
        vec,
        valid,
        (sums_in, sums_mid, sums_att, shift_sum),
        pieces_a,
    )
    recv_a, small_sums = sync(recv_a, small_sums)
    give_a, keep_a = first.keep(recv_a)
    columns_f2, (sent,) = together(
        place,
        to_send_z(keep_f2, side_f2, after(column_f2, give_a)),
        to_send_x(keep_f1, side_f1),
    )
    pieces_f2 = fc2.over_z(columns_f2, "F2")
    column_f1 = swap(sent, "shard", 1, "F1")
    side_ra = swap(give_a, "dp", 2, "RA")
    side_ra, column_f1, pieces_f2 = sync(side_ra, column_f1, pieces_f2)
    (sent,), columns_f1, (piece_f2,) = together(
        place,
        to_send_x(keep_a, side_ra),
        to_send_z(keep_f1, side_f1, column_f1),
        to_add_pieces(columns_f2[0], pieces_f2),
    )
    piece_f2 = over_rest(piece_f2, plus)
    other_f2 = swap(piece_f2, "dp", 2, "F2")
    pieces_f1 = fc1.over_z(columns_f1, "F1")
    column_a = swap(sent, "shard", 1, "RA")
    column_a, pieces_f1, other_f2 = sync(column_a, pieces_f1, other_f2)
    columns_a, (piece_f1,), (owned_f2, squares) = together(
        place,
        to_send_z(keep_a, side_ra, column_a),
        to_add_pieces(columns_f1[0], pieces_f1),
        to_join_planes(piece_f2, other_f2, jnp.zeros((1, model_width), WIDE)),
    )
    theirs_f2 = gather_core(owned_f2, "F2")
    piece_f1 = over_rest(piece_f1, plus)
    other_f1 = swap(piece_f1, "dp", 2, "F1")
    pieces_ra = first.over_z(columns_a, "RA")
    pieces_ra, other_f1, theirs_f2 = sync(pieces_ra, other_f1, theirs_f2)
    (piece_a,), (owned_f1, squares) = together(
        place,
        to_add_pieces(columns_a[0], pieces_ra),
        to_join_planes(piece_f1, other_f1, squares),
    )
    piece_a = over_rest(piece_a, plus)
    other_a = swap(piece_a, "dp", 2, "RA")
    small_more = swap(after(small_sums, piece_a), "dp", 2)
    theirs_f1 = gather_core(owned_f1, "F1")
    ((grad_fc2,),) = together(place, to_join_cores(owned_f2, after(theirs_f2, piece_a)))
    other_a, theirs_f1, small_more, grad_fc2 = sync(other_a, theirs_f1, small_more, grad_fc2)
    (owned_a, squares), (small_sums,) = together(
        place,
        to_join_planes(piece_a, other_a, squares),
        (add_sums, (small_sums, small_more), [shape(small_sums.shape, WIDE)]),
    )
    small_sums = over_rest(small_sums, jnp.add)
    theirs_a = gather_core(owned_a, "RA")
    small_sums = jnp.concatenate([small_sums, squares])
    small_more = swap(small_sums, "dp", 1)
    ((grad_fc1,),) = together(place, to_join_cores(owned_f1, after(theirs_f1, small_sums)))
    theirs_a, small_more, grad_fc1 = sync(theirs_a, small_more, grad_fc1)
    small_sums = small_sums + small_more
    small_more = swap(small_sums, "shard", 1)
    ((grad_qkv, grad_out),) = together(
        place,
        to_join_cores(owned_a, after(theirs_a, small_sums), w_qkv.shape[1] // 2, owned_a.shape[2]),
    )
    small_more, grad_qkv = sync(small_more, grad_qkv)
    small_sums = small_sums + small_more
    small_sums = small_sums + swap(small_sums, "shard", 2)
    small_more = swap(small_sums, "shard", 4)
    clip, stream_rms, own_vectors, own_shift, vector_step, new_shift = finish(
        place, small_sums, small_more, vectors, moments_vectors, fc1_bias, moments_fc1_bias
    )
    grads = (grad_qkv, grad_out, grad_fc1, grad_fc2)
    updated = update(
        clip,
        grads,
        (w_qkv, w_out, w_fc1, w_fc2),
        (moments_qkv, moments_out, moments_fc1, moments_fc2),
    )
    owner_grads = (*grads, own_vectors, own_shift)
    updated = (*updated, vector_step, new_shift)
    return (layer_out, tokens_grad, *owner_grads, *updated, stream_rms)


def solution(mesh):
    placed = (
        P(("dp", "shard"), None),
        P(("dp", "shard")),
        P(("dp", "shard"), None),
        P("shard", None),
        P("shard", None),
        P("shard", None),
        P("shard", None),
        P(None, "shard"),
        P("shard"),
        P(None, "shard", None),
        P(None, "shard", None),
        P(None, "shard", None),
        P(None, "shard", None),
        P(None, None, "shard"),
        P(None, "shard"),
    )
    return jax.shard_map(
        body,
        mesh=mesh,
        in_specs=placed,
        out_specs=(
            P(("dp", "shard"), None),
            P(("dp", "shard"), None),
            P("shard", None),
            P("shard", None),
            P("shard", None),
            P("shard", None),
            P(None, "shard"),
            P("shard"),
            P("shard", None),
            P("shard", None),
            P("shard", None),
            P("shard", None),
            P(None, "shard"),
            P("shard"),
            P(),
        ),
        check_vma=False,
    )
```

```python
from functools import partial

import jax
import jax.numpy as jnp
from jax import lax
from jax.experimental import pallas as pl
from jax.experimental.pallas import tpu as pltpu
from jax.sharding import PartitionSpec as P

HEADS = 12
HEAD_DIM = 64
ROW = 512
STEP = 2

NORM_EPS = 1e-06
ADAM_BETA = 0.5
LEARN_RATE = 0.03
WEIGHT_DECAY = 0.1
ADAM_EPS = 1e-08
CLIP_NORM = 1.0
MASKED = -1e30
GELU_SCALE = 0.7978845608028654
GELU_CUBE = 0.044715

LOW = jnp.bfloat16
WIDE = jnp.float32


def swap(entry, axis, mask, name="sums"):
    count = lax.axis_size(axis)
    with jax.named_scope(name + "_" + axis + str(mask)):
        return lax.ppermute(entry, axis, [(place, place ^ mask) for place in range(count)])


def in_vmem():
    return pl.BlockSpec(memory_space=pltpu.VMEM)


def in_hbm():
    return pl.BlockSpec(memory_space=pltpu.HBM)


def hbm(entries):
    return [pltpu.with_memory_space_constraint(entry, pltpu.HBM) for entry in entries]


def in_smem():
    return pl.BlockSpec(memory_space=pltpu.SMEM)


def shape(dims, kind=LOW):
    return jax.ShapeDtypeStruct(dims, kind)


def cost(flops, moved):
    return pl.CostEstimate(flops=1, bytes_accessed=1, transcendentals=0)


def kernel_params(mib):
    return pltpu.CompilerParams(vmem_limit_bytes=mib * 2**20)


def dot(left, right):
    return jnp.dot(left, right, preferred_element_type=WIDE)


def dot_t(left, right):
    return lax.dot_general(left, right, (((1,), (1,)), ((), ())), preferred_element_type=WIDE)


def normalize(entries):
    center = entries - jnp.mean(entries, axis=-1, keepdims=True)
    scale = lax.rsqrt(jnp.mean(center * center, axis=-1, keepdims=True) + NORM_EPS)
    return center * scale, scale


def normalize_back(grad, normed, scale):
    inner = jnp.mean(grad * normed, axis=-1, keepdims=True)
    return scale * (grad - jnp.mean(grad, axis=-1, keepdims=True) - normed * inner)


def column_sum(entries):
    return jnp.sum(entries, axis=0, keepdims=True)


def own_pieces_kernel(place_ref, *refs):
    sources, vectors_in, shift_in = refs[:4], refs[4], refs[5]
    qkv_ref, mid_ref, fc2_ref = refs[6:9]
    scratch, vectors_ref, shift_ref, sem = refs[9:13], refs[13], refs[14], refs[15]
    core, plane = place_ref[1], place_ref[2]
    copies = []
    for number, (source, held) in enumerate(zip(sources, scratch)):
        rows, lanes = held.shape
        column = pl.multiple_of(core * lanes, 128)
        size = rows // (1, 2, 2, 3)[number]
        spans = [(plane * size, 0, size)]
        if number > 0:
            spans.append((2 * size, size, rows - size))
        for start, at, length in spans:
            copies.append(
                pltpu.make_async_copy(
                    source.at[pl.ds(pl.multiple_of(start, size), length), pl.ds(column, lanes)],
                    held.at[pl.ds(at, length)],
                    sem.at[len(copies)],
                )
            )
    copies.append(pltpu.make_async_copy(vectors_in, vectors_ref, sem.at[len(copies)]))
    copies.append(pltpu.make_async_copy(shift_in, shift_ref, sem.at[len(copies)]))
    for copy in copies:
        copy.start()
    qkv, out, fc1, fc2 = scratch
    width = qkv.shape[1]
    qkv_ref[:, width:] = jnp.zeros((qkv.shape[0], 128), LOW)
    for copy in copies:
        copy.wait()
    qkv_ref[0:8, width : width + vectors_ref.shape[1]] = vectors_ref[...].astype(LOW)
    qkv_ref[8 : 8 + shift_ref.shape[0], width:] = shift_ref[...].astype(LOW)
    qkv_ref[:, :width] = qkv[...].astype(LOW)
    width = out.shape[1]
    mid_ref[:, :width] = out[...].astype(LOW)
    mid_ref[:, width:] = fc1[...].astype(LOW)
    fc2_ref[...] = fc2[...].astype(LOW)


def own_pieces(place, w_qkv, w_out, w_fc1, w_fc2, vectors, fc1_bias):
    shift = fc1_bias.reshape(-1, 128)
    weights = (w_qkv, w_out, w_fc1, w_fc2)
    dims = [
        (entry.shape[0] * share // 12, entry.shape[1] // 2)
        for share, entry in zip((6, 8, 8, 9), weights)
    ]
    return pl.pallas_call(
        own_pieces_kernel,
        out_shape=[
            shape((dims[0][0], dims[0][1] + 128)),
            shape((dims[1][0], dims[1][1] + dims[2][1])),
            shape(dims[3]),
        ],
        in_specs=[in_smem()] + [in_hbm()] * 6,
        out_specs=[in_vmem()] * 3,
        scratch_shapes=[pltpu.VMEM(entry, WIDE) for entry in (*dims, vectors.shape, shift.shape)]
        + [pltpu.SemaphoreType.DMA((9,))],
        compiler_params=kernel_params(8),
    )(place, *hbm((*weights, vectors, shift)))


def after(entry, *others):
    return sync(entry, *others)[0]


def sync(*entries):
    leaves, tree = jax.tree.flatten(entries)
    return jax.tree.unflatten(tree, lax.optimization_barrier(leaves))


def gather_z(own, name):
    return [own] + [swap(own, "shard", mask, name) for mask in (2, 4, 6)]


def gather_x(near, name):
    return swap(near, "shard", 1, name)


def gather_y(near, far, name, rows=None, lanes=None):
    return swap(jnp.concatenate([near[:, :rows, :lanes], far[:, :rows, :lanes]]), "dp", 2, name)


def gather_core(entry, name):
    return swap(entry, "dp", 1, name)


def load_weight(place_ref, pieces, first, width, full, sem):
    shard, core, plane = place_ref[0], place_ref[1], place_ref[2]
    lanes = pl.ds(first, width)
    count = len(pieces) // 2
    owned = full.shape[0] // 8
    rows = pieces[2].shape[1] if count == 3 else owned
    shared = pieces[0].shape[1] - rows

    def put(source, owner, start, which):
        row = pl.multiple_of(owner * owned + start, 16)
        column = pl.multiple_of(which * width, 128)
        target = full.at[pl.ds(row, source.shape[0]), pl.ds(column, width)]
        pltpu.make_async_copy(source, target, sem).start()

    for which, half in ((core, pieces[:count]), (1 - core, pieces[count:])):
        for flip in range(2):
            for step in range(4):
                owner = shard ^ (2 * step + flip)
                ref = half[flip].at[step]
                put(ref.at[pl.ds(0, rows), lanes], owner, plane * rows if count == 3 else 0, which)
                if shared:
                    put(ref.at[pl.ds(rows, shared), lanes], owner, 2 * rows, which)
                if count == 3:
                    side = half[2].at[4 * flip + step, :, lanes]
                    put(side, owner, (1 - plane) * rows, which)
    return pltpu.make_async_copy(full, full, sem)


def gather_vectors(place_ref, near, far, held, sem, vec_ref, shift_ref):
    lane = near.shape[2] - 128
    owned = vec_ref.shape[1] // 8
    for flip, ref in ((0, near), (1, far)):
        for step in range(4):
            source = ref.at[step, pl.ds(0, 16), pl.ds(lane, 128)]
            pltpu.make_async_copy(source, held.at[4 * flip + step], sem).start()
    pltpu.make_async_copy(held, held, sem).wait()
    source = lax.broadcasted_iota(jnp.int32, (128, vec_ref.shape[1]), 0)
    target = lax.broadcasted_iota(jnp.int32, (128, vec_ref.shape[1]), 1)
    rows = jnp.zeros((16, vec_ref.shape[1]), WIDE)
    count = shift_ref.shape[1] // (8 * 128)
    for order in range(8):
        owner = place_ref[0] ^ (2 * (order % 4) + order // 4)
        move = (target == source + owner * owned) & (source < owned)
        rows = rows + dot(held[order], move.astype(WIDE).astype(LOW))
        for row in range(count):
            start = pl.multiple_of((owner * count + row) * 128, 128)
            shift_ref[0:1, pl.ds(start, 128)] = held[order, 8 + row : 9 + row, :].astype(WIDE)
    vec_ref[...] = rows[0:8]


def attention_kernel(place_ref, stream_ref, ids_ref, *refs):
    pieces = refs[:6]
    vec_ref, shift_ref, valid_ref, a1_t_ref, mix_ref, mix_t_ref, qkv_out, prob_out = refs[6:14]
    weight, qkv_ref, prob, bias, v_t, weight_sem, vec_held, vec_sem, out_sem = refs[14:]
    width = mix_ref.shape[1]
    pairs = width // 128
    loading = load_weight(place_ref, pieces, 0, weight.shape[1] // 2, weight, weight_sem)
    gather_vectors(place_ref, *pieces[:2], vec_held, vec_sem, vec_ref, shift_ref)
    normed, _ = normalize(stream_ref[...].astype(WIDE))
    a1 = (normed * vec_ref[0:1, :] + vec_ref[1:2, :]).astype(LOW)
    a1_t_ref[...] = a1.T
    ids = ids_ref[...].astype(WIDE)
    column = jnp.broadcast_to(ids, (128, ROW)).T[:, 0:1]
    bias[...] = jnp.where(column == ids, 0.0, MASKED)
    valid_ref[...] = jnp.where(column == 0.0, 0.0, 1.0)
    loading.wait()
    queries = dot(a1, weight[:, :width]) + vec_ref[2:3, :]
    qkv_ref[:, :width] = queries.astype(LOW)
    qkv_ref[:, width : 2 * width] = dot(a1, weight[:, width : 2 * width]).astype(LOW)
    values = (dot(a1, weight[:, 2 * width :]) + vec_ref[3:4, :]).astype(LOW)
    qkv_ref[:, 2 * width :] = values
    qkv_copy = pltpu.make_async_copy(qkv_ref, qkv_out, out_sem.at[pairs])
    qkv_copy.start()
    v_t[...] = values.T

    def out_copy(pair):
        heads = pl.ds(2 * pair, 2)
        return pltpu.make_async_copy(prob.at[heads], prob_out.at[heads], out_sem.at[pair])

    left = lax.broadcasted_iota(jnp.int32, (ROW, 128), 1) < HEAD_DIM

    @pl.loop(0, pairs, unroll=2)
    def _(pair):
        lane = pl.multiple_of(pair * 128, 128)
        scaled = qkv_ref[:, pl.ds(lane, 128)] * HEAD_DIM**-0.5
        keys = qkv_ref[:, pl.ds(width + lane, 128)]
        blank = jnp.zeros_like(keys)
        halves = jnp.concatenate([jnp.where(left, keys, blank), jnp.where(left, blank, keys)])
        scores = dot_t(halves, scaled)
        for half in range(2):
            v_rows = pl.ds(pl.multiple_of(lane + half * HEAD_DIM, HEAD_DIM), HEAD_DIM)
            head = scores[half * ROW : (half + 1) * ROW] + bias[...]
            weights = jnp.exp(head - jnp.max(head, axis=0, keepdims=True))
            weights = weights * (1.0 / jnp.sum(weights, axis=0, keepdims=True))
            low = weights.astype(LOW)
            prob[2 * pair + half] = low
            mix_t_ref[v_rows, :] = dot(v_t[v_rows, :], low).astype(LOW)
        out_copy(pair).start()

    mix_ref[...] = mix_t_ref[...].T
    qkv_copy.wait()

    @pl.loop(0, pairs)
    def _(pair):
        out_copy(pair).wait()


def attention(place, stream, ids, hidden, pieces):
    width = stream.shape[1]
    return pl.pallas_call(
        attention_kernel,
        out_shape=[
            shape((8, width), WIDE),
            shape((1, hidden), WIDE),
            shape((ROW, 1), WIDE),
            shape((width, ROW)),
            shape((ROW, width)),
            shape((width, ROW)),
            pltpu.HBM((ROW, 3 * width), LOW),
            pltpu.HBM((HEADS, ROW, ROW), LOW),
        ],
        in_specs=[in_smem()] + [in_vmem()] * 2 + [in_hbm()] * 6,
        out_specs=[in_vmem()] * 6 + [in_hbm()] * 2,
        scratch_shapes=[
            pltpu.VMEM((width, 3 * width), LOW),
            pltpu.VMEM((ROW, 3 * width), LOW),
            pltpu.VMEM((HEADS, ROW, ROW), LOW),
            pltpu.VMEM((ROW, ROW), WIDE),
            pltpu.VMEM((width, ROW), LOW),
            pltpu.SemaphoreType.DMA,
            pltpu.VMEM((8, 16, 128), LOW),
            pltpu.SemaphoreType.DMA,
            pltpu.SemaphoreType.DMA((HEADS // 2 + 1,)),
        ],
        compiler_params=kernel_params(22),
        cost_estimate=cost(12e9, 24e6),
    )(place, stream, ids.reshape(1, ROW), *hbm(pieces))


def hidden_kernel(place_ref, tokens_ref, mix_ref, valid_ref, vec_ref, bias_ref, *refs):
    pieces = refs[:6]
    mid_ref, a2_t_ref, act_ref, act_t_ref, slope_ref, sums_ref, w_out, w_fc1 = refs[6:14]
    out_sem, fc1_sem = refs[14:]
    width = tokens_ref.shape[1]
    hidden = bias_ref.shape[1]
    out_ready = load_weight(place_ref, pieces, 0, width // 2, w_out, out_sem)
    fc1_ready = load_weight(place_ref, pieces, width // 2, hidden // 2, w_fc1, fc1_sem)
    stream = tokens_ref[...].astype(WIDE)
    valid = valid_ref[...]
    out_ready.wait()
    branch = dot(mix_ref[...], w_out[...]) + vec_ref[4:5, :]
    middle = stream + branch
    mid_ref[...] = middle
    sums_ref[0:1, :] = column_sum(valid * stream * stream)
    sums_ref[1:2, :] = column_sum(valid * branch * branch)
    sums_ref[2:3, :] = column_sum(valid * middle * middle)
    sums_ref[3:8, :] = jnp.zeros((5, width), WIDE)
    normed, _ = normalize(middle)
    a2 = (normed * vec_ref[5:6, :] + vec_ref[6:7, :]).astype(LOW)
    a2_t_ref[...] = a2.T
    fc1_ready.wait()
    step = 512
    for first in range(0, hidden, step):
        lanes = slice(first, first + step)
        pre = dot(a2, w_fc1[:, lanes]) + bias_ref[:, lanes]
        square = pre * pre
        turn = jnp.tanh(GELU_SCALE * (pre + GELU_CUBE * (square * pre)))
        half = 0.5 * (1.0 + turn)
        act = (pre * half).astype(LOW)
        act_ref[:, lanes] = act
        act_t_ref[lanes, :] = act.T
        bend = (1.0 - turn * turn) * (GELU_SCALE + 3.0 * GELU_SCALE * GELU_CUBE * square)
        slope_ref[:, lanes] = (half + 0.5 * pre * bend).astype(LOW)


def hidden_layer(place, tokens, mix, valid, vec, bias, pieces):
    width, hidden = tokens.shape[1], bias.shape[1]
    return pl.pallas_call(
        hidden_kernel,
        out_shape=[
            shape((ROW, width), WIDE),
            shape((width, ROW)),
            shape((ROW, hidden)),
            shape((hidden, ROW)),
            shape((ROW, hidden)),
            shape((8, width), WIDE),
            shape((width, width)),
            shape((width, hidden)),
        ],
        in_specs=[in_smem()] + [in_vmem()] * 5 + [in_hbm()] * 6,
        out_specs=[in_vmem()] * 8,
        scratch_shapes=[
            pltpu.SemaphoreType.DMA,
            pltpu.SemaphoreType.DMA,
        ],
        compiler_params=kernel_params(22),
        cost_estimate=cost(10e9, 20e6),
    )(place, tokens, mix, valid, vec, bias, *hbm(pieces))


def hidden_back_kernel(place_ref, cot_ref, slope_ref, *refs):
    pieces = refs[:6]
    d_pre_ref, shift_ref, w_fc2, sem = refs[6:]
    hidden = slope_ref.shape[1]
    loading = load_weight(place_ref, pieces, 0, w_fc2.shape[1] // 2, w_fc2, sem)
    cot = cot_ref[...]
    loading.wait()
    step = 512
    for first in range(0, hidden, step):
        lanes = slice(first, first + step)
        d_pre = dot_t(cot, w_fc2[lanes, :]) * slope_ref[:, lanes].astype(WIDE)
        shift_ref[:, lanes] = column_sum(d_pre)
        d_pre_ref[:, lanes] = d_pre.astype(LOW)


def hidden_back(place, cot, slope, pieces):
    width, hidden = cot.shape[1], slope.shape[1]
    return pl.pallas_call(
        hidden_back_kernel,
        out_shape=[shape((ROW, hidden)), shape((1, hidden), WIDE), shape((hidden, width))],
        in_specs=[in_smem()] + [in_vmem()] * 2 + [in_hbm()] * 6,
        out_specs=[in_vmem()] * 3,
        scratch_shapes=[pltpu.SemaphoreType.DMA],
        compiler_params=kernel_params(18),
        cost_estimate=cost(3e9, 14e6),
    )(place, cot, slope, *hbm(pieces))


def middle_kernel(mid_ref, act_ref, d_pre_ref, cot_ref, valid_ref, vec_ref, *refs):
    w_out, w_fc1, w_fc2 = refs[:3]
    layer_ref, d_mid_ref, d_mid_low_ref, d_mix_ref, sums_ref = refs[3:]
    middle = mid_ref[...]
    valid = valid_ref[...]
    mlp = dot(act_ref[...], w_fc2[...]) + vec_ref[7:8, :]
    result = middle + mlp
    layer_ref[...] = result.astype(LOW)
    sums_ref[4:5, :] = column_sum(valid * mlp * mlp)
    sums_ref[5:6, :] = column_sum(valid * result * result)
    sums_ref[6:8, :] = jnp.zeros((2, mid_ref.shape[1]), WIDE)
    d_a2 = dot_t(d_pre_ref[...], w_fc1[...])
    normed, scale = normalize(middle)
    dy = cot_ref[...].astype(WIDE)
    d_mid = dy + normalize_back(d_a2 * vec_ref[5:6, :], normed, scale)
    d_mid_ref[...] = d_mid
    low = d_mid.astype(LOW)
    d_mid_low_ref[...] = low
    sums_ref[0:1, :] = column_sum(d_mid)
    sums_ref[1:2, :] = column_sum(d_a2 * normed)
    sums_ref[2:3, :] = column_sum(d_a2)
    sums_ref[3:4, :] = column_sum(dy)
    d_mix_ref[...] = dot_t(low, w_out[...]).astype(LOW)


def middle_layer(mid, act, d_pre, cot, valid, vec, w_out, w_fc1, w_fc2):
    width = mid.shape[1]
    return pl.pallas_call(
        middle_kernel,
        out_shape=[
            shape((ROW, width)),
            shape((ROW, width), WIDE),
            shape((ROW, width)),
            shape((ROW, width)),
            shape((8, width), WIDE),
        ],
        in_specs=[in_vmem()] * 9,
        out_specs=[in_vmem()] * 5,
        compiler_params=kernel_params(20),
        cost_estimate=cost(14e9, 30e6),
    )(mid, act, d_pre, cot, valid, vec, w_out, w_fc1, w_fc2)


def attention_back_kernel(qkv_ref, mix_t_ref, d_mix_ref, prob_in, d_proj_ref, sums_ref, *rest):
    k_t, d_mix_t, d_q_t, prob, sem = rest
    width = mix_t_ref.shape[0]
    pairs = width // 128

    def in_copy(pair):
        heads = pl.ds(2 * pair, 2)
        return pltpu.make_async_copy(prob_in.at[heads], prob.at[heads], sem.at[pair])

    @pl.loop(0, pairs)
    def _(pair):
        in_copy(pair).start()


    k_t[...] = qkv_ref[:, width : 2 * width].T
    d_mix_t[...] = d_mix_ref[...].T
    left = lax.broadcasted_iota(jnp.int32, (ROW, 128), 1) < HEAD_DIM

    @pl.loop(0, pairs, unroll=2)
    def _(pair):
        lane = pl.multiple_of(pair * 128, 128)
        queries = qkv_ref[:, pl.ds(lane, 128)]
        values = qkv_ref[:, pl.ds(2 * width + lane, 128)]
        d_mix = d_mix_ref[:, pl.ds(lane, 128)]
        in_copy(pair).wait()
        d_keys, d_values = [], []
        for half in range(2):
            rows = pl.ds(pl.multiple_of(lane + half * HEAD_DIM, HEAD_DIM), HEAD_DIM)
            inner = column_sum(mix_t_ref[rows, :].astype(WIDE) * d_mix_t[rows, :].astype(WIDE))
            value_half = jnp.where(left == (half == 0), values, jnp.zeros_like(values))
            low = prob[2 * pair + half]
            d_prob = dot_t(value_half, d_mix)
            d_score = (low.astype(WIDE) * (d_prob - inner)).astype(LOW)
            d_keys.append(dot(d_score, queries))
            d_values.append(dot(low, d_mix))
            d_q_t[rows, :] = dot(k_t[rows, :], d_score)
        d_k = jnp.where(left, d_keys[0], d_keys[1]) * HEAD_DIM**-0.5
        d_v = jnp.where(left, d_values[0], d_values[1])
        d_proj_ref[:, pl.ds(width + lane, 128)] = d_k.astype(LOW)
        d_proj_ref[:, pl.ds(2 * width + lane, 128)] = d_v.astype(LOW)
        sums_ref[1:2, pl.ds(lane, 128)] = column_sum(d_v)

    d_q = d_q_t[...].T * HEAD_DIM**-0.5
    d_proj_ref[:, :width] = d_q.astype(LOW)
    sums_ref[0:1, :] = column_sum(d_q)
    sums_ref[2:8, :] = jnp.zeros((6, width), WIDE)


def attention_back(qkv, mix_t, d_mix, prob):
    width = mix_t.shape[0]
    heads = prob.shape[0]
    return pl.pallas_call(
        attention_back_kernel,
        out_shape=[shape((ROW, 3 * width)), shape((8, width), WIDE)],
        in_specs=[in_vmem()] * 3 + [in_hbm()],
        out_specs=[in_vmem()] * 2,
        scratch_shapes=[
            pltpu.VMEM((width, ROW), LOW),
            pltpu.VMEM((width, ROW), LOW),
            pltpu.VMEM((width, ROW), WIDE),
            pltpu.VMEM((heads, ROW, ROW), LOW),
            pltpu.SemaphoreType.DMA((heads // 2,)),
        ],
        compiler_params=kernel_params(20),
        cost_estimate=cost(1.2e9 * heads, 2e6 * heads),
    )(qkv, mix_t, d_mix, *hbm([prob]))


def first_norm_kernel(place_ref, tokens_ref, d_proj_ref, d_mid_ref, vec_ref, *refs):
    valid_ref, in_ref, mid_ref, att_ref, shift_ref = refs[:5]
    pieces = refs[5:11]
    grad_ref, sums_ref, weight, sem = refs[11:]
    width = tokens_ref.shape[1]
    loading = load_weight(place_ref, pieces, 0, weight.shape[1] // 2, weight, sem)
    sums_ref[2:4, :] = att_ref[0:2, :]
    sums_ref[4:8, :] = mid_ref[0:4, :]
    sums_ref[8:11, :] = in_ref[0:3, :]
    sums_ref[11:13, :] = mid_ref[4:6, :]
    sums_ref[13:14, :] = jnp.sum(valid_ref[...]) * jnp.ones((1, width), WIDE)
    for row in range(shift_ref.shape[1] // width):
        sums_ref[14 + row : 15 + row, :] = shift_ref[:, row * width : (row + 1) * width]
    normed, scale = normalize(tokens_ref[...].astype(WIDE))
    loading.wait()
    d_a1 = dot_t(d_proj_ref[...], weight[...])
    d_in = normalize_back(d_a1 * vec_ref[0:1, :], normed, scale)
    grad_ref[...] = (d_mid_ref[...] + d_in).astype(LOW)
    sums_ref[0:1, :] = column_sum(d_a1 * normed)
    sums_ref[1:2, :] = column_sum(d_a1)


def first_norm_back(place, tokens, d_proj, d_mid, vec, valid, sums, pieces):
    width = tokens.shape[1]
    rows = 14 + sums[-1].shape[1] // width
    return pl.pallas_call(
        first_norm_kernel,
        out_shape=[shape((ROW, width)), shape((rows, width), WIDE)],
        in_specs=[in_smem()] + [in_vmem()] * 9 + [in_hbm()] * 6,
        out_specs=[in_vmem()] * 2,
        scratch_shapes=[pltpu.VMEM((width, d_proj.shape[1]), LOW), pltpu.SemaphoreType.DMA],
        compiler_params=kernel_params(16),
        cost_estimate=pl.CostEstimate(flops=4_000_000_000, bytes_accessed=1, transcendentals=0),
    )(place, tokens, d_proj, d_mid, vec, valid, *sums, *hbm(pieces))


def product_half(left_refs, right_ref, which, sums, first):
    half = right_ref.shape[1] // 2
    row = 0
    for left_ref in left_refs:
        count = left_ref.shape[0]
        for start in range(0, half, 384):
            lane = pl.multiple_of(which * half + start, 128)
            sums[row : row + count, first + start : first + start + 384] = dot(
                left_ref[...], right_ref[:, pl.ds(lane, 384)]
            )
        row += count


def products(groups, refs, which, sums):
    first = 0
    for count in groups:
        product_half(refs[:count], refs[count], which, sums, first)
        first += refs[count].shape[1] // 2
        refs = refs[count + 1 :]


def give_kernel(groups, place_ref, *refs):
    out_ref, sums = refs[-2:]
    shard, core = place_ref[0], place_ref[1]
    products(groups, refs[:-2], 1 - core, sums)
    rows = out_ref.shape[2]
    for order in range(8):
        owner = shard ^ (2 * (order % 4) + order // 4)
        for part in range(3):
            start = pl.multiple_of((owner * 3 + part) * rows, rows)
            out_ref[order, part] = sums[pl.ds(start, rows), :].astype(LOW)


def keep_kernel(groups, place_ref, received_ref, *refs):
    give_ref, keep_ref, sums = refs[-3:]
    shard, core, plane = place_ref[0], place_ref[1], place_ref[2]
    products(groups, refs[:-3], core, sums)
    rows = give_ref.shape[1]
    for order in range(8):
        owner = shard ^ (2 * (order % 4) + order // 4)

        def total(part):
            start = pl.multiple_of((owner * 3 + part) * rows, rows)
            mine = sums[pl.ds(start, rows), :]
            return (mine + received_ref[order, part].astype(WIDE)).astype(LOW)

        give_ref[order] = total(1 - plane)
        keep_ref[0, order] = total(plane)
        keep_ref[1, order] = total(2)


class Reduction:
    def __init__(self, place, groups):
        self.place = place
        self.counts = tuple(len(group) - 1 for group in groups)
        self.operands = [entry for group in groups for entry in group]
        self.height = sum(entry.shape[0] for entry in groups[0][:-1])
        self.half = sum(group[-1].shape[1] for group in groups) // 2
        self.rows = self.height // 24
        self.scratch = [pltpu.VMEM((self.height, self.half), WIDE)]
        self.cost = cost(2 * self.height * self.half * ROW, 4 * self.height * self.half)

    def give(self):
        return pl.pallas_call(
            partial(give_kernel, self.counts),
            out_shape=shape((8, 3, self.rows, self.half)),
            in_specs=[in_smem()] + [in_vmem()] * len(self.operands),
            out_specs=in_vmem(),
            scratch_shapes=self.scratch,
            compiler_params=kernel_params(10),
            cost_estimate=self.cost,
        )(self.place, *self.operands)

    def keep(self, received):
        return pl.pallas_call(
            partial(keep_kernel, self.counts),
            out_shape=[shape((8, self.rows, self.half)), shape((2, 8, self.rows, self.half))],
            in_specs=[in_smem()] + [in_vmem()] * (1 + len(self.operands)),
            out_specs=[in_vmem()] * 2,
            scratch_shapes=self.scratch,
            compiler_params=kernel_params(12),
            cost_estimate=self.cost,
        )(self.place, received, *self.operands)

    def over_z(self, columns, name):
        return [swap(columns[step], "shard", 2 * step, name) for step in (1, 2, 3)]


def together(place, *tasks):
    counts = [(len(inputs), len(outputs)) for _, inputs, outputs in tasks]
    inputs = [entry for task in tasks for entry in task[1]]
    outputs = [entry for task in tasks for entry in task[2]]

    def kernel(place_ref, *refs):
        sources, targets = refs[: len(inputs)], refs[len(inputs) :]
        for (step, _, _), (given, made) in zip(tasks, counts):
            step(place_ref, *sources[:given], *targets[:made])
            sources, targets = sources[given:], targets[made:]

    results = pl.pallas_call(
        kernel,
        out_shape=outputs,
        in_specs=[in_smem()] + [in_vmem()] * len(inputs),
        out_specs=[in_vmem()] * len(outputs),
        compiler_params=kernel_params(16),
        cost_estimate=cost(1, 1),
    )(place, *inputs)
    groups = []
    for _, made in counts:
        groups.append(results[:made])
        results = results[made:]
    return groups


def wide(entry):
    return entry.astype(WIDE)


def stack_four(place_ref, first, second, third, fourth, stacked):
    for number, entry in enumerate((first, second, third, fourth)):
        stacked[number] = entry[...]


def to_stack(entries):
    return stack_four, tuple(entries), [shape((4,) + entries[0].shape)]


def send_y(place_ref, near, far, sent):
    rows = sent.shape[1]
    for step in range(4):
        sent[step] = near[step, 0:rows]
        sent[4 + step] = far[step, 0:rows]


def to_send_y(near, far, rows):
    return send_y, (near, far), [shape((8, rows, near.shape[2]))]


def send_x(place_ref, kept, side, sent):
    sent[0] = (wide(kept[0, 4:8]) + wide(side[4:8])).astype(LOW)
    sent[1] = kept[1, 4:8]


def to_send_x(kept, side):
    return send_x, (kept, side), [shape((2, 4) + kept.shape[2:])]


def send_z(place_ref, kept, side, column, *columns):
    for step in range(4):
        part = wide(kept[0, step]) + wide(side[step]) + wide(column[0, step])
        columns[step][0] = part.astype(LOW)
        columns[step][1] = (wide(kept[1, step]) + wide(column[1, step])).astype(LOW)


def to_send_z(kept, side, column):
    return send_z, (kept, side, column), [shape((2,) + kept.shape[2:])] * 4


def add_pieces(place_ref, first, second, third, fourth, total):
    total[...] = (wide(first[...]) + wide(second[...]) + wide(third[...]) + wide(fourth[...])).astype(LOW)


def to_add_pieces(mine, pieces):
    return add_pieces, (mine, *pieces), [shape(mine.shape)]


def join_planes(place_ref, piece, other, before, owned, squares):
    even = place_ref[2] == 0
    mine, theirs = piece[0], other[0]
    owned[0] = jnp.where(even, mine, theirs)
    owned[1] = jnp.where(even, theirs, mine)
    owned[2] = (wide(piece[1]) + wide(other[1])).astype(LOW)
    width = squares.shape[1]
    row = before[...]
    for part in range(3):
        entries = wide(owned[part])
        sums = column_sum(entries * entries)
        if sums.shape[1] < width:
            sums = jnp.concatenate([sums, jnp.zeros((1, width - sums.shape[1]), WIDE)], axis=1)
        for start in range(0, sums.shape[1], width):
            row = row + sums[:, start : start + width]
    squares[...] = row


def to_join_planes(piece, other, before):
    return join_planes, (piece, other, before), [shape((3,) + piece.shape[1:]), shape(before.shape, WIDE)]


def join_cores(bounds):
    def step(place_ref, mine, theirs, *grads):
        low = place_ref[1] == 0
        rows = mine.shape[1]
        for (start, stop), grad in zip(bounds, grads):
            half = stop - start
            for part in range(3):
                own, other = wide(mine[part, :, start:stop]), wide(theirs[part, :, start:stop])
                lines = slice(part * rows, (part + 1) * rows)
                grad[lines, :half] = jnp.where(low, own, other)
                grad[lines, half:] = jnp.where(low, other, own)

    return step


def to_join_cores(mine, theirs, *stops):
    stops = stops or (mine.shape[2],)
    bounds = list(zip((0,) + stops[:-1], stops))
    rows = 3 * mine.shape[1]
    return join_cores(bounds), (mine, theirs), [shape((rows, 2 * (b - a)), WIDE) for a, b in bounds]


def add_sums(place_ref, mine, more, total):
    total[...] = mine[...] + more[...]


def over_rest(entry, add):
    for bit in range(2, lax.axis_size("dp").bit_length() - 1):
        entry = add(entry, swap(entry, "dp", 2**bit))
    return entry


def plus(*entries):
    return sum(entry.astype(WIDE) for entry in entries).astype(LOW)


def step_of(master, grad, first, second, clip, decay):
    correction = 1.0 / (1.0 - ADAM_BETA**STEP)
    clipped = grad * clip
    first = ADAM_BETA * first + (1.0 - ADAM_BETA) * clipped
    second = ADAM_BETA * second + (1.0 - ADAM_BETA) * clipped * clipped
    second = second * correction
    root = second * lax.rsqrt(second) + ADAM_EPS
    change = first * correction * lax.rsqrt(root * root)
    return LEARN_RATE * (change + decay * master)


def update_kernel(clip_ref, *refs):
    clip = clip_ref[...]
    for grad, master, moments, new in zip(*(refs[4 * k : 4 * k + 4] for k in range(4))):
        held = master[...]
        new[...] = held - step_of(held, grad[...], moments[0], moments[1], clip, WEIGHT_DECAY)


def update(clip, grads, masters, moments):
    steps = 3
    flat = [
        pl.BlockSpec((entry.shape[0] // steps, entry.shape[1]), lambda step: (step, 0))
        for entry in masters
    ]
    pairs = [
        pl.BlockSpec((2, entry.shape[0] // steps, entry.shape[1]), lambda step: (0, step, 0))
        for entry in masters
    ]
    return pl.pallas_call(
        update_kernel,
        grid=(steps,),
        out_shape=[shape(entry.shape, WIDE) for entry in masters],
        in_specs=[pl.BlockSpec((1, 1), lambda step: (0, 0)), *flat, *flat, *pairs],
        out_specs=flat,
        compiler_params=kernel_params(24),
        cost_estimate=cost(1, 1),
    )(clip, *hbm(grads), *hbm(masters), *hbm(moments))


def finish_kernel(place_ref, mine_ref, more_ref, vectors_ref, pair_ref, shift_ref, pair2_ref, *refs):
    clip_ref, rms_ref, own_ref, own2_ref, step_ref, new_ref, held = refs
    shard = place_ref[0]
    held[...] = mine_ref[...] + more_ref[...]
    rows, width = held.shape
    entries = held[...]
    number = lax.broadcasted_iota(jnp.int32, (rows, 1), 0)
    power = jnp.where(number == rows - 1, entries, entries * entries)
    power = jnp.sum(power, axis=1, keepdims=True)
    counted = (number < 8) | (number >= 14)
    total = jnp.sum(jnp.where(counted, power, 0.0), axis=0, keepdims=True)
    clip = CLIP_NORM / jnp.maximum(jnp.sqrt(total), CLIP_NORM)
    clip_ref[...] = clip
    tokens = held[13:14, 0:1]
    means = jnp.sqrt(jnp.sum(entries, axis=1, keepdims=True) / (tokens * width))
    lane = lax.broadcasted_iota(jnp.int32, (rows, 128), 1)
    line = jnp.sum(jnp.where(number == lane + 8, means, 0.0), axis=0, keepdims=True)
    rms_ref[...] = line[0, 0:5]
    owned = own_ref.shape[1]
    grad = pltpu.roll(held[0:8, :], width - shard * owned, axis=1)[:, :owned]
    own_ref[...] = grad
    step_ref[...] = step_of(vectors_ref[...], grad, pair_ref[0], pair_ref[1], clip, 0.0)
    owned = own2_ref.shape[0]
    each = width // owned
    lanes = pl.ds(pl.multiple_of((shard % each) * owned, 128), owned)
    grad = held[pl.ds(14 + shard // each, 1), lanes]
    own2_ref[...] = grad[0]
    new = shift_ref[...] - step_of(
        shift_ref[...], grad, pair2_ref[0:1, :], pair2_ref[1:2, :], clip, 0.0
    )
    new_ref[...] = new[0]


def finish(place, mine, more, vectors, pair, shift, pair2):
    count = shift.shape[0]
    shift = shift.reshape(1, count)
    return pl.pallas_call(
        finish_kernel,
        out_shape=[
            shape((1, 1), WIDE),
            shape((5,), WIDE),
            shape(vectors.shape, WIDE),
            shape((count,), WIDE),
            shape(vectors.shape, WIDE),
            shape((count,), WIDE),
        ],
        in_specs=[in_smem()] + [in_vmem()] * 6,
        out_specs=[in_vmem()] * 6,
        scratch_shapes=[pltpu.VMEM(mine.shape, WIDE)],
        compiler_params=kernel_params(4),
        cost_estimate=cost(1, 1),
    )(place, mine, more, vectors, pair, shift, pair2)


def body(
    tokens,
    picture_ids,
    cotangent,
    w_qkv,
    w_out,
    w_fc1,
    w_fc2,
    vectors,
    fc1_bias,
    moments_qkv,
    moments_out,
    moments_fc1,
    moments_fc2,
    moments_vectors,
    moments_fc1_bias,
):
    model_width = tokens.shape[1]
    shard = lax.axis_index("shard")
    data = lax.axis_index("dp")
    place = jnp.stack([shard, data % 2, (data // 2) % 2]).astype(jnp.int32)
    own_a, own_b, own_c = own_pieces(place, w_qkv, w_out, w_fc1, w_fc2, vectors, fc1_bias)
    near_a = jnp.stack(gather_z(own_a, "A"))
    near_a, own_b, own_c = sync(near_a, own_b, own_c)
    far_a, near2_a = gather_x(near_a, "A"), gather_core(near_a, "A")
    near_b = jnp.stack(gather_z(own_b, "B"))
    far_a, near_b, near2_a, own_c = sync(far_a, near_b, near2_a, own_c)
    z_c = gather_z(own_c, "C")
    far_b = gather_x(near_b, "B")
    side_a = gather_y(near_a, far_a, "A", lanes=w_qkv.shape[1] // 2)
    z_c, far_b, side_a = sync(z_c, far_b, side_a)
    far2_a, side2_a = gather_core(far_a, "A"), gather_core(side_a, "A")
    (near_c,), (sent,) = together(
        place, to_stack(z_c), to_send_y(near_b, far_b, w_out.shape[0] // 3)
    )
    pieces_a = (near_a, far_a, side_a, near2_a, far2_a, side2_a)
    side_b, near2_b = swap(sent, "dp", 2, "B"), gather_core(near_b, "B")
    far_c = gather_x(near_c, "C")
    far2_b = gather_core(after(far_b, side2_a), "B")
    vec, bias, valid, a1_t, mix, mix_t, qkv, prob = attention(
        place, after(tokens, side2_a, near_c), picture_ids, w_fc1.shape[1], pieces_a
    )
    side_b, far2_b, near2_b, far_c, mix = sync(side_b, far2_b, near2_b, far_c, mix)
    side2_b, near2_c = gather_core(side_b, "B"), gather_core(near_c, "C")
    ((sent,),) = together(place, to_send_y(near_c, far_c, w_fc2.shape[0] // 4))
    side_c, far2_c = swap(sent, "dp", 2, "C"), gather_core(far_c, "C")
    pieces_b = (near_b, far_b, side_b, near2_b, far2_b, side2_b)
    mid, a2_t, act, act_t, slope, sums_in, wide_out, wide_fc1 = hidden_layer(
        place, tokens, mix, valid, vec, bias, pieces_b
    )
    fc2 = Reduction(place, [(act_t, cotangent)])
    given = fc2.give()
    side_c, far2_c, near2_c, given = sync(side_c, far2_c, near2_c, given)
    recv_f2, side2_c = gather_core(given, "F2"), gather_core(side_c, "C")
    pieces_c = (near_c, far_c, side_c, near2_c, far2_c, side2_c)
    give_f2, keep_f2 = fc2.keep(recv_f2)
    side_f2 = swap(give_f2, "dp", 2, "F2")
    d_pre, shift_sum, wide_fc2 = hidden_back(place, cotangent, after(slope, give_f2), pieces_c)
    layer_out, d_mid, d_mid_low, d_mix, sums_mid = middle_layer(
        mid, act, d_pre, cotangent, valid, vec, wide_out, wide_fc1, wide_fc2
    )
    fc1 = Reduction(place, [(a2_t, after(d_pre, d_mix))])
    given = fc1.give()
    side_f2, given, d_mix = sync(side_f2, given, d_mix)
    recv_f1 = gather_core(given, "F1")
    ((sent,),) = together(place, to_send_x(keep_f2, side_f2))
    column_f2 = swap(sent, "shard", 1, "F2")
    give_f1, keep_f1 = fc1.keep(after(recv_f1, sent))
    side_f1 = swap(give_f1, "dp", 2, "F1")
    d_proj, sums_att = attention_back(qkv, mix_t, after(d_mix, give_f1), prob)
    first = Reduction(place, [(a1_t, d_proj), (mix_t, d_mid_low)])
    given = first.give()
    column_f2, side_f1, given = sync(column_f2, side_f1, given)
    recv_a = gather_core(given, "RA")
    tokens_grad, small_sums = first_norm_back(
        place,
        tokens,
        d_proj,
        after(d_mid, given),
        vec,
        valid,
        (sums_in, sums_mid, sums_att, shift_sum),
        pieces_a,
    )
    recv_a, small_sums = sync(recv_a, small_sums)
    give_a, keep_a = first.keep(recv_a)
    columns_f2, (sent,) = together(
        place,
        to_send_z(keep_f2, side_f2, after(column_f2, give_a)),
        to_send_x(keep_f1, side_f1),
    )
    pieces_f2 = fc2.over_z(columns_f2, "F2")
    column_f1 = swap(sent, "shard", 1, "F1")
    side_ra = swap(give_a, "dp", 2, "RA")
    side_ra, column_f1, pieces_f2 = sync(side_ra, column_f1, pieces_f2)
    (sent,), columns_f1, (piece_f2,) = together(
        place,
        to_send_x(keep_a, side_ra),
        to_send_z(keep_f1, side_f1, column_f1),
        to_add_pieces(columns_f2[0], pieces_f2),
    )
    piece_f2 = over_rest(piece_f2, plus)
    other_f2 = swap(piece_f2, "dp", 2, "F2")
    pieces_f1 = fc1.over_z(columns_f1, "F1")
    column_a = swap(sent, "shard", 1, "RA")
    column_a, pieces_f1, other_f2 = sync(column_a, pieces_f1, other_f2)
    columns_a, (piece_f1,), (owned_f2, squares) = together(
        place,
        to_send_z(keep_a, side_ra, column_a),
        to_add_pieces(columns_f1[0], pieces_f1),
        to_join_planes(piece_f2, other_f2, jnp.zeros((1, model_width), WIDE)),
    )
    theirs_f2 = gather_core(owned_f2, "F2")
    piece_f1 = over_rest(piece_f1, plus)
    other_f1 = swap(piece_f1, "dp", 2, "F1")
    pieces_ra = first.over_z(columns_a, "RA")
    pieces_ra, other_f1, theirs_f2 = sync(pieces_ra, other_f1, theirs_f2)
    (piece_a,), (owned_f1, squares) = together(
        place,
        to_add_pieces(columns_a[0], pieces_ra),
        to_join_planes(piece_f1, other_f1, squares),
    )
    piece_a = over_rest(piece_a, plus)
    other_a = swap(piece_a, "dp", 2, "RA")
    small_more = swap(after(small_sums, piece_a), "dp", 2)
    theirs_f1 = gather_core(owned_f1, "F1")
    ((grad_fc2,),) = together(place, to_join_cores(owned_f2, after(theirs_f2, piece_a)))
    other_a, theirs_f1, small_more, grad_fc2 = sync(other_a, theirs_f1, small_more, grad_fc2)
    (owned_a, squares), (small_sums,) = together(
        place,
        to_join_planes(piece_a, other_a, squares),
        (add_sums, (small_sums, small_more), [shape(small_sums.shape, WIDE)]),
    )
    small_sums = over_rest(small_sums, jnp.add)
    theirs_a = gather_core(owned_a, "RA")
    small_sums = jnp.concatenate([small_sums, squares])
    small_more = swap(small_sums, "dp", 1)
    ((grad_fc1,),) = together(place, to_join_cores(owned_f1, after(theirs_f1, small_sums)))
    theirs_a, small_more, grad_fc1 = sync(theirs_a, small_more, grad_fc1)
    small_sums = small_sums + small_more
    small_more = swap(small_sums, "shard", 1)
    ((grad_qkv, grad_out),) = together(
        place,
        to_join_cores(owned_a, after(theirs_a, small_sums), w_qkv.shape[1] // 2, owned_a.shape[2]),
    )
    small_more, grad_qkv = sync(small_more, grad_qkv)
    small_sums = small_sums + small_more
    small_sums = small_sums + swap(small_sums, "shard", 2)
    small_more = swap(small_sums, "shard", 4)
    clip, stream_rms, own_vectors, own_shift, vector_step, new_shift = finish(
        place, small_sums, small_more, vectors, moments_vectors, fc1_bias, moments_fc1_bias
    )
    grads = (grad_qkv, grad_out, grad_fc1, grad_fc2)
    updated = update(
        clip,
        grads,
        (w_qkv, w_out, w_fc1, w_fc2),
        (moments_qkv, moments_out, moments_fc1, moments_fc2),
    )
    owner_grads = (*grads, own_vectors, own_shift)
    updated = (*updated, vector_step, new_shift)
    return (layer_out, tokens_grad, *owner_grads, *updated, stream_rms)


def solution(mesh):
    placed = (
        P(("dp", "shard"), None),
        P(("dp", "shard")),
        P(("dp", "shard"), None),
        P("shard", None),
        P("shard", None),
        P("shard", None),
        P("shard", None),
        P(None, "shard"),
        P("shard"),
        P(None, "shard", None),
        P(None, "shard", None),
        P(None, "shard", None),
        P(None, "shard", None),
        P(None, None, "shard"),
        P(None, "shard"),
    )
    return jax.shard_map(
        body,
        mesh=mesh,
        in_specs=placed,
        out_specs=(
            P(("dp", "shard"), None),
            P(("dp", "shard"), None),
            P("shard", None),
            P("shard", None),
            P("shard", None),
            P("shard", None),
            P(None, "shard"),
            P("shard"),
            P("shard", None),
            P("shard", None),
            P("shard", None),
            P("shard", None),
            P(None, "shard"),
            P("shard"),
            P(),
        ),
        check_vma=False,
    )
```
